32 devices in a mesh: dp: 4 (over y, core), tensor: 8 (over z, x).
Axes of the slice: x: 2, y: 2, z: 4, core: 2. Of those that a mesh axis runs over, the one named last changes fastest.
Arguments:
- frames: bfloat16 [16, 1536, 1280], P('dp', 'tensor'), may hold values from -6 to 6
- upstream: bfloat16 [16, 1536, 1280], P('dp', 'tensor'), may hold values from -6 to 6
- clip_frame_length: int32 [16], P('dp'), may hold values from 512 to 1536, as said below
- clip_adapter_index: int32 [16, 6], P('dp'), may hold values from 0 to 7
- attention_norm_gain: float32 [1280], replicated, may hold values from 0.1 to 1.9
- feedforward_norm_gain: float32 [1280], replicated, may hold values from 0.1 to 1.9
- query_key_value_frozen_weight: bfloat16 [3, 1280, 1280], P(None, 'dp', 'tensor'), may hold values from -0.15625 to 0.15625
- output_frozen_weight: bfloat16 [1280, 1280], P('tensor', 'dp'), may hold values from -0.5 to 0.5
- first_ffn_frozen_weight: bfloat16 [1280, 5120], P('dp', 'tensor'), may hold values from -0.15625 to 0.15625
- second_ffn_frozen_weight: bfloat16 [5120, 1280], P('tensor', 'dp'), may hold values from -0.078125 to 0.078125
- query_key_value_adapter_down: bfloat16 [3, 8, 1280, 16], replicated, may hold values from -0.15625 to 0.15625
- query_key_value_adapter_up: bfloat16 [3, 8, 16, 1280], P(None, None, None, 'tensor'), may hold values from -1.5 to 1.5
- output_adapter_down: bfloat16 [8, 1280, 16], P(None, 'tensor'), may hold values from -0.5 to 0.5
- output_adapter_up: bfloat16 [8, 16, 1280], replicated, may hold values from -1.5 to 1.5
- first_ffn_adapter_down: bfloat16 [8, 1280, 16], replicated, may hold values from -0.15625 to 0.15625
- first_ffn_adapter_up: bfloat16 [8, 16, 5120], P(None, None, 'tensor'), may hold values from -1.5 to 1.5
- second_ffn_adapter_down: bfloat16 [8, 5120, 16], P(None, 'tensor'), may hold values from -0.078125 to 0.078125
- second_ffn_adapter_up: bfloat16 [8, 16, 1280], replicated, may hold values from -1.5 to 1.5
Outputs:
- layer_output: bfloat16 [16, 1536, 1280], P('dp', 'tensor')
- frames_grad: float32 [16, 1536, 1280], P('dp', 'tensor')
- qkv_grad_a: float32 [3, 8, 1280, 16], P(None, None, 'tensor', 'dp')
- qkv_grad_b: float32 [3, 8, 16, 1280], P(None, None, 'dp', 'tensor')
- out_grad_a: float32 [8, 1280, 16], P(None, 'tensor', 'dp')
- out_grad_b: float32 [8, 16, 1280], P(None, 'dp', 'tensor')
- fc1_grad_a: float32 [8, 1280, 16], P(None, 'tensor', 'dp')
- fc1_grad_b: float32 [8, 16, 5120], P(None, 'dp', 'tensor')
- fc2_grad_a: float32 [8, 5120, 16], P(None, 'tensor', 'dp')
- fc2_grad_b: float32 [8, 16, 1280], P(None, 'dp', 'tensor')
The draws below stay inside these ranges and needn't reach their ends.
Inputs may be any that keep to these rules, and one draw needn't show every extreme that they name: `clip_frame_length`: each clip's valid frames are the first of its buffer; some clip in every draw has all 1536.
All inputs are finite; a program needn't handle non-finite values.
Results may differ from the reference program's by a relative error of at most 0.04.
Values may be sent and summed in bfloat16 or wider, within the bound.
No kernel may reach another device: no remote copies, remote signals or barrier semaphores. Data moves between devices by JAX's collectives and lax.ppermute only.
A program may use at most 320 MiB of HBM per device.

```python
import jax
import jax.numpy as jnp
from jax import lax

MODEL_WIDTH = 1280
HEADS = 16
HEAD = 80
HIDDEN_UNITS = 5120
ADAPTER_COUNT = 8
ADAPTER_RANK = 16
FRAMES = 1536
CLIPS = 16


def draw_clip_frame_length(key, part):
    first_key, second_key = jax.random.split(jax.random.fold_in(key, 11))
    lengths = jax.random.randint(first_key, (CLIPS,), FRAMES // 3, FRAMES + 1)
    longest = jax.random.randint(second_key, (), 0, CLIPS)
    return jnp.where(jnp.arange(CLIPS) == longest, FRAMES, lengths).astype(jnp.int32)


def set_ends(entries, stream_key, low, largest):
    place = [jax.random.randint(jax.random.fold_in(stream_key, axis), (), 0, length) for axis, length in enumerate(entries.shape)]
    main_axis = entries.shape.index(max(entries.shape))
    beside = place[:main_axis] + [(place[main_axis] + 1) % entries.shape[main_axis]] + place[main_axis + 1:]
    return entries.at[tuple(place)].set(low).at[tuple(beside)].set(largest)


def steps_of(own_key, dims, pieces, smallest, top_value):
    loudness = 1.0
    for position, shards_of in pieces:
        steps = jax.random.uniform(jax.random.fold_in(jax.random.fold_in(own_key, 6), position), (shards_of,), jnp.float32, smallest / len(pieces), top_value / len(pieces))
        loudness = loudness * jnp.repeat(jnp.exp(steps), dims[position] // shards_of).reshape((-1,) + (1,) * (len(dims) - 1 - position))
    return loudness


def noise(rng, shape, width, most, pieces=(), held_as=jnp.bfloat16):
    values = width * jax.random.normal(rng, shape, jnp.float32)
    if pieces:
        values = values * steps_of(rng, shape, pieces, -0.22, 0.18)
    return jnp.clip(values, -most, most).astype(held_as)


def setup_inputs(seed: int = 0) -> dict:
    key_of = jax.random.split(jax.random.key(seed), 19)
    return {
        "frames": noise(key_of[0], (CLIPS, FRAMES, MODEL_WIDTH), 1.0, 6.0, ((0, 4), (1, 8))),
        "upstream": noise(key_of[1], (CLIPS, FRAMES, MODEL_WIDTH), 1.0, 6.0, ((0, 4), (1, 8))),
        "clip_frame_length": draw_clip_frame_length(jax.random.fold_in(key_of[18], 71), 0),
        "clip_adapter_index": set_ends(jax.random.randint(key_of[3], (CLIPS, 6), 0, ADAPTER_COUNT), jax.random.fold_in(key_of[3], 1), 0, ADAPTER_COUNT - 1).astype(jnp.int32),
        "attention_norm_gain": jnp.clip(1.0 + 0.18 * jax.random.normal(key_of[4], (MODEL_WIDTH,), jnp.float32), 0.1, 1.9),
        "feedforward_norm_gain": jnp.clip(1.0 + 0.18 * jax.random.normal(key_of[5], (MODEL_WIDTH,), jnp.float32), 0.1, 1.9),
        "query_key_value_frozen_weight": noise(key_of[6], (3, MODEL_WIDTH, MODEL_WIDTH), MODEL_WIDTH ** -0.5, 0.15625, ((1, 4), (2, 8))),
        "output_frozen_weight": noise(key_of[7], (MODEL_WIDTH, MODEL_WIDTH), (MODEL_WIDTH // 8) ** -0.5, 0.5, ((0, 8), (1, 4))),
        "first_ffn_frozen_weight": noise(key_of[8], (MODEL_WIDTH, HIDDEN_UNITS), MODEL_WIDTH ** -0.5, 0.15625, ((0, 4), (1, 8))),
        "second_ffn_frozen_weight": noise(key_of[9], (HIDDEN_UNITS, MODEL_WIDTH), HIDDEN_UNITS ** -0.5, 0.078125, ((0, 8), (1, 4))),
        "query_key_value_adapter_down": noise(key_of[10], (3, ADAPTER_COUNT, MODEL_WIDTH, ADAPTER_RANK), MODEL_WIDTH ** -0.5, 0.15625),
        "query_key_value_adapter_up": noise(key_of[11], (3, ADAPTER_COUNT, ADAPTER_RANK, MODEL_WIDTH), ADAPTER_RANK ** -0.5, 1.5, ((3, 8),)),
        "output_adapter_down": noise(key_of[12], (ADAPTER_COUNT, MODEL_WIDTH, ADAPTER_RANK), (MODEL_WIDTH // 8) ** -0.5, 0.5, ((1, 8),)),
        "output_adapter_up": noise(key_of[13], (ADAPTER_COUNT, ADAPTER_RANK, MODEL_WIDTH), ADAPTER_RANK ** -0.5, 1.5),
        "first_ffn_adapter_down": noise(key_of[14], (ADAPTER_COUNT, MODEL_WIDTH, ADAPTER_RANK), MODEL_WIDTH ** -0.5, 0.15625),
        "first_ffn_adapter_up": noise(key_of[15], (ADAPTER_COUNT, ADAPTER_RANK, HIDDEN_UNITS), ADAPTER_RANK ** -0.5, 1.5, ((2, 8),)),
        "second_ffn_adapter_down": noise(key_of[16], (ADAPTER_COUNT, HIDDEN_UNITS, ADAPTER_RANK), HIDDEN_UNITS ** -0.5, 0.078125, ((1, 8),)),
        "second_ffn_adapter_up": noise(key_of[17], (ADAPTER_COUNT, ADAPTER_RANK, MODEL_WIDTH), ADAPTER_RANK ** -0.5, 1.5),
    }


@jax.custom_vjp
def low(v):
    return lax.optimization_barrier(v.astype(jnp.bfloat16)).astype(jnp.float32)

@jax.custom_vjp
def low_back(v):
    return v

def low_keep(v):
    return (low(v), None)

def low_pass(kept, grad):
    return (grad,)

def back_keep(v):
    return (v, None)

def back_low(kept, grad):
    return (low(grad),)
low.defvjp(low_keep, low_pass)
low_back.defvjp(back_keep, back_low)

def matmul(left, right):
    return jnp.matmul(left, right, precision=lax.Precision.HIGHEST)

def layer_norm(values, gain):
    center = values - lax.optimization_barrier(jnp.mean(values, axis=-1, keepdims=True))
    spread = lax.optimization_barrier(jnp.mean(center * center, axis=-1, keepdims=True))
    return center * lax.rsqrt(spread + 1e-05) * gain

def apply_projection(source, weight, entry_input, exit_input):
    return matmul(source, weight) + matmul(matmul(source, entry_input), exit_input)

def clip_forward(frames_clip, length, adapter_picks, frozen, adapter_list):
    attention_norm_gain, feedforward_norm_gain, query_key_value_frozen_weight, output_frozen_weight, first_ffn_frozen_weight, second_ffn_frozen_weight = frozen
    query_key_value_adapter_down, query_key_value_adapter_up, output_adapter_down, output_adapter_up, first_ffn_adapter_down, first_ffn_adapter_up, second_ffn_adapter_down, second_ffn_adapter_up = adapter_list
    live = jnp.arange(FRAMES) < length
    first_normalized = low(layer_norm(frames_clip, attention_norm_gain))
    parts = []
    for part in range(3):
        value_rows = apply_projection(first_normalized, query_key_value_frozen_weight[part], query_key_value_adapter_down[part][adapter_picks[part]], query_key_value_adapter_up[part][adapter_picks[part]])
        parts.append(low_back(low(value_rows)).reshape(FRAMES, HEADS, HEAD))
    query, keys_all, values_all = parts
    scores = jnp.einsum('qhd,khd->hqk', query, keys_all, precision=lax.Precision.HIGHEST) * HEAD ** (-0.5)
    scores = low_back(scores)
    scores = jnp.where(live[None, None, :], scores, -1e+30)
    top = lax.optimization_barrier(jnp.max(scores, axis=-1, keepdims=True))
    expo = jnp.exp(scores - top)
    probs = low(expo / lax.optimization_barrier(jnp.sum(expo, axis=-1, keepdims=True)))
    mixed_heads = jnp.einsum('hqk,khd->qhd', probs, values_all, precision=lax.Precision.HIGHEST).reshape(FRAMES, MODEL_WIDTH)
    mixed_heads = low_back(low(mixed_heads))
    attention_output = low_back(apply_projection(mixed_heads, output_frozen_weight, output_adapter_down[adapter_picks[3]], output_adapter_up[adapter_picks[3]]))
    hidden = frames_clip + attention_output
    second_normalized = low(layer_norm(hidden, feedforward_norm_gain))
    upper_hidden = low_back(apply_projection(second_normalized, first_ffn_frozen_weight, first_ffn_adapter_down[adapter_picks[4]], first_ffn_adapter_up[adapter_picks[4]]))
    active_rows = low(jax.nn.gelu(upper_hidden, approximate=False))
    branch_output = low_back(apply_projection(active_rows, second_ffn_frozen_weight, second_ffn_adapter_down[adapter_picks[5]], second_ffn_adapter_up[adapter_picks[5]]))
    return jnp.where(live[:, None], hidden + branch_output, 0.0)

def reference(frames, upstream, clip_frame_length, clip_adapter_index, attention_norm_gain, feedforward_norm_gain, query_key_value_frozen_weight, output_frozen_weight, first_ffn_frozen_weight, second_ffn_frozen_weight, query_key_value_adapter_down, query_key_value_adapter_up, output_adapter_down, output_adapter_up, first_ffn_adapter_down, first_ffn_adapter_up, second_ffn_adapter_down, second_ffn_adapter_up):
    frozen = tuple((clip_item.astype(jnp.float32) for clip_item in (attention_norm_gain, feedforward_norm_gain, query_key_value_frozen_weight, output_frozen_weight, first_ffn_frozen_weight, second_ffn_frozen_weight)))
    adapter_list = tuple((clip_item.astype(jnp.float32) for clip_item in (query_key_value_adapter_down, query_key_value_adapter_up, output_adapter_down, output_adapter_up, first_ffn_adapter_down, first_ffn_adapter_up, second_ffn_adapter_down, second_ffn_adapter_up)))

    def whole(rows_all, adapter_set):

        def one_clip(clip_item):
            return clip_forward(clip_item[0], clip_item[1], clip_item[2], frozen, adapter_set)
        return lax.map(jax.checkpoint(one_clip), (rows_all, clip_frame_length, clip_adapter_index))
    layer, pull = jax.vjp(whole, frames.astype(jnp.float32), adapter_list)
    frames_grad, adapter_grads = pull(upstream.astype(jnp.float32))
    return (layer.astype(jnp.bfloat16), frames_grad, adapter_grads[0], adapter_grads[1], adapter_grads[2], adapter_grads[3], adapter_grads[4], adapter_grads[5], adapter_grads[6], adapter_grads[7])
```

```python
import functools

import jax
import jax.numpy as jnp
from jax import lax
from jax.sharding import PartitionSpec as P

HEAD = 80
BF = jnp.bfloat16
F32 = jnp.float32


def mm(a, b):
    return jnp.dot(a, b, preferred_element_type=F32)


def mm_nt(a, b):
    return lax.dot_general(a, b, (((1,), (1,)), ((), ())), preferred_element_type=F32)


def mm_tn(a, b):
    return lax.dot_general(a, b, (((0,), (0,)), ((), ())), preferred_element_type=F32)


def norm_parts(values):
    center = values - jnp.mean(values, axis=-1, keepdims=True)
    rate = lax.rsqrt(jnp.mean(center * center, axis=-1, keepdims=True) + 1e-5)
    return center * rate, rate


def norm_back(z, rate, grad):
    return rate * (
        grad
        - jnp.mean(grad, axis=-1, keepdims=True)
        - z * jnp.mean(grad * z, axis=-1, keepdims=True)
    )


class Place:
    def __init__(self, clips, local_frames):
        self.D, self.T = lax.axis_size("dp"), lax.axis_size("tensor")
        self.d, self.t = lax.axis_index("dp"), lax.axis_index("tensor")
        self.core = self.d % 2
        self.C, self.LF = clips, local_frames
        self.Q = self.T // (2 * clips)
        self.S = local_frames // (2 * self.Q)
        self.rows = self.T * self.S
        self.swap = [(i, i ^ 1) for i in range(self.D)]

    def swap_core(self, x):
        return lax.ppermute(x, "dp", self.swap)

    def positions(self, core, q):
        source = jnp.arange(self.T, dtype=jnp.int32)[:, None] * self.LF
        inner = (q * 2 + core) * self.S + jnp.arange(self.S, dtype=jnp.int32)[None, :]
        return (source + inner).reshape(self.rows)


def to_clip(pl_, x):
    C, LF, W = x.shape
    parts = x.reshape(C, pl_.Q, 2, pl_.S, W)
    even, odd = parts[:, :, 0], parts[:, :, 1]
    first = pl_.core == 0
    mine, theirs = jnp.where(first, even, odd), jnp.where(first, odd, even)
    got = pl_.swap_core(theirs)
    both = jnp.stack([jnp.where(first, mine, got), jnp.where(first, got, mine)])
    both = both.reshape(pl_.T, pl_.S, W)
    return lax.all_to_all(both, "tensor", 0, 0).reshape(pl_.rows, W)


def from_clip(pl_, y):
    W = y.shape[-1]
    both = lax.all_to_all(y.reshape(pl_.T, pl_.S, W), "tensor", 0, 0)
    both = both.reshape(2, pl_.C, pl_.Q, pl_.S, W)
    first = pl_.core == 0
    mine, theirs = jnp.where(first, both[0], both[1]), jnp.where(first, both[1], both[0])
    got = pl_.swap_core(theirs)
    even, odd = jnp.where(first, mine, got), jnp.where(first, got, mine)
    return jnp.stack([even, odd], axis=2).reshape(pl_.C, pl_.LF, W)


def gather_rows(x):
    return lax.all_gather(x, ("tensor", "dp"))


def group_values(pl_, x):
    out = [x, pl_.swap_core(x)]
    for step in range(1, pl_.Q):
        perm = [
            (i, i - i % pl_.Q + (i + step) % pl_.Q) for i in range(pl_.T)
        ]
        out.append(lax.ppermute(out[0], "tensor", perm))
        out.append(lax.ppermute(out[1], "tensor", perm))
    return out


def group_places(pl_):
    q = pl_.t % pl_.Q
    out = []
    for step in range(pl_.Q):
        sender = (q - step) % pl_.Q
        out.append((pl_.core, sender))
        out.append((1 - pl_.core, sender))
    return out


def group_sums(pl_, blocks):
    total = blocks[0]
    total = total + pl_.swap_core(blocks[1].astype(BF)).astype(F32)
    for step in range(1, pl_.Q):
        perm = [
            (i - i % pl_.Q + (i + step) % pl_.Q, i) for i in range(pl_.T)
        ]
        own = lax.ppermute(blocks[2 * step].astype(BF), "tensor", perm)
        other = lax.ppermute(pl_.swap_core(blocks[2 * step + 1].astype(BF)), "tensor", perm)
        total = total + own.astype(F32) + other.astype(F32)
    return total


def attend(q, k, v, bias):
    def head(item):
        qh, kh, vh = item
        scores = mm_nt(qh, kh) * HEAD**-0.5 + bias[None, :]
        top = jnp.max(scores, axis=-1, keepdims=True)
        expo = jnp.exp(scores - top)
        total = jnp.sum(expo, axis=-1, keepdims=True)
        mixed = mm((expo / total).astype(BF), vh)
        return mixed.astype(BF), top + jnp.log(total)

    return lax.map(head, (q, k, v))


def attend_back(q, k, v, bias, lse, dmixed):
    def head(item):
        qh, kh, vh, lh, dh = item
        scores = mm_nt(qh, kh) * HEAD**-0.5 + bias[None, :]
        probs = jnp.exp(scores - lh)
        dprobs = mm_nt(dh, vh)
        delta = jnp.sum(probs * dprobs, axis=-1, keepdims=True)
        dscores = (probs * (dprobs - delta)).astype(BF)
        dq = mm(dscores, kh) * HEAD**-0.5
        dk = mm_tn(dscores, qh) * HEAD**-0.5
        dv = mm_tn(probs.astype(BF), dh)
        return dq, dk, dv

    return lax.map(head, (q, k, v, lse, dmixed))


def body(
    frames,
    upstream,
    clip_frame_length,
    clip_adapter_index,
    gain1,
    gain2,
    w_qkv,
    w_out,
    w_up,
    w_down,
    qkv_a,
    qkv_b,
    out_a,
    out_b,
    fc1_a,
    fc1_b,
    fc2_a,
    fc2_b,
):
    C, LF, W = frames.shape
    pl_ = Place(C, LF)
    D, T, d, t = pl_.D, pl_.T, pl_.d, pl_.t
    Hc = w_qkv.shape[2]
    U = w_up.shape[1]
    A, R = fc1_a.shape[0], fc1_a.shape[2]
    AR = A * R
    rows = pl_.rows
    heads = W // HEAD

    meta = jnp.concatenate([clip_frame_length[:, None], clip_adapter_index], axis=1)
    metas = lax.all_gather(meta, "dp")
    g = t // pl_.Q
    here = metas[d - pl_.core + g // C, g % C]
    length, picks = here[0], here[1:]
    marks = (jnp.arange(AR)[None, :] // R == picks[:, None]).astype(F32)

    qkvo = jnp.concatenate([w_qkv.transpose(0, 2, 1), w_out[None]]).reshape(4 * Hc, W // D)
    qkvo = lax.all_to_all(qkvo, "dp", 0, 1, tiled=True)
    qkvo_low = jnp.concatenate(
        [qkv_b.transpose(0, 3, 1, 2).reshape(3, Hc, AR), out_a.transpose(1, 0, 2).reshape(1, Hc, AR)]
    ).reshape(D, 4 * Hc // D, AR)
    qkvo = jnp.concatenate([qkvo, lax.dynamic_index_in_dim(qkvo_low, d, 0, False)], axis=1)
    ffn = jnp.stack([w_up.T, w_down])
    ffn = lax.all_to_all(ffn, "dp", 1, 2, tiled=True)
    ffn_low = jnp.stack(
        [fc1_b.transpose(2, 0, 1).reshape(U, AR), fc2_a.transpose(1, 0, 2).reshape(U, AR)]
    ).reshape(2, D, U // D, AR)
    ffn = jnp.concatenate([ffn, lax.dynamic_index_in_dim(ffn_low, d, 1, False)], axis=2)
    all_qkvo = gather_rows(qkvo).reshape(T, 4, Hc, W + AR).transpose(1, 0, 2, 3).reshape(4, W, W + AR)
    all_ffn = gather_rows(ffn).transpose(1, 0, 2, 3).reshape(2, T * U, W + AR)

    flat_a = lambda a: a.transpose(1, 0, 2).reshape(W, AR)
    flat_b = lambda b: b.reshape(AR, W)

    x_in = to_clip(pl_, frames).astype(F32)
    live = (pl_.positions(pl_.core, t % pl_.Q) < length)[:, None]
    z1, rate1 = norm_parts(x_in)
    n1 = (z1 * gain1).astype(BF)
    proj, inner = [], []
    for j in range(3):
        low = (mm(n1, flat_a(qkv_a[j])) * marks[j]).astype(BF)
        proj.append(mm_nt(jnp.concatenate([n1, low], axis=1), all_qkvo[j]).astype(BF))
        inner.append(low)
    split = lambda a: a.reshape(-1, heads, HEAD).transpose(1, 0, 2)
    join = lambda a: a.transpose(1, 0, 2).reshape(-1, W)
    q = split(proj[0])
    kv = group_values(pl_, jnp.stack([split(proj[1]), split(proj[2])]))
    kv_all = jnp.concatenate(kv, axis=2)
    keys_live = jnp.concatenate([pl_.positions(c, s) for c, s in group_places(pl_)]) < length
    bias = jnp.where(keys_live, 0.0, -1e30).astype(F32)
    mixed_heads, lse = attend(q, kv_all[0], kv_all[1], bias)
    mixed = join(mixed_heads)
    both = mm(mixed, all_qkvo[3])
    inner_out = (both[:, W:] * marks[3]).astype(BF)
    hidden = x_in + both[:, :W] + mm(inner_out, flat_b(out_b))
    z2, rate2 = norm_parts(hidden)
    n2 = (z2 * gain2).astype(BF)
    inner_up = (mm(n2, flat_a(fc1_a)) * marks[4]).astype(BF)
    upper = mm_nt(jnp.concatenate([n2, inner_up], axis=1), all_ffn[0])
    cdf = 0.5 * (1.0 + lax.erf(upper * (0.5**0.5)))
    active = (upper * cdf).astype(BF)
    both = mm(active, all_ffn[1])
    inner_down = (both[:, W:] * marks[5]).astype(BF)
    branch = both[:, :W] + mm(inner_down, flat_b(fc2_b))
    layer_rows = jnp.where(live, hidden + branch, 0.0).astype(BF)
    layer_output = from_clip(pl_, layer_rows)

    seed = jnp.where(live, to_clip(pl_, upstream), 0).astype(BF)
    dinner_down = (mm_nt(seed, flat_b(fc2_b)) * marks[5]).astype(BF)
    dactive = mm_nt(jnp.concatenate([seed, dinner_down], axis=1), all_ffn[1])
    slope = cdf + upper * jnp.exp(-0.5 * upper * upper) * (1.0 / (2.0 * jnp.pi) ** 0.5)
    dupper = (dactive * slope).astype(BF)
    both = mm(dupper, all_ffn[0])
    dinner_up = (both[:, W:] * marks[4]).astype(BF)
    dn2 = both[:, :W] + mm_nt(dinner_up, flat_a(fc1_a))
    dhidden = seed.astype(F32) + norm_back(z2, rate2, dn2 * gain2)
    dattn = dhidden.astype(BF)
    dinner_out = (mm_nt(dattn, flat_b(out_b)) * marks[3]).astype(BF)
    dmixed = mm_nt(jnp.concatenate([dattn, dinner_out], axis=1), all_qkvo[3]).astype(BF)
    dq, dk, dv = attend_back(q, kv_all[0], kv_all[1], bias, lse, split(dmixed))
    dkv = jnp.stack([dk, dv])
    dkv = group_sums(pl_, [dkv[:, :, i * rows : (i + 1) * rows] for i in range(2 * pl_.Q)])
    dproj = [join(a).astype(BF) for a in (dq, dkv[0], dkv[1])]
    dn1 = jnp.zeros((rows, W), F32)
    dinner = []
    for j in range(3):
        both = mm(dproj[j], all_qkvo[j])
        low = (both[:, W:] * marks[j]).astype(BF)
        dn1 = dn1 + both[:, :W] + mm_nt(low, flat_a(qkv_a[j]))
        dinner.append(low)
    dframes = dhidden + norm_back(z1, rate1, dn1 * gain1)
    frames_grad = from_clip(pl_, dframes.astype(BF)).astype(F32)

    def pick(low, j):
        return lax.dynamic_slice_in_dim(low, picks[j] * R, R, 1)

    model_side = [
        mm_tn(pick(dinner[0], 0), n1),
        mm_tn(pick(dinner[1], 1), n1),
        mm_tn(pick(dinner[2], 2), n1),
        mm_tn(pick(inner_out, 3), dattn),
        mm_tn(pick(dinner_up, 4), n2),
        mm_tn(pick(inner_down, 5), seed),
    ]
    head_side = [
        mm_tn(pick(inner[0], 0), dproj[0]),
        mm_tn(pick(inner[1], 1), dproj[1]),
        mm_tn(pick(inner[2], 2), dproj[2]),
        mm_tn(pick(dinner_out, 3), mixed),
    ]
    unit_side = [mm_tn(pick(inner_up, 4), dupper), mm_tn(pick(dinner_down, 5), active)]
    terms = jnp.concatenate(
        [a.reshape(R, T, -1) for a in model_side + head_side + unit_side], axis=2
    )
    K = D // 2
    RD = R // D if R >= D else 1
    width = terms.shape[2]
    terms = terms.reshape(K, 2, RD, T, width)
    even, odd = terms[:, 0], terms[:, 1]
    first = pl_.core == 0
    mine, theirs = jnp.where(first, even, odd), jnp.where(first, odd, even)
    mine = mine + pl_.swap_core(theirs)
    mine = lax.all_to_all(mine.transpose(2, 0, 1, 3), "tensor", 0, 0)
    planes = [[2 * k + c for k in range(K)] for c in range(2)]
    mine = lax.all_to_all(mine.transpose(1, 0, 2, 3), "dp", 0, 0, axis_index_groups=planes)
    clips = metas.reshape(K, 2 * C, 7)[:, :, 1:]
    clips = jnp.repeat(clips, pl_.Q, axis=1)
    hot = (clips[..., None] == jnp.arange(A)).astype(F32)
    hot = hot.reshape(K * T, 6, A)
    mine = mine.reshape(K * T, RD, width)

    def owned(j, start, size):
        return jnp.einsum(
            "sa,srw->arw", hot[:, j], mine[:, :, start : start + size], precision=lax.Precision.HIGHEST
        )

    wm, wu = W // T, U
    model = [owned(j, j * wm, wm) for j in range(6)]
    head = [owned(j, (6 + j) * wm, wm) for j in range(4)]
    unit = [owned(4, 10 * wm, wu), owned(5, 10 * wm + wu, wu)]
    flip = lambda a: jnp.swapaxes(a, -1, -2)
    return (
        layer_output,
        frames_grad,
        flip(jnp.stack(model[:3])),
        jnp.stack(head[:3]),
        flip(head[3]),
        model[3],
        flip(model[4]),
        unit[0],
        flip(unit[1]),
        model[5],
    )


def solution(mesh):
    placed = (
        P("dp", "tensor", None),
        P("dp", "tensor", None),
        P("dp"),
        P("dp", None),
        P(),
        P(),
        P(None, "dp", "tensor"),
        P("tensor", "dp"),
        P("dp", "tensor"),
        P("tensor", "dp"),
        P(),
        P(None, None, None, "tensor"),
        P(None, "tensor", None),
        P(),
        P(),
        P(None, None, "tensor"),
        P(None, "tensor", None),
        P(),
    )
    return jax.shard_map(
        body,
        mesh=mesh,
        in_specs=placed,
        out_specs=(
            P("dp", "tensor", None),
            P("dp", "tensor", None),
            P(None, None, "tensor", "dp"),
            P(None, None, "dp", "tensor"),
            P(None, "tensor", "dp"),
            P(None, "dp", "tensor"),
            P(None, "tensor", "dp"),
            P(None, "dp", "tensor"),
            P(None, "tensor", "dp"),
            P(None, "dp", "tensor"),
        ),
        check_vma=False,
    )
```

```python
import functools

import jax
import jax.numpy as jnp
from jax import lax
from jax.experimental import pallas as pl
from jax.experimental.pallas import tpu as pltpu
from jax.sharding import PartitionSpec as P

HEAD = 80
BF = jnp.bfloat16
F32 = jnp.float32


def mm(a, b):
    return jnp.dot(a, b, preferred_element_type=F32)


def mm_nt(a, b):
    return lax.dot_general(a, b, (((1,), (1,)), ((), ())), preferred_element_type=F32)


def mm_tn(a, b):
    return lax.dot_general(a, b, (((0,), (0,)), ((), ())), preferred_element_type=F32)


def norm_parts(values):
    center = values - jnp.mean(values, axis=-1, keepdims=True)
    rate = lax.rsqrt(jnp.mean(center * center, axis=-1, keepdims=True) + 1e-5)
    return center * rate, rate


def norm_back(z, rate, grad):
    return rate * (
        grad
        - jnp.mean(grad, axis=-1, keepdims=True)
        - z * jnp.mean(grad * z, axis=-1, keepdims=True)
    )


class Place:
    def __init__(self, clips, local_frames):
        self.D, self.T = lax.axis_size("dp"), lax.axis_size("tensor")
        self.d, self.t = lax.axis_index("dp"), lax.axis_index("tensor")
        self.core = self.d % 2
        self.C, self.LF = clips, local_frames
        self.Q = self.T // (2 * clips)
        self.S = local_frames // (2 * self.Q)
        self.rows = self.T * self.S
        self.swap = [(i, i ^ 1) for i in range(self.D)]

    def swap_core(self, x):
        return lax.ppermute(x, "dp", self.swap)

    def positions(self, core, q):
        source = jnp.arange(self.T, dtype=jnp.int32)[:, None] * self.LF
        inner = (q * 2 + core) * self.S + jnp.arange(self.S, dtype=jnp.int32)[None, :]
        return (source + inner).reshape(self.rows)


def by_chip(pl_, x):
    C, LF, W = x.shape
    parts = x.reshape(C, pl_.Q, 2, pl_.S, W)
    even, odd = parts[:, :, 0], parts[:, :, 1]
    first = pl_.core == 0
    mine, theirs = jnp.where(first, even, odd), jnp.where(first, odd, even)
    got = pl_.swap_core(theirs)
    both = jnp.stack([jnp.where(first, mine, got), jnp.where(first, got, mine)])
    return both.reshape(pl_.T, pl_.S, W)


def to_clip(pl_, both):
    return lax.all_to_all(both, "tensor", 0, 0).reshape(pl_.rows, both.shape[2])


def from_clip(pl_, y):
    W = y.shape[-1]
    both = lax.all_to_all(y.reshape(pl_.T, pl_.S, W), "tensor", 0, 0)
    both = both.reshape(2, pl_.C, pl_.Q, pl_.S, W)
    first = pl_.core == 0
    mine, theirs = jnp.where(first, both[0], both[1]), jnp.where(first, both[1], both[0])
    got = pl_.swap_core(theirs)
    even, odd = jnp.where(first, mine, got), jnp.where(first, got, mine)
    return jnp.stack([even, odd], axis=2).reshape(pl_.C, pl_.LF, W)


def ring(x, axis, stride, size):
    perm = [(i, (i + stride) % size) for i in range(size)]
    out = [x]
    for _ in range(size // stride - 1):
        out.append(lax.ppermute(out[-1], axis, perm))
    return jnp.stack(out)


class Gather:
    def __init__(self, place, first, second):
        self.place = place
        self.parts = (first, second)

    def line(self):
        self.parts = [ring(v, "tensor", 2, self.place.T) for v in self.parts]

    def pair(self, v):
        perm = [(i, i ^ 1) for i in range(self.place.T)]
        return jnp.stack([v, lax.ppermute(v, "tensor", perm)])

    def plane(self, v):
        return ring(v, "dp", 2, self.place.D)

    def middle(self):
        self.parts = [self.pair(self.parts[0]), self.plane(self.parts[1])]

    def last(self):
        self.parts = [self.plane(self.parts[0]), self.pair(self.parts[1])]

    def core(self):
        self.parts = [*self.parts, *[self.place.swap_core(v) for v in self.parts]]


def tie(gathers, *values):
    moved = [g.parts for g in gathers]
    moved, values = lax.optimization_barrier((moved, values))
    for g, parts in zip(gathers, moved):
        g.parts = list(parts)
    return values


def places(pl_, pair_first):
    T, D = pl_.T, pl_.D
    tt, dd = jnp.meshgrid(jnp.arange(T), jnp.arange(D), indexing="ij")
    fx = (pl_.t ^ tt) & 1
    s = ((pl_.t ^ fx) - tt) // 2 % (T // 2)
    fc = (pl_.d ^ dd) & 1
    u = ((pl_.d ^ fc) - dd) // 2 % (D // 2)
    if pair_first:
        index = ((fc * (D // 2) + u) * 2 + fx) * (T // 2) + s
    else:
        index = ((fc * 2 + fx) * (D // 2) + u) * (T // 2) + s
    return index.reshape(-1)


def plane_places(pl_):
    dd = jnp.arange(pl_.D)
    fc = (pl_.d ^ dd) & 1
    return fc * (pl_.D // 2) + ((pl_.d ^ fc) - dd) // 2 % (pl_.D // 2)


def group_values(pl_, x):
    out = [x, pl_.swap_core(x)]
    for step in range(1, pl_.Q):
        perm = [
            (i, i - i % pl_.Q + (i + step) % pl_.Q) for i in range(pl_.T)
        ]
        out.append(lax.ppermute(out[0], "tensor", perm))
        out.append(lax.ppermute(out[1], "tensor", perm))
    return out


def group_places(pl_):
    q = pl_.t % pl_.Q
    out = []
    for step in range(pl_.Q):
        sender = (q - step) % pl_.Q
        out.append((pl_.core, sender))
        out.append((1 - pl_.core, sender))
    return out


def group_received(pl_, blocks):
    total = pl_.swap_core(blocks[1])
    for step in range(1, pl_.Q):
        perm = [(i - i % pl_.Q + (i + step) % pl_.Q, i) for i in range(pl_.T)]
        own = lax.ppermute(blocks[2 * step], "tensor", perm)
        other = lax.ppermute(pl_.swap_core(blocks[2 * step + 1]), "tensor", perm)
        total = (total.astype(F32) + own.astype(F32) + other.astype(F32)).astype(BF)
    return total


RATE = HEAD**-0.5
TO_LOG2 = RATE * 1.4426950408889634
EXTRA = 16


def attend_kernel(q_ref, k_refs, v_refs, bias_ref, out_ref, lse_ref):
    rows = q_ref.shape[1]
    keys = bias_ref.shape[1]
    k = jnp.concatenate(
        [jnp.concatenate([r[...] for r in k_refs], axis=1), bias_ref[...].astype(BF), jnp.zeros((EXTRA - 1, keys), BF)]
    ).T
    v = jnp.concatenate(
        [jnp.concatenate([r[...] for r in v_refs], axis=1), jnp.ones((EXTRA, keys), BF)]
    )
    q = jnp.concatenate([q_ref[...], jnp.ones((EXTRA, rows), BF)])
    scores = mm(k, q)
    top = jnp.max(scores, axis=0, keepdims=True)
    expo = jnp.exp2((scores - top) * TO_LOG2).astype(BF)
    both = mm(v, expo)
    total = both[HEAD : HEAD + 1]
    out_ref[...] = (both[:HEAD] / total).astype(BF)
    lse_ref[0] = top + jnp.log2(total) * (1.0 / TO_LOG2)


def attend(q, ks, vs, bias):
    width, rows = q.shape
    heads, n = width // HEAD, len(ks)
    head = pl.BlockSpec((HEAD, rows), lambda h: (h, 0))

    def kernel(*refs):
        attend_kernel(refs[0], refs[1 : 1 + n], refs[1 + n : 1 + 2 * n], *refs[1 + 2 * n :])

    return pl.pallas_call(
        kernel,
        grid=(heads,),
        in_specs=[head] * (1 + 2 * n) + [pl.BlockSpec(bias.shape, lambda h: (0, 0))],
        out_specs=[head, pl.BlockSpec((1, 1, rows), lambda h: (h, 0, 0))],
        out_shape=[
            jax.ShapeDtypeStruct((width, rows), BF),
            jax.ShapeDtypeStruct((heads, 1, rows), F32),
        ],
        compiler_params=pltpu.CompilerParams(vmem_limit_bytes=56 * 2**20),
        cost_estimate=pl.CostEstimate(
            flops=4 * heads * rows * bias.shape[1] * 256, bytes_accessed=6 * width * rows, transcendentals=0
        ),
        name="attend_forward",
    )(q, *ks, *vs, bias)


def attend_back_kernel(
    q_ref, k_refs, v_refs, bias_ref, lse_ref, mixed_ref, dmixed_ref, dq_ref, dk_refs, dv_refs, *, span
):
    rows = q_ref.shape[1]
    keys = bias_ref.shape[1]
    k_flat = jnp.concatenate([r[...] for r in k_refs], axis=1)
    k = jnp.concatenate(
        [k_flat, bias_ref[...].astype(BF), jnp.ones((3, keys), BF), jnp.zeros((EXTRA - 4, keys), BF)]
    ).T
    v = jnp.concatenate(
        [jnp.concatenate([r[...] for r in v_refs], axis=1), jnp.ones((EXTRA, keys), BF)]
    ).T
    dmixed = dmixed_ref[...]
    delta = -jnp.sum(dmixed.astype(F32) * mixed_ref[...].astype(F32), axis=0, keepdims=True)
    d0 = delta.astype(BF)
    d1 = (delta - d0.astype(F32)).astype(BF)
    dmixed_more = jnp.concatenate([dmixed, d0, d1, jnp.zeros((EXTRA - 2, rows), BF)])
    lse = -lse_ref[0]
    l0 = lse.astype(BF)
    rest = lse - l0.astype(F32)
    l1 = rest.astype(BF)
    l2 = (rest - l1.astype(F32)).astype(BF)
    q_flat = q_ref[...]
    q = jnp.concatenate([q_flat, jnp.ones((1, rows), BF), l0, l1, l2, jnp.zeros((EXTRA - 4, rows), BF)])
    dk = jnp.zeros((HEAD, keys), F32)
    dv = jnp.zeros((HEAD, keys), F32)
    for start in range(0, rows, span):
        part = slice(start, start + span)
        probs = jnp.exp2(mm(k, q[:, part]) * TO_LOG2)
        dscores = (probs * mm(v, dmixed_more[:, part])).astype(BF)
        dq_ref[:, part] = (mm(k_flat, dscores) * RATE).astype(BF)
        dk = dk + mm_nt(q_flat[:, part], dscores)
        dv = dv + mm_nt(dmixed[:, part], probs.astype(BF))
    for i, (dk_ref, dv_ref) in enumerate(zip(dk_refs, dv_refs)):
        part = slice(i * rows, (i + 1) * rows)
        dk_ref[...] = (dk[:, part] * RATE).astype(BF)
        dv_ref[...] = dv[:, part].astype(BF)


def attend_back(q, ks, vs, bias, lse, mixed, dmixed):
    width, rows = q.shape
    keys = bias.shape[1]
    heads, n = width // HEAD, len(ks)
    span = rows // 2 if rows % 256 == 0 else rows
    head = pl.BlockSpec((HEAD, rows), lambda h: (h, 0))

    def kernel(*refs):
        ins, outs = refs[: 5 + 2 * n], refs[5 + 2 * n :]
        attend_back_kernel(
            ins[0], ins[1 : 1 + n], ins[1 + n : 1 + 2 * n], *ins[1 + 2 * n :], outs[0], outs[1 : 1 + n], outs[1 + n :], span=span
        )

    return pl.pallas_call(
        kernel,
        grid=(heads,),
        in_specs=[head] * (1 + 2 * n)
        + [
            pl.BlockSpec(bias.shape, lambda h: (0, 0)),
            pl.BlockSpec((1, 1, rows), lambda h: (h, 0, 0)),
            head,
            head,
        ],
        out_specs=[head] * (1 + 2 * n),
        out_shape=[jax.ShapeDtypeStruct((width, rows), BF)] * (1 + 2 * n),
        compiler_params=pltpu.CompilerParams(vmem_limit_bytes=56 * 2**20),
        cost_estimate=pl.CostEstimate(
            flops=8 * heads * rows * keys * 256, bytes_accessed=12 * width * rows, transcendentals=0
        ),
        name="attend_backward",
    )(q, *ks, *vs, bias, lse, mixed, dmixed)


def heads_weights(pl_, parts):
    first, second, first_other, second_other = parts
    planes, pairs, lines, half, width = first.shape
    D, T = pl_.D, pl_.T
    if D == 4 and half == HEAD:
        index = plane_places(pl_)
        order = jnp.stack([index // 2, index % 2], axis=1).reshape(-1).astype(jnp.int32)
        flat = lambda v: v.reshape(*v.shape[:2], lines * half, width)
        return (flat(first), flat(second), flat(first_other), flat(second_other), order), True
    gathered = [
        jnp.stack([first, first_other]).reshape(D, T, half, width),
        jnp.stack([second, second_other]).transpose(0, 2, 1, 3, 4, 5).reshape(D, T, half, width),
    ]
    index = plane_places(pl_)
    gathered = [[lax.dynamic_index_in_dim(v, index[i], 0, False) for v in gathered] for i in range(D)]
    gathered = jnp.stack([jnp.concatenate(v, axis=1) for v in gathered])
    gathered = gathered.reshape(4, D // 4, T, 2 * half, width).transpose(0, 2, 1, 3, 4)
    gathered = gathered.reshape(4, 1, -1, width)
    middle = gathered.shape[2] // 2
    first, second = gathered[:, :, :middle], gathered[:, :, middle:].transpose(1, 0, 2, 3)
    order = jnp.stack([jnp.zeros(4, jnp.int32), jnp.arange(4, dtype=jnp.int32)], axis=1).reshape(-1)
    return (first, second, first, second, order), False


def weight_copies(refs, buf, sems, plane, other):
    first, second = refs[2 * other], refs[2 * other + 1]
    pairs, size = first.shape[1], first.shape[2]
    copies = [
        pltpu.make_async_copy(first.at[plane, x], buf.at[pl.ds(x * size, size)], sems.at[x])
        for x in range(pairs)
    ]
    pairs, at, size = second.shape[0], pairs * size, second.shape[2]
    return copies + [
        pltpu.make_async_copy(second.at[x, plane], buf.at[pl.ds(at + x * size, size)], sems.at[2 + x])
        for x in range(pairs)
    ]


def load_weight(refs, order_ref, number, buf, sems):
    for other in range(2):

        @pl.when(order_ref[2 * number] == other)
        def _():
            for copy in weight_copies(refs, buf, sems, order_ref[2 * number + 1], other):
                copy.start()


def weight_wait(refs, buf, sems):
    for copy in weight_copies(refs, buf, sems, 0, 0):
        copy.wait()


def weight_specs():
    return [pl.BlockSpec(memory_space=pl.ANY)] * 4 + [pl.BlockSpec(memory_space=pltpu.SMEM)]


def whole(shape, dims=0):
    return pl.BlockSpec(shape, lambda *_: (0,) * len(shape))


def block_of(rows):
    return 256 if rows % 256 == 0 else 128


def by_rows(size, width):
    return pl.BlockSpec((size, width), lambda i: (i, 0))


def by_columns(height, size):
    return pl.BlockSpec((height, size), lambda i: (0, i))


def project_kernel(x_ref, gain_ref, a_ref, mark_ref, sel_ref, *refs):
    *w_refs, order_ref, q_ref, k_ref, v_ref, low_ref, bufs, sems = refs
    i = pl.program_id(0)

    @pl.when(i == 0)
    def _():
        for j in range(3):
            load_weight(w_refs, order_ref, j, bufs.at[j], sems.at[j])

    z, _ = norm_parts(x_ref[...].astype(F32))
    n1 = (z * gain_ref[...]).astype(BF)
    for j, out_ref in enumerate((q_ref, k_ref, v_ref)):
        low = (mm(n1, a_ref[j]) * mark_ref[j]).astype(BF)
        low_ref[j] = mm_nt(sel_ref[j], low).astype(BF)

        @pl.when(i == 0)
        def _():
            weight_wait(w_refs, bufs.at[j], sems.at[j])

        out_ref[...] = mm_nt(bufs[j], jnp.concatenate([n1, low], axis=1)).astype(BF)


def project(x, gain, a, marks, sels, w):
    rows, width = x.shape
    AR, R = a.shape[2], sels.shape[1]
    size = block_of(rows)
    return pl.pallas_call(
        project_kernel,
        grid=(rows // size,),
        in_specs=[
            by_rows(size, width),
            whole((1, width)),
            whole((3, width, AR)),
            whole((3, 1, AR)),
            whole((3, R, AR)),
            *weight_specs(),
        ],
        out_specs=[by_columns(width, size)] * 3 + [pl.BlockSpec((3, R, size), lambda i: (0, 0, i))],
        out_shape=[jax.ShapeDtypeStruct((width, rows), BF)] * 3 + [jax.ShapeDtypeStruct((3, R, rows), BF)],
        scratch_shapes=[
            pltpu.VMEM((3, width, width + AR), BF),
            pltpu.SemaphoreType.DMA((3, 4)),
        ],
        compiler_params=pltpu.CompilerParams(vmem_limit_bytes=56 * 2**20),
        cost_estimate=pl.CostEstimate(
            flops=6 * rows * width * width, bytes_accessed=6 * width * width, transcendentals=0
        ),
        name="project",
    )(x, gain, a, marks, sels, *w)


def leave_kernel(mixed_ref, x_ref, bo_ref, a1_ref, gain_ref, mark_ref, sel_ref, *refs):
    *w_refs, order_ref, hidden_ref, n2_ref, low_ref, buf, sems = refs
    i = pl.program_id(0)
    width = x_ref.shape[1]

    @pl.when(i == 0)
    def _():
        load_weight(w_refs, order_ref, 3, buf, sems)

    mixed = mixed_ref[...].T

    @pl.when(i == 0)
    def _():
        weight_wait(w_refs, buf, sems)

    both = mm(mixed, buf[...])
    low = (both[:, width:] * mark_ref[3]).astype(BF)
    low_ref[0] = mm_nt(sel_ref[3], low).astype(BF)
    hidden = x_ref[...].astype(F32) + both[:, :width] + mm(low, bo_ref[...])
    hidden_ref[...] = hidden
    z, _ = norm_parts(hidden)
    n2 = (z * gain_ref[...]).astype(BF)
    n2_ref[:, :width] = n2
    low = (mm(n2, a1_ref[...]) * mark_ref[4]).astype(BF)
    n2_ref[:, width:] = low
    low_ref[1] = mm_nt(sel_ref[4], low).astype(BF)


def leave(mixed, x, bo, a1, gain, marks, sels, w):
    rows, width = x.shape
    AR, R = a1.shape[1], sels.shape[1]
    size = block_of(rows)
    return pl.pallas_call(
        leave_kernel,
        grid=(rows // size,),
        in_specs=[
            by_columns(width, size),
            by_rows(size, width),
            whole((AR, width)),
            whole((width, AR)),
            whole((1, width)),
            whole((6, 1, AR)),
            whole((6, R, AR)),
            *weight_specs(),
        ],
        out_specs=[
            by_rows(size, width),
            by_rows(size, width + AR),
            pl.BlockSpec((2, R, size), lambda i: (0, 0, i)),
        ],
        out_shape=[
            jax.ShapeDtypeStruct((rows, width), F32),
            jax.ShapeDtypeStruct((rows, width + AR), BF),
            jax.ShapeDtypeStruct((2, R, rows), BF),
        ],
        scratch_shapes=[pltpu.VMEM((width, width + AR), BF), pltpu.SemaphoreType.DMA((4,))],
        compiler_params=pltpu.CompilerParams(vmem_limit_bytes=56 * 2**20),
        cost_estimate=pl.CostEstimate(
            flops=4 * rows * width * width, bytes_accessed=2 * width * width, transcendentals=0
        ),
        name="leave_attention",
    )(mixed, x, bo, a1, gain, marks, sels, *w)


def feed_kernel(
    x_ref, up_ref, live_ref, b2_ref, mark_ref, sel_ref, low_ref, w_ref, acc1_ref, acc2_ref, ga_ref, gb_ref, s_ref, ld_ref
):
    width = up_ref.shape[1]

    @pl.when(pl.program_id(0) == 0)
    def _():
        acc1_ref[...] = jnp.zeros_like(acc1_ref)
        acc2_ref[...] = jnp.zeros_like(acc2_ref)
        seed = (up_ref[...].astype(F32) * live_ref[...]).astype(BF)
        s_ref[:, :width] = seed
        low = (mm_nt(seed, b2_ref[...]) * mark_ref[5]).astype(BF)
        s_ref[:, width:] = low
        ld_ref[...] = mm_nt(sel_ref[5], low).astype(BF)

    wide = w_ref.shape[3]
    first = w_ref[:, 0].reshape(-1, wide)
    second = w_ref[:, 1].reshape(-1, wide)
    upper = mm_nt(x_ref[...], first)
    cdf = 0.5 * (1.0 + lax.erf(upper * (0.5**0.5)))
    active = (upper * cdf).astype(BF)
    dactive = mm_nt(s_ref[...], second)
    slope = cdf + upper * jnp.exp(-0.5 * upper * upper) * (1.0 / (2.0 * jnp.pi) ** 0.5)
    dupper = (dactive * slope).astype(BF)
    acc1_ref[...] += mm(active, second)
    acc2_ref[...] += mm(dupper, first)
    ga_ref[...] = mm(ld_ref[...], active)
    gb_ref[...] = mm(low_ref[1], dupper)


def feed(x, upstream, live, b2, marks, sels, low, w):
    rows, width = upstream.shape
    blocks, _, h, wide = w.shape
    AR, R = wide - width, low.shape[1]
    step = blocks
    while step * h > 1280:
        step //= 2
    part = pl.BlockSpec((R, step * h), lambda i: (0, i))
    return pl.pallas_call(
        feed_kernel,
        grid=(blocks // step,),
        in_specs=[
            whole((rows, wide)),
            whole((rows, width)),
            whole((rows, 1)),
            whole((AR, width)),
            whole((6, 1, AR)),
            whole((6, R, AR)),
            whole((2, R, rows)),
            pl.BlockSpec((step, 2, h, wide), lambda i: (i, 0, 0, 0)),
        ],
        out_specs=[whole((rows, wide)), whole((rows, wide)), part, part],
        out_shape=[jax.ShapeDtypeStruct((rows, wide), F32)] * 2
        + [jax.ShapeDtypeStruct((R, blocks * h), F32)] * 2,
        scratch_shapes=[pltpu.VMEM((rows, wide), BF), pltpu.VMEM((R, rows), BF)],
        compiler_params=pltpu.CompilerParams(vmem_limit_bytes=60 * 2**20),
        cost_estimate=pl.CostEstimate(
            flops=8 * rows * wide * blocks * h, bytes_accessed=4 * blocks * h * wide, transcendentals=0
        ),
        name="feed_forward",
    )(x, upstream, live, b2, marks, sels, low, w)


def turn_kernel(
    acc1_ref, acc2_ref, hidden_ref, n2_ref, up_ref, live_ref, mixed_ref, bo_ref, a1_ref, b2_ref, gain_ref,
    mark_ref, sel_ref, low_ref, *refs
):
    *w_refs, order_ref, layer_ref, dhidden_ref, dmixed_ref, grad_ref, buf, sems = refs
    i = pl.program_id(0)
    width = hidden_ref.shape[1]

    @pl.when(i == 0)
    def _():
        load_weight(w_refs, order_ref, 3, buf, sems)
        grad_ref[...] = jnp.zeros_like(grad_ref)

    hidden = hidden_ref[...]
    seed = (up_ref[...].astype(F32) * live_ref[...]).astype(BF)
    low = (acc1_ref[:, width:] * mark_ref[5]).astype(BF)
    branch = acc1_ref[:, :width] + mm(low, b2_ref[...])
    layer_ref[...] = jnp.where(live_ref[...] > 0, hidden + branch, 0.0).astype(BF)
    grad_ref[3] += mm(mm_nt(sel_ref[5], low).astype(BF), seed)
    low = (acc2_ref[:, width:] * mark_ref[4]).astype(BF)
    grad_ref[2] += mm(mm_nt(sel_ref[4], low).astype(BF), n2_ref[:, :width])
    dn2 = acc2_ref[:, :width] + mm_nt(low, a1_ref[...])
    z, rate = norm_parts(hidden)
    dhidden = seed.astype(F32) + norm_back(z, rate, dn2 * gain_ref[...])
    dhidden_ref[...] = dhidden
    dattn = dhidden.astype(BF)
    grad_ref[1] += mm(low_ref[0], dattn)
    low = (mm_nt(dattn, bo_ref[...]) * mark_ref[3]).astype(BF)
    grad_ref[0] += mm_nt(mm_nt(sel_ref[3], low).astype(BF), mixed_ref[...])

    @pl.when(i == 0)
    def _():
        weight_wait(w_refs, buf, sems)

    dmixed_ref[...] = mm_nt(buf[...], jnp.concatenate([dattn, low], axis=1)).astype(BF)


def turn(acc1, acc2, hidden, n2, upstream, live, mixed, bo, a1, b2, gain, marks, sels, low, w):
    rows, width = hidden.shape
    AR, R = a1.shape[1], sels.shape[1]
    size = block_of(rows)
    return pl.pallas_call(
        turn_kernel,
        grid=(rows // size,),
        in_specs=[
            by_rows(size, width + AR),
            by_rows(size, width + AR),
            by_rows(size, width),
            by_rows(size, width + AR),
            by_rows(size, width),
            by_rows(size, 1),
            by_columns(width, size),
            whole((AR, width)),
            whole((width, AR)),
            whole((AR, width)),
            whole((1, width)),
            whole((6, 1, AR)),
            whole((6, R, AR)),
            pl.BlockSpec((2, R, size), lambda i: (0, 0, i)),
            *weight_specs(),
        ],
        out_specs=[by_rows(size, width), by_rows(size, width), by_columns(width, size), whole((4, R, width))],
        out_shape=[
            jax.ShapeDtypeStruct((rows, width), BF),
            jax.ShapeDtypeStruct((rows, width), F32),
            jax.ShapeDtypeStruct((width, rows), BF),
            jax.ShapeDtypeStruct((4, R, width), F32),
        ],
        scratch_shapes=[pltpu.VMEM((width, width + AR), BF), pltpu.SemaphoreType.DMA((4,))],
        compiler_params=pltpu.CompilerParams(vmem_limit_bytes=56 * 2**20),
        cost_estimate=pl.CostEstimate(
            flops=4 * rows * width * width, bytes_accessed=16 * rows * width, transcendentals=0
        ),
        name="turn",
    )(acc1, acc2, hidden, n2, upstream, live, mixed, bo, a1, b2, gain, marks, sels, low, *w)


def finish_kernel(
    x_ref, dhidden_ref, gain_ref, a_ref, mark_ref, sel_ref, low_ref, dq_ref, dk_ref, dk2_ref, dv_ref, dv2_ref, *refs
):
    *w_refs, order_ref, out_ref, grad_ref, bufs, sems = refs
    i = pl.program_id(0)
    width = x_ref.shape[1]

    @pl.when(i == 0)
    def _():
        for j in range(3):
            load_weight(w_refs, order_ref, j, bufs.at[j], sems.at[j])
        grad_ref[...] = jnp.zeros_like(grad_ref)

    z, rate = norm_parts(x_ref[...].astype(F32))
    n1 = (z * gain_ref[...]).astype(BF)
    dn1 = jnp.zeros(x_ref.shape, F32)
    for j, own in enumerate((dq_ref, dk_ref, dv_ref)):
        dy = own[...]
        if j:
            dy = (dy.astype(F32) + (dk2_ref, dv2_ref)[j - 1][...].astype(F32)).astype(BF)

        @pl.when(i == 0)
        def _():
            weight_wait(w_refs, bufs.at[j], sems.at[j])

        both = mm(dy.T, bufs[j])
        low = (both[:, width:] * mark_ref[j]).astype(BF)
        grad_ref[0, j] += mm(mm_nt(sel_ref[j], low).astype(BF), n1)
        grad_ref[1, j] += mm_nt(low_ref[j], dy)
        dn1 = dn1 + both[:, :width] + mm_nt(low, a_ref[j])
    out_ref[...] = (dhidden_ref[...] + norm_back(z, rate, dn1 * gain_ref[...])).astype(BF)


def finish(x, dhidden, gain, a, marks, sels, low, dq, dk, dk2, dv, dv2, w):
    rows, width = x.shape
    AR, R = a.shape[2], sels.shape[1]
    size = block_of(rows)
    return pl.pallas_call(
        finish_kernel,
        grid=(rows // size,),
        in_specs=[
            by_rows(size, width),
            by_rows(size, width),
            whole((1, width)),
            whole((3, width, AR)),
            whole((3, 1, AR)),
            whole((3, R, AR)),
            pl.BlockSpec((3, R, size), lambda i: (0, 0, i)),
        ]
        + [by_columns(width, size)] * 5
        + weight_specs(),
        out_specs=[by_rows(size, width), whole((2, 3, R, width))],
        out_shape=[
            jax.ShapeDtypeStruct((rows, width), BF),
            jax.ShapeDtypeStruct((2, 3, R, width), F32),
        ],
        scratch_shapes=[
            pltpu.VMEM((3, width, width + AR), BF),
            pltpu.SemaphoreType.DMA((3, 4)),
        ],
        compiler_params=pltpu.CompilerParams(vmem_limit_bytes=58 * 2**20),
        cost_estimate=pl.CostEstimate(
            flops=6 * rows * width * width, bytes_accessed=6 * width * width, transcendentals=0
        ),
        name="finish",
    )(x, dhidden, gain, a, marks, sels, low, dq, dk, dk2, dv, dv2, *w)


def body(
    frames,
    upstream,
    clip_frame_length,
    clip_adapter_index,
    gain1,
    gain2,
    w_qkv,
    w_out,
    w_up,
    w_down,
    qkv_a,
    qkv_b,
    out_a,
    out_b,
    fc1_a,
    fc1_b,
    fc2_a,
    fc2_b,
):
    C, LF, W = frames.shape
    pl_ = Place(C, LF)
    D, T, d, t = pl_.D, pl_.T, pl_.d, pl_.t
    Hc = w_qkv.shape[2]
    U = w_up.shape[1]
    A, R = fc1_a.shape[0], fc1_a.shape[2]
    AR = A * R
    rows = pl_.rows
    heads = W // HEAD

    meta = jnp.concatenate([clip_frame_length[:, None], clip_adapter_index], axis=1)
    metas = lax.all_gather(meta, "dp")
    qkvo = jnp.concatenate([w_qkv.transpose(0, 2, 1), w_out[None]]).reshape(4 * Hc, W // D)
    qkvo = lax.all_to_all(qkvo, "dp", 0, 1, tiled=True)
    qkvo_low = jnp.concatenate(
        [qkv_b.transpose(0, 3, 1, 2).reshape(3, Hc, AR), out_a.transpose(1, 0, 2).reshape(1, Hc, AR)]
    ).reshape(D, 4 * Hc // D, AR)
    qkvo = jnp.concatenate([qkvo, lax.dynamic_index_in_dim(qkvo_low, d, 0, False)], axis=1)
    ffn = jnp.stack([w_up.T, w_down])
    ffn = lax.all_to_all(ffn, "dp", 1, 2, tiled=True)
    ffn_low = jnp.stack(
        [fc1_b.transpose(2, 0, 1).reshape(U, AR), fc2_a.transpose(1, 0, 2).reshape(U, AR)]
    ).reshape(2, D, U // D, AR)
    ffn = jnp.concatenate([ffn, lax.dynamic_index_in_dim(ffn_low, d, 1, False)], axis=2)
    count = qkvo.shape[0]
    half = count // 2
    heads_part = Gather(pl_, qkvo[:half], qkvo[half:])
    frames_by = by_chip(pl_, frames)
    heads_part.line()
    frames_by, ffn, metas = tie([heads_part], frames_by, ffn, metas)
    all_ffn = lax.all_gather(ffn, ("tensor", "dp"))
    frames_in = to_clip(pl_, frames_by)
    heads_part.middle()
    heads_part.last()
    (frames_in,) = tie([heads_part], frames_in)
    heads_part.core()
    weights, line = heads_weights(pl_, heads_part.parts)

    g = t // pl_.Q
    here = metas[d - pl_.core + g // C, g % C]
    length, picks = here[0], here[1:]
    marks = (jnp.arange(AR)[None, :] // R == picks[:, None]).astype(F32)

    flat_a = lambda a: a.swapaxes(-3, -2).reshape(*a.shape[:-3], W, AR)
    flat_b = lambda b: b.reshape(AR, W)
    marks = marks[:, None, :]
    sels = (jnp.arange(AR)[None, None, :] == (picks * R)[:, None, None] + jnp.arange(R)[None, :, None]).astype(BF)
    live = (pl_.positions(pl_.core, t % pl_.Q) < length).astype(F32)[:, None]
    keys_live = jnp.concatenate([pl_.positions(c, s) for c, s in group_places(pl_)]) < length
    bias = jnp.where(keys_live, 0.0, -1e30).astype(F32)[None]
    gain1, gain2 = gain1[None], gain2[None]
    a_all = flat_a(qkv_a)

    q, k, v, low1 = project(frames_in, gain1, a_all, marks[:3], sels[:3], weights)
    ks, vs = group_values(pl_, k), group_values(pl_, v)
    q, ks, vs, upstream = tie([], q, ks, vs, upstream)
    upstream_in = to_clip(pl_, by_chip(pl_, upstream))
    mixed, lse = attend(q, ks, vs, bias)
    bo, a1, b2 = flat_b(out_b), flat_a(fc1_a), flat_b(fc2_b)
    hidden, n2, low2 = leave(mixed, frames_in, bo, a1, gain2, marks, sels, weights)
    hidden, n2, low2, upstream_in = tie([], hidden, n2, low2, upstream_in)
    acc1, acc2, unit_a, unit_b = feed(n2, upstream_in, live, b2, marks, sels, low2, all_ffn)
    layer_rows, dhidden, dmixed, grads2 = turn(
        acc1, acc2, hidden, n2, upstream_in, live, mixed, bo, a1, b2, gain2, marks, sels, low2, weights
    )
    layer_output = from_clip(pl_, layer_rows)
    head_order = places(pl_, True).reshape(T, D)[:, d] % T
    clips = metas.reshape(D // 2, 2 * C, 7)[:, :, 1:]
    clips = jnp.repeat(clips, pl_.Q, axis=1)[:, None]
    clips = jnp.broadcast_to(clips, (D // 2, 2, T, 6)).reshape(D * T, 6)
    hot = (clips[:, :, None] == jnp.arange(A)).astype(BF)

    def owned(terms, picks_of):
        sizes = [v.shape[2] for v in terms]
        sent = jnp.concatenate([v.astype(BF) for v in terms], axis=2)
        sent = sent.reshape(D, R // D, T, -1).transpose(0, 2, 1, 3).reshape(D * T, R // D, -1)
        got = lax.all_to_all(sent, ("dp", "tensor"), 0, 0)
        out, at = [], 0
        for size, j in zip(sizes, picks_of):
            out.append(
                jnp.einsum("sa,srw->arw", hot[:, j], got[:, :, at : at + size], preferred_element_type=F32)
            )
            at += size
        return out

    by_tensor = lambda v: v.reshape(R, T, -1)

    def by_head(v):
        if line:
            v = v.reshape(R, 2, T, -1).swapaxes(1, 2)
        return jnp.take(by_tensor(v), head_order, axis=1)

    out_ga, out_gb, fc1_ga, fc2_gb, fc1_gb, fc2_ga = owned(
        [by_head(grads2[0]), *map(by_tensor, (grads2[1], grads2[2], grads2[3], unit_b, unit_a))],
        (3, 3, 4, 5, 4, 5),
    )

    dq, *dkv = attend_back(q, ks, vs, bias, lse, mixed, dmixed)
    dks, dvs = dkv[: len(dkv) // 2], dkv[len(dkv) // 2 :]
    dk2, dv2 = group_received(pl_, dks), group_received(pl_, dvs)
    early = (out_ga, out_gb, fc1_ga, fc2_gb, fc1_gb, fc2_ga)
    dq, layer_output, early = tie([], dq, layer_output, early)
    out_ga, out_gb, fc1_ga, fc2_gb, fc1_gb, fc2_ga = early
    dframes, grads1 = finish(
        frames_in, dhidden, gain1, a_all, marks[:3], sels[:3], low1, dq, dks[0], dk2, dvs[0], dv2, weights
    )
    frames_grad = from_clip(pl_, dframes).astype(F32)

    late = owned(
        [by_tensor(grads1[0, j]) for j in range(3)] + [by_head(grads1[1, j]) for j in range(3)],
        (0, 1, 2, 0, 1, 2),
    )
    flip = lambda a: jnp.swapaxes(a, -1, -2)
    return (
        layer_output,
        frames_grad,
        flip(jnp.stack(late[:3])),
        jnp.stack(late[3:]),
        flip(out_ga),
        out_gb,
        flip(fc1_ga),
        fc1_gb,
        flip(fc2_ga),
        fc2_gb,
    )


def solution(mesh):
    placed = (
        P("dp", "tensor", None),
        P("dp", "tensor", None),
        P("dp"),
        P("dp", None),
        P(),
        P(),
        P(None, "dp", "tensor"),
        P("tensor", "dp"),
        P("dp", "tensor"),
        P("tensor", "dp"),
        P(),
        P(None, None, None, "tensor"),
        P(None, "tensor", None),
        P(),
        P(),
        P(None, None, "tensor"),
        P(None, "tensor", None),
        P(),
    )
    return jax.shard_map(
        body,
        mesh=mesh,
        in_specs=placed,
        out_specs=(
            P("dp", "tensor", None),
            P("dp", "tensor", None),
            P(None, None, "tensor", "dp"),
            P(None, None, "dp", "tensor"),
            P(None, "tensor", "dp"),
            P(None, "dp", "tensor"),
            P(None, "tensor", "dp"),
            P(None, "dp", "tensor"),
            P(None, "tensor", "dp"),
            P(None, "dp", "tensor"),
        ),
        check_vma=False,
    )
```

```python
import functools

import jax
import jax.numpy as jnp
from jax import lax
from jax.experimental import pallas as pl
from jax.experimental.pallas import tpu as pltpu
from jax.sharding import PartitionSpec as P

HEAD = 80
BF = jnp.bfloat16
F32 = jnp.float32


def mm(a, b):
    return jnp.dot(a, b, preferred_element_type=F32)


def mm_nt(a, b):
    return lax.dot_general(a, b, (((1,), (1,)), ((), ())), preferred_element_type=F32)


def mm_tn(a, b):
    return lax.dot_general(a, b, (((0,), (0,)), ((), ())), preferred_element_type=F32)


def norm_parts(values):
    center = values - jnp.mean(values, axis=-1, keepdims=True)
    rate = lax.rsqrt(jnp.mean(center * center, axis=-1, keepdims=True) + 1e-5)
    return center * rate, rate


def norm_back(z, rate, grad):
    return rate * (
        grad
        - jnp.mean(grad, axis=-1, keepdims=True)
        - z * jnp.mean(grad * z, axis=-1, keepdims=True)
    )


class Place:
    def __init__(self, clips, local_frames):
        self.D, self.T = lax.axis_size("dp"), lax.axis_size("tensor")
        self.d, self.t = lax.axis_index("dp"), lax.axis_index("tensor")
        self.core = self.d % 2
        self.C, self.LF = clips, local_frames
        self.Q = self.T // (2 * clips)
        self.S = local_frames // (2 * self.Q)
        self.rows = self.T * self.S
        self.swap = [(i, i ^ 1) for i in range(self.D)]

    def swap_core(self, x):
        return lax.ppermute(x, "dp", self.swap)

    def positions(self, core, q):
        source = jnp.arange(self.T, dtype=jnp.int32)[:, None] * self.LF
        inner = (q * 2 + core) * self.S + jnp.arange(self.S, dtype=jnp.int32)[None, :]
        return (source + inner).reshape(self.rows)


def by_chip(pl_, x):
    C, LF, W = x.shape
    parts = x.reshape(C, pl_.Q, 2, pl_.S, W)
    even, odd = parts[:, :, 0], parts[:, :, 1]
    first = pl_.core == 0
    mine, theirs = jnp.where(first, even, odd), jnp.where(first, odd, even)
    got = pl_.swap_core(theirs)
    both = jnp.stack([jnp.where(first, mine, got), jnp.where(first, got, mine)])
    return both.reshape(pl_.T, pl_.S, W)


def to_clip(pl_, both):
    return lax.all_to_all(both, "tensor", 0, 0).reshape(pl_.rows, both.shape[2])


def from_clip(pl_, y, terms):
    W = y.shape[-1]
    T, R, w = terms.shape
    sent = jnp.concatenate([y.reshape(T, pl_.S, W), terms.astype(BF).reshape(T, -1, W)], axis=1)
    got = lax.all_to_all(sent, "tensor", 0, 0)
    both = got[:, : pl_.S].reshape(2, pl_.C, pl_.Q, pl_.S, W)
    first = pl_.core == 0
    mine, theirs = jnp.where(first, both[0], both[1]), jnp.where(first, both[1], both[0])
    other = pl_.swap_core(theirs)
    even, odd = jnp.where(first, mine, other), jnp.where(first, other, mine)
    rows = jnp.stack([even, odd], axis=2).reshape(pl_.C, pl_.LF, W)
    return rows, got[:, pl_.S :].reshape(T, R, w)


def to_owners(pl_, terms):
    T, R, w = terms.shape
    D = pl_.D
    parts = terms.reshape(T, D, R // D, w).swapaxes(0, 1)
    out = []
    for step in range(D):
        part = lax.dynamic_index_in_dim(parts, pl_.d ^ step, 0, False)
        out.append(lax.ppermute(part, "dp", [(i, i ^ step) for i in range(D)]) if step else part)
    return jnp.stack(out)


def ring(x, axis, stride, size):
    perm = [(i, (i + stride) % size) for i in range(size)]
    out = [x]
    for _ in range(size // stride - 1):
        out.append(lax.ppermute(out[-1], axis, perm))
    return jnp.stack(out)


class Gather:
    def __init__(self, place, first, second):
        self.place = place
        self.parts = (first, second)

    def line(self, between):
        size = self.place.T
        perm = [(i, (i + 2) % size) for i in range(size)]
        lines = [[v] for v in self.parts]
        for step in range(size // 2 - 1):
            for line in lines:
                line.append(lax.ppermute(line[-1], "tensor", perm))
            if step == 0:
                lines, between = lax.optimization_barrier((lines, between))
        self.parts = [jnp.stack(line) for line in lines]
        return between

    def pair(self, v):
        perm = [(i, i ^ 1) for i in range(self.place.T)]
        return jnp.stack([v, lax.ppermute(v, "tensor", perm)])

    def plane(self, v):
        return ring(v, "dp", 2, self.place.D)

    def middle(self):
        self.parts = [self.pair(self.parts[0]), self.plane(self.parts[1])]

    def last(self):
        self.parts = [self.plane(self.parts[0]), self.pair(self.parts[1])]

    def core(self):
        self.parts = [*self.parts, *[self.place.swap_core(v) for v in self.parts]]


def tie(gathers, *values):
    moved = [g.parts for g in gathers]
    moved, values = lax.optimization_barrier((moved, values))
    for g, parts in zip(gathers, moved):
        g.parts = list(parts)
    return values


def places(pl_, pair_first):
    T, D = pl_.T, pl_.D
    tt, dd = jnp.meshgrid(jnp.arange(T), jnp.arange(D), indexing="ij")
    fx = (pl_.t ^ tt) & 1
    s = ((pl_.t ^ fx) - tt) // 2 % (T // 2)
    fc = (pl_.d ^ dd) & 1
    u = ((pl_.d ^ fc) - dd) // 2 % (D // 2)
    if pair_first:
        index = ((fc * (D // 2) + u) * 2 + fx) * (T // 2) + s
    else:
        index = ((fc * 2 + fx) * (D // 2) + u) * (T // 2) + s
    return index.reshape(-1)


def plane_places(pl_):
    dd = jnp.arange(pl_.D)
    fc = (pl_.d ^ dd) & 1
    return fc * (pl_.D // 2) + ((pl_.d ^ fc) - dd) // 2 % (pl_.D // 2)


def group_values(pl_, x):
    out = [x, pl_.swap_core(x)]
    for step in range(1, pl_.Q):
        perm = [
            (i, i - i % pl_.Q + (i + step) % pl_.Q) for i in range(pl_.T)
        ]
        out.append(lax.ppermute(out[0], "tensor", perm))
        out.append(lax.ppermute(out[1], "tensor", perm))
    return out


def group_places(pl_):
    q = pl_.t % pl_.Q
    out = []
    for step in range(pl_.Q):
        sender = (q - step) % pl_.Q
        out.append((pl_.core, sender))
        out.append((1 - pl_.core, sender))
    return out


def group_received(pl_, blocks):
    total = pl_.swap_core(blocks[1])
    for step in range(1, pl_.Q):
        perm = [(i - i % pl_.Q + (i + step) % pl_.Q, i) for i in range(pl_.T)]
        own = lax.ppermute(blocks[2 * step], "tensor", perm)
        other = lax.ppermute(pl_.swap_core(blocks[2 * step + 1]), "tensor", perm)
        total = (total.astype(F32) + own.astype(F32) + other.astype(F32)).astype(BF)
    return total


RATE = HEAD**-0.5
TO_LOG2 = RATE * 1.4426950408889634
EXTRA = 16


def attend_kernel(q_ref, k_refs, v_refs, bias_ref, out_ref, lse_ref):
    rows = q_ref.shape[1]
    keys = bias_ref.shape[1]
    k = jnp.concatenate(
        [jnp.concatenate([r[...] for r in k_refs], axis=1), bias_ref[...].astype(BF), jnp.zeros((EXTRA - 1, keys), BF)]
    ).T
    v = jnp.concatenate(
        [jnp.concatenate([r[...] for r in v_refs], axis=1), jnp.ones((EXTRA, keys), BF)]
    )
    q = jnp.concatenate([q_ref[...], jnp.ones((EXTRA, rows), BF)])
    scores = mm(k, q)
    top = jnp.max(scores, axis=0, keepdims=True)
    expo = jnp.exp2((scores - top) * TO_LOG2).astype(BF)
    both = mm(v, expo)
    total = both[HEAD : HEAD + 1]
    out_ref[...] = (both[:HEAD] / total).astype(BF)
    lse_ref[0] = top + jnp.log2(total) * (1.0 / TO_LOG2)


def attend(q, ks, vs, bias):
    width, rows = q.shape
    heads, n = width // HEAD, len(ks)
    head = pl.BlockSpec((HEAD, rows), lambda h: (h, 0))

    def kernel(*refs):
        attend_kernel(refs[0], refs[1 : 1 + n], refs[1 + n : 1 + 2 * n], *refs[1 + 2 * n :])

    return pl.pallas_call(
        kernel,
        grid=(heads,),
        in_specs=[head] * (1 + 2 * n) + [pl.BlockSpec(bias.shape, lambda h: (0, 0))],
        out_specs=[head, pl.BlockSpec((1, 1, rows), lambda h: (h, 0, 0))],
        out_shape=[
            jax.ShapeDtypeStruct((width, rows), BF),
            jax.ShapeDtypeStruct((heads, 1, rows), F32),
        ],
        compiler_params=pltpu.CompilerParams(vmem_limit_bytes=56 * 2**20),
        cost_estimate=pl.CostEstimate(
            flops=4 * heads * rows * bias.shape[1] * 256, bytes_accessed=6 * width * rows, transcendentals=0
        ),
        name="attend_forward",
    )(q, *ks, *vs, bias)


def attend_back_kernel(
    q_ref, k_refs, v_refs, bias_ref, lse_ref, mixed_ref, dmixed_ref, dq_ref, dk_refs, dv_refs, *, span
):
    rows = q_ref.shape[1]
    keys = bias_ref.shape[1]
    k_flat = jnp.concatenate([r[...] for r in k_refs], axis=1)
    k = jnp.concatenate(
        [k_flat, bias_ref[...].astype(BF), jnp.ones((3, keys), BF), jnp.zeros((EXTRA - 4, keys), BF)]
    ).T
    v = jnp.concatenate(
        [jnp.concatenate([r[...] for r in v_refs], axis=1), jnp.ones((EXTRA, keys), BF)]
    ).T
    dmixed = dmixed_ref[...]
    delta = -jnp.sum(dmixed.astype(F32) * mixed_ref[...].astype(F32), axis=0, keepdims=True)
    d0 = delta.astype(BF)
    d1 = (delta - d0.astype(F32)).astype(BF)
    dmixed_more = jnp.concatenate([dmixed, d0, d1, jnp.zeros((EXTRA - 2, rows), BF)])
    lse = -lse_ref[0]
    l0 = lse.astype(BF)
    rest = lse - l0.astype(F32)
    l1 = rest.astype(BF)
    l2 = (rest - l1.astype(F32)).astype(BF)
    q_flat = q_ref[...]
    q = jnp.concatenate([q_flat, jnp.ones((1, rows), BF), l0, l1, l2, jnp.zeros((EXTRA - 4, rows), BF)])
    dk = jnp.zeros((HEAD, keys), F32)
    dv = jnp.zeros((HEAD, keys), F32)
    for start in range(0, rows, span):
        part = slice(start, start + span)
        probs = jnp.exp2(mm(k, q[:, part]) * TO_LOG2)
        dscores = (probs * mm(v, dmixed_more[:, part])).astype(BF)
        dq_ref[:, part] = (mm(k_flat, dscores) * RATE).astype(BF)
        dk = dk + mm_nt(q_flat[:, part], dscores)
        dv = dv + mm_nt(dmixed[:, part], probs.astype(BF))
    for i, (dk_ref, dv_ref) in enumerate(zip(dk_refs, dv_refs)):
        part = slice(i * rows, (i + 1) * rows)
        dk_ref[...] = (dk[:, part] * RATE).astype(BF)
        dv_ref[...] = dv[:, part].astype(BF)


def attend_back(q, ks, vs, bias, lse, mixed, dmixed):
    width, rows = q.shape
    keys = bias.shape[1]
    heads, n = width // HEAD, len(ks)
    span = rows // 2 if rows % 256 == 0 else rows
    head = pl.BlockSpec((HEAD, rows), lambda h: (h, 0))

    def kernel(*refs):
        ins, outs = refs[: 5 + 2 * n], refs[5 + 2 * n :]
        attend_back_kernel(
            ins[0], ins[1 : 1 + n], ins[1 + n : 1 + 2 * n], *ins[1 + 2 * n :], outs[0], outs[1 : 1 + n], outs[1 + n :], span=span
        )

    return pl.pallas_call(
        kernel,
        grid=(heads,),
        in_specs=[head] * (1 + 2 * n)
        + [
            pl.BlockSpec(bias.shape, lambda h: (0, 0)),
            pl.BlockSpec((1, 1, rows), lambda h: (h, 0, 0)),
            head,
            head,
        ],
        out_specs=[head] * (1 + 2 * n),
        out_shape=[jax.ShapeDtypeStruct((width, rows), BF)] * (1 + 2 * n),
        compiler_params=pltpu.CompilerParams(vmem_limit_bytes=56 * 2**20),
        cost_estimate=pl.CostEstimate(
            flops=8 * heads * rows * keys * 256, bytes_accessed=12 * width * rows, transcendentals=0
        ),
        name="attend_backward",
    )(q, *ks, *vs, bias, lse, mixed, dmixed)


def heads_weights(pl_, parts):
    first, second, first_other, second_other = parts
    planes, pairs, lines, half, width = first.shape
    D, T = pl_.D, pl_.T
    if D == 4 and half == HEAD:
        index = plane_places(pl_)
        order = jnp.stack([index // 2, index % 2], axis=1).reshape(-1).astype(jnp.int32)
        flat = lambda v: v.reshape(*v.shape[:2], lines * half, width)
        return (flat(first), flat(second), flat(first_other), flat(second_other), order), True
    gathered = [
        jnp.stack([first, first_other]).reshape(D, T, half, width),
        jnp.stack([second, second_other]).transpose(0, 2, 1, 3, 4, 5).reshape(D, T, half, width),
    ]
    index = plane_places(pl_)
    gathered = [[lax.dynamic_index_in_dim(v, index[i], 0, False) for v in gathered] for i in range(D)]
    gathered = jnp.stack([jnp.concatenate(v, axis=1) for v in gathered])
    gathered = gathered.reshape(4, D // 4, T, 2 * half, width).transpose(0, 2, 1, 3, 4)
    gathered = gathered.reshape(4, 1, -1, width)
    middle = gathered.shape[2] // 2
    first, second = gathered[:, :, :middle], gathered[:, :, middle:].transpose(1, 0, 2, 3)
    order = jnp.stack([jnp.zeros(4, jnp.int32), jnp.arange(4, dtype=jnp.int32)], axis=1).reshape(-1)
    return (first, second, first, second, order), False


def weight_copies(refs, buf, sems, plane, other):
    first, second = refs[2 * other], refs[2 * other + 1]
    pairs, size = first.shape[1], first.shape[2]
    copies = [
        pltpu.make_async_copy(first.at[plane, x], buf.at[pl.ds(x * size, size)], sems.at[x])
        for x in range(pairs)
    ]
    pairs, at, size = second.shape[0], pairs * size, second.shape[2]
    return copies + [
        pltpu.make_async_copy(second.at[x, plane], buf.at[pl.ds(at + x * size, size)], sems.at[2 + x])
        for x in range(pairs)
    ]


def load_weight(refs, order_ref, number, buf, sems):
    for other in range(2):

        @pl.when(order_ref[2 * number] == other)
        def _():
            for copy in weight_copies(refs, buf, sems, order_ref[2 * number + 1], other):
                copy.start()


def weight_wait(refs, buf, sems):
    for copy in weight_copies(refs, buf, sems, 0, 0):
        copy.wait()


def weight_specs():
    return [pl.BlockSpec(memory_space=pl.ANY)] * 4 + [pl.BlockSpec(memory_space=pltpu.SMEM)]


def whole(shape, dims=0):
    return pl.BlockSpec(shape, lambda *_: (0,) * len(shape))


def block_of(rows):
    return 256 if rows % 256 == 0 else 128


def by_rows(size, width):
    return pl.BlockSpec((size, width), lambda i: (i, 0))


def by_columns(height, size):
    return pl.BlockSpec((height, size), lambda i: (0, i))


def project_kernel(x_ref, gain_ref, a_ref, mark_ref, sel_ref, *refs):
    *w_refs, order_ref, q_ref, k_ref, v_ref, low_ref, bufs, sems = refs
    i = pl.program_id(0)

    @pl.when(i == 0)
    def _():
        for j in range(3):
            load_weight(w_refs, order_ref, j, bufs.at[j], sems.at[j])

    z, _ = norm_parts(x_ref[...].astype(F32))
    n1 = (z * gain_ref[...]).astype(BF)
    for j, out_ref in enumerate((q_ref, k_ref, v_ref)):
        low = (mm(n1, a_ref[j]) * mark_ref[j]).astype(BF)
        low_ref[j] = mm_nt(sel_ref[j], low).astype(BF)

        @pl.when(i == 0)
        def _():
            weight_wait(w_refs, bufs.at[j], sems.at[j])

        out_ref[...] = mm_nt(bufs[j], jnp.concatenate([n1, low], axis=1)).astype(BF)


def project(x, gain, a, marks, sels, w):
    rows, width = x.shape
    AR, R = a.shape[2], sels.shape[1]
    size = rows
    return pl.pallas_call(
        project_kernel,
        grid=(rows // size,),
        in_specs=[
            by_rows(size, width),
            whole((1, width)),
            whole((3, width, AR)),
            whole((3, 1, AR)),
            whole((3, R, AR)),
            *weight_specs(),
        ],
        out_specs=[by_columns(width, size)] * 3 + [pl.BlockSpec((3, R, size), lambda i: (0, 0, i))],
        out_shape=[jax.ShapeDtypeStruct((width, rows), BF)] * 3 + [jax.ShapeDtypeStruct((3, R, rows), BF)],
        scratch_shapes=[
            pltpu.VMEM((3, width, width + AR), BF),
            pltpu.SemaphoreType.DMA((3, 4)),
        ],
        compiler_params=pltpu.CompilerParams(vmem_limit_bytes=56 * 2**20),
        cost_estimate=pl.CostEstimate(
            flops=6 * rows * width * width, bytes_accessed=6 * width * width, transcendentals=0
        ),
        name="project",
    )(x, gain, a, marks, sels, *w)


def leave_kernel(mixed_ref, x_ref, bo_ref, a1_ref, gain_ref, mark_ref, sel_ref, *refs):
    *w_refs, order_ref, hidden_ref, n2_ref, low_ref, buf, sems = refs
    i = pl.program_id(0)
    width = x_ref.shape[1]

    @pl.when(i == 0)
    def _():
        load_weight(w_refs, order_ref, 3, buf, sems)

    mixed = mixed_ref[...].T

    @pl.when(i == 0)
    def _():
        weight_wait(w_refs, buf, sems)

    both = mm(mixed, buf[...])
    low = (both[:, width:] * mark_ref[3]).astype(BF)
    low_ref[0] = mm_nt(sel_ref[3], low).astype(BF)
    hidden = x_ref[...].astype(F32) + both[:, :width] + mm(low, bo_ref[...])
    hidden_ref[...] = hidden
    z, _ = norm_parts(hidden)
    n2 = (z * gain_ref[...]).astype(BF)
    n2_ref[:, :width] = n2
    low = (mm(n2, a1_ref[...]) * mark_ref[4]).astype(BF)
    n2_ref[:, width:] = low
    low_ref[1] = mm_nt(sel_ref[4], low).astype(BF)


def leave(mixed, x, bo, a1, gain, marks, sels, w):
    rows, width = x.shape
    AR, R = a1.shape[1], sels.shape[1]
    size = block_of(rows)
    return pl.pallas_call(
        leave_kernel,
        grid=(rows // size,),
        in_specs=[
            by_columns(width, size),
            by_rows(size, width),
            whole((AR, width)),
            whole((width, AR)),
            whole((1, width)),
            whole((6, 1, AR)),
            whole((6, R, AR)),
            *weight_specs(),
        ],
        out_specs=[
            by_rows(size, width),
            by_rows(size, width + AR),
            pl.BlockSpec((2, R, size), lambda i: (0, 0, i)),
        ],
        out_shape=[
            jax.ShapeDtypeStruct((rows, width), F32),
            jax.ShapeDtypeStruct((rows, width + AR), BF),
            jax.ShapeDtypeStruct((2, R, rows), BF),
        ],
        scratch_shapes=[pltpu.VMEM((width, width + AR), BF), pltpu.SemaphoreType.DMA((4,))],
        compiler_params=pltpu.CompilerParams(vmem_limit_bytes=56 * 2**20),
        cost_estimate=pl.CostEstimate(
            flops=4 * rows * width * width, bytes_accessed=2 * width * width, transcendentals=0
        ),
        name="leave_attention",
    )(mixed, x, bo, a1, gain, marks, sels, *w)


def feed_kernel(
    x_ref, up_ref, live_ref, b2_ref, mark_ref, sel_ref, low_ref, w_ref, acc1_ref, acc2_ref, ga_ref, gb_ref, s_ref, ld_ref
):
    width = up_ref.shape[1]

    @pl.when(pl.program_id(0) == 0)
    def _():
        acc1_ref[...] = jnp.zeros_like(acc1_ref)
        acc2_ref[...] = jnp.zeros_like(acc2_ref)
        seed = (up_ref[...].astype(F32) * live_ref[...]).astype(BF)
        s_ref[:, :width] = seed
        low = (mm_nt(seed, b2_ref[...]) * mark_ref[5]).astype(BF)
        s_ref[:, width:] = low
        ld_ref[...] = mm_nt(sel_ref[5], low).astype(BF)

    wide = w_ref.shape[3]
    first = w_ref[:, 0].reshape(-1, wide)
    second = w_ref[:, 1].reshape(-1, wide)
    upper = mm_nt(x_ref[...], first)
    cdf = 0.5 * (1.0 + lax.erf(upper * (0.5**0.5)))
    active = (upper * cdf).astype(BF)
    dactive = mm_nt(s_ref[...], second)
    slope = cdf + upper * jnp.exp(-0.5 * upper * upper) * (1.0 / (2.0 * jnp.pi) ** 0.5)
    dupper = (dactive * slope).astype(BF)
    acc1_ref[...] += mm(active, second)
    acc2_ref[...] += mm(dupper, first)
    ga_ref[...] = mm(ld_ref[...], active)
    gb_ref[...] = mm(low_ref[1], dupper)


def feed(x, upstream, live, b2, marks, sels, low, w):
    rows, width = upstream.shape
    blocks, _, h, wide = w.shape
    AR, R = wide - width, low.shape[1]
    step = blocks
    while step * h > 1280:
        step //= 2
    part = pl.BlockSpec((R, step * h), lambda i: (0, i))
    return pl.pallas_call(
        feed_kernel,
        grid=(blocks // step,),
        in_specs=[
            whole((rows, wide)),
            whole((rows, width)),
            whole((rows, 1)),
            whole((AR, width)),
            whole((6, 1, AR)),
            whole((6, R, AR)),
            whole((2, R, rows)),
            pl.BlockSpec((step, 2, h, wide), lambda i: (i, 0, 0, 0)),
        ],
        out_specs=[whole((rows, wide)), whole((rows, wide)), part, part],
        out_shape=[jax.ShapeDtypeStruct((rows, wide), F32)] * 2
        + [jax.ShapeDtypeStruct((R, blocks * h), F32)] * 2,
        scratch_shapes=[pltpu.VMEM((rows, wide), BF), pltpu.VMEM((R, rows), BF)],
        compiler_params=pltpu.CompilerParams(vmem_limit_bytes=60 * 2**20),
        cost_estimate=pl.CostEstimate(
            flops=8 * rows * wide * blocks * h, bytes_accessed=4 * blocks * h * wide, transcendentals=0
        ),
        name="feed_forward",
    )(x, upstream, live, b2, marks, sels, low, w)


def turn_kernel(
    acc1_ref, acc2_ref, hidden_ref, n2_ref, up_ref, live_ref, mixed_ref, bo_ref, a1_ref, b2_ref, gain_ref,
    mark_ref, sel_ref, low_ref, *refs
):
    *w_refs, order_ref, layer_ref, dhidden_ref, dmixed_ref, grad_ref, buf, sems = refs
    i = pl.program_id(0)
    width = hidden_ref.shape[1]

    @pl.when(i == 0)
    def _():
        load_weight(w_refs, order_ref, 3, buf, sems)
        grad_ref[...] = jnp.zeros_like(grad_ref)

    hidden = hidden_ref[...]
    seed = (up_ref[...].astype(F32) * live_ref[...]).astype(BF)
    low = (acc1_ref[:, width:] * mark_ref[5]).astype(BF)
    branch = acc1_ref[:, :width] + mm(low, b2_ref[...])
    layer_ref[...] = jnp.where(live_ref[...] > 0, hidden + branch, 0.0).astype(BF)
    grad_ref[3] += mm(mm_nt(sel_ref[5], low).astype(BF), seed)
    low = (acc2_ref[:, width:] * mark_ref[4]).astype(BF)
    grad_ref[2] += mm(mm_nt(sel_ref[4], low).astype(BF), n2_ref[:, :width])
    dn2 = acc2_ref[:, :width] + mm_nt(low, a1_ref[...])
    z, rate = norm_parts(hidden)
    dhidden = seed.astype(F32) + norm_back(z, rate, dn2 * gain_ref[...])
    dhidden_ref[...] = dhidden
    dattn = dhidden.astype(BF)
    grad_ref[1] += mm(low_ref[0], dattn)
    low = (mm_nt(dattn, bo_ref[...]) * mark_ref[3]).astype(BF)
    grad_ref[0] += mm_nt(mm_nt(sel_ref[3], low).astype(BF), mixed_ref[...])

    @pl.when(i == 0)
    def _():
        weight_wait(w_refs, buf, sems)

    dmixed_ref[...] = mm_nt(buf[...], jnp.concatenate([dattn, low], axis=1)).astype(BF)


def turn(acc1, acc2, hidden, n2, upstream, live, mixed, bo, a1, b2, gain, marks, sels, low, w):
    rows, width = hidden.shape
    AR, R = a1.shape[1], sels.shape[1]
    size = block_of(rows)
    return pl.pallas_call(
        turn_kernel,
        grid=(rows // size,),
        in_specs=[
            by_rows(size, width + AR),
            by_rows(size, width + AR),
            by_rows(size, width),
            by_rows(size, width + AR),
            by_rows(size, width),
            by_rows(size, 1),
            by_columns(width, size),
            whole((AR, width)),
            whole((width, AR)),
            whole((AR, width)),
            whole((1, width)),
            whole((6, 1, AR)),
            whole((6, R, AR)),
            pl.BlockSpec((2, R, size), lambda i: (0, 0, i)),
            *weight_specs(),
        ],
        out_specs=[by_rows(size, width), by_rows(size, width), by_columns(width, size), whole((4, R, width))],
        out_shape=[
            jax.ShapeDtypeStruct((rows, width), BF),
            jax.ShapeDtypeStruct((rows, width), F32),
            jax.ShapeDtypeStruct((width, rows), BF),
            jax.ShapeDtypeStruct((4, R, width), F32),
        ],
        scratch_shapes=[pltpu.VMEM((width, width + AR), BF), pltpu.SemaphoreType.DMA((4,))],
        compiler_params=pltpu.CompilerParams(vmem_limit_bytes=56 * 2**20),
        cost_estimate=pl.CostEstimate(
            flops=4 * rows * width * width, bytes_accessed=16 * rows * width, transcendentals=0
        ),
        name="turn",
    )(acc1, acc2, hidden, n2, upstream, live, mixed, bo, a1, b2, gain, marks, sels, low, *w)


def finish_kernel(
    x_ref, dhidden_ref, gain_ref, a_ref, mark_ref, sel_ref, low_ref, dq_ref, dk_ref, dk2_ref, dv_ref, dv2_ref, *refs
):
    *w_refs, order_ref, out_ref, grad_ref, bufs, sems = refs
    i = pl.program_id(0)
    width = x_ref.shape[1]

    @pl.when(i == 0)
    def _():
        for j in range(3):
            load_weight(w_refs, order_ref, j, bufs.at[j], sems.at[j])
        grad_ref[...] = jnp.zeros_like(grad_ref)

    z, rate = norm_parts(x_ref[...].astype(F32))
    n1 = (z * gain_ref[...]).astype(BF)
    dn1 = jnp.zeros(x_ref.shape, F32)
    for j, own in enumerate((dq_ref, dk_ref, dv_ref)):
        dy = own[...]
        if j:
            dy = (dy.astype(F32) + (dk2_ref, dv2_ref)[j - 1][...].astype(F32)).astype(BF)

        @pl.when(i == 0)
        def _():
            weight_wait(w_refs, bufs.at[j], sems.at[j])

        both = mm(dy.T, bufs[j])
        low = (both[:, width:] * mark_ref[j]).astype(BF)
        grad_ref[0, j] += mm(mm_nt(sel_ref[j], low).astype(BF), n1)
        grad_ref[1, j] += mm_nt(low_ref[j], dy)
        dn1 = dn1 + both[:, :width] + mm_nt(low, a_ref[j])
    out_ref[...] = (dhidden_ref[...] + norm_back(z, rate, dn1 * gain_ref[...])).astype(BF)


def finish(x, dhidden, gain, a, marks, sels, low, dq, dk, dk2, dv, dv2, w):
    rows, width = x.shape
    AR, R = a.shape[2], sels.shape[1]
    size = block_of(rows)
    return pl.pallas_call(
        finish_kernel,
        grid=(rows // size,),
        in_specs=[
            by_rows(size, width),
            by_rows(size, width),
            whole((1, width)),
            whole((3, width, AR)),
            whole((3, 1, AR)),
            whole((3, R, AR)),
            pl.BlockSpec((3, R, size), lambda i: (0, 0, i)),
        ]
        + [by_columns(width, size)] * 5
        + weight_specs(),
        out_specs=[by_rows(size, width), whole((2, 3, R, width))],
        out_shape=[
            jax.ShapeDtypeStruct((rows, width), BF),
            jax.ShapeDtypeStruct((2, 3, R, width), F32),
        ],
        scratch_shapes=[
            pltpu.VMEM((3, width, width + AR), BF),
            pltpu.SemaphoreType.DMA((3, 4)),
        ],
        compiler_params=pltpu.CompilerParams(vmem_limit_bytes=58 * 2**20),
        cost_estimate=pl.CostEstimate(
            flops=6 * rows * width * width, bytes_accessed=6 * width * width, transcendentals=0
        ),
        name="finish",
    )(x, dhidden, gain, a, marks, sels, low, dq, dk, dk2, dv, dv2, *w)


def body(
    frames,
    upstream,
    clip_frame_length,
    clip_adapter_index,
    gain1,
    gain2,
    w_qkv,
    w_out,
    w_up,
    w_down,
    qkv_a,
    qkv_b,
    out_a,
    out_b,
    fc1_a,
    fc1_b,
    fc2_a,
    fc2_b,
):
    C, LF, W = frames.shape
    pl_ = Place(C, LF)
    D, T, d, t = pl_.D, pl_.T, pl_.d, pl_.t
    Hc = w_qkv.shape[2]
    U = w_up.shape[1]
    A, R = fc1_a.shape[0], fc1_a.shape[2]
    AR = A * R
    rows = pl_.rows
    heads = W // HEAD

    meta = jnp.concatenate([clip_frame_length[:, None], clip_adapter_index], axis=1)
    metas = lax.all_gather(meta, "dp")
    qkvo = jnp.concatenate([w_qkv.transpose(0, 2, 1), w_out[None]]).reshape(4 * Hc, W // D)
    qkvo = lax.all_to_all(qkvo, "dp", 0, 1, tiled=True)
    qkvo_low = jnp.concatenate(
        [qkv_b.transpose(0, 3, 1, 2).reshape(3, Hc, AR), out_a.transpose(1, 0, 2).reshape(1, Hc, AR)]
    ).reshape(D, 4 * Hc // D, AR)
    qkvo = jnp.concatenate([qkvo, lax.dynamic_index_in_dim(qkvo_low, d, 0, False)], axis=1)
    ffn = jnp.stack([w_up.T, w_down])
    ffn = lax.all_to_all(ffn, "dp", 1, 2, tiled=True)
    ffn_low = jnp.stack(
        [fc1_b.transpose(2, 0, 1).reshape(U, AR), fc2_a.transpose(1, 0, 2).reshape(U, AR)]
    ).reshape(2, D, U // D, AR)
    ffn = jnp.concatenate([ffn, lax.dynamic_index_in_dim(ffn_low, d, 1, False)], axis=2)
    count = qkvo.shape[0]
    half = count // 2
    heads_part = Gather(pl_, qkvo[:half], qkvo[half:])
    frames_by, upstream_by = by_chip(pl_, frames), by_chip(pl_, upstream)
    ffn = heads_part.line(ffn)
    frames_by, metas = tie([heads_part], frames_by, metas)
    all_ffn = lax.all_gather(ffn, ("tensor", "dp"))
    frames_in = to_clip(pl_, frames_by)
    heads_part.middle()
    heads_part.last()
    frames_in, upstream_by = tie([heads_part], frames_in, upstream_by)
    upstream_in = to_clip(pl_, upstream_by)
    heads_part.core()
    weights, line = heads_weights(pl_, heads_part.parts)

    g = t // pl_.Q
    here = metas[d - pl_.core + g // C, g % C]
    length, picks = here[0], here[1:]
    marks = (jnp.arange(AR)[None, :] // R == picks[:, None]).astype(F32)

    flat_a = lambda a: a.swapaxes(-3, -2).reshape(*a.shape[:-3], W, AR)
    flat_b = lambda b: b.reshape(AR, W)
    marks = marks[:, None, :]
    sels = (jnp.arange(AR)[None, None, :] == (picks * R)[:, None, None] + jnp.arange(R)[None, :, None]).astype(BF)
    live = (pl_.positions(pl_.core, t % pl_.Q) < length).astype(F32)[:, None]
    keys_live = jnp.concatenate([pl_.positions(c, s) for c, s in group_places(pl_)]) < length
    bias = jnp.where(keys_live, 0.0, -1e30).astype(F32)[None]
    gain1, gain2 = gain1[None], gain2[None]
    a_all = flat_a(qkv_a)

    q, k, v, low1 = project(frames_in, gain1, a_all, marks[:3], sels[:3], weights)
    ks, vs = group_values(pl_, k), group_values(pl_, v)
    mixed, lse = attend(q, ks, vs, bias)
    bo, a1, b2 = flat_b(out_b), flat_a(fc1_a), flat_b(fc2_b)
    hidden, n2, low2 = leave(mixed, frames_in, bo, a1, gain2, marks, sels, weights)
    hidden, n2, low2, upstream_in = tie([], hidden, n2, low2, upstream_in)
    acc1, acc2, unit_a, unit_b = feed(n2, upstream_in, live, b2, marks, sels, low2, all_ffn)
    layer_rows, dhidden, dmixed, grads2 = turn(
        acc1, acc2, hidden, n2, upstream_in, live, mixed, bo, a1, b2, gain2, marks, sels, low2, weights
    )
    head_order = places(pl_, True).reshape(T, D)[:, d] % T
    clips = metas.reshape(D // 2, 2 * C, 7)[:, :, 1:]
    clips = jnp.repeat(clips, pl_.Q, axis=1)[:, None]
    clips = jnp.broadcast_to(clips, (D // 2, 2, T, 6)).reshape(D, T, 6)
    clips = jnp.take(clips, d ^ jnp.arange(D), axis=0).reshape(D * T, 6)
    hot = (clips[:, :, None] == jnp.arange(A)).astype(BF)
    by_tensor = lambda v: v.reshape(R, T, -1)

    def by_head(v):
        if line:
            v = v.reshape(R, 2, T, -1).swapaxes(1, 2)
        return jnp.take(by_tensor(v), head_order, axis=1)

    def joined(terms):
        return jnp.concatenate([v.astype(BF) for v in terms], axis=2).swapaxes(0, 1)

    def owned(got, sizes, picks_of):
        got = to_owners(pl_, got)
        got = got.reshape(D * T, R // D, -1)
        out, at = [], 0
        for size, j in zip(sizes, picks_of):
            out.append(
                jnp.einsum("sa,srw->arw", hot[:, j], got[:, :, at : at + size], preferred_element_type=F32)
            )
            at += size
        return out

    wm = W // T
    terms = joined([by_head(grads2[0]), *map(by_tensor, (grads2[1], grads2[2], grads2[3], unit_b, unit_a))])
    layer_output, early = from_clip(pl_, layer_rows, terms)
    dq, *dkv = attend_back(q, ks, vs, bias, lse, mixed, dmixed)
    dks, dvs = dkv[: len(dkv) // 2], dkv[len(dkv) // 2 :]
    dk2, dv2 = group_received(pl_, dks), group_received(pl_, dvs)
    dq, layer_output, early = tie([], dq, layer_output, early)
    dframes, grads1 = finish(
        frames_in, dhidden, gain1, a_all, marks[:3], sels[:3], low1, dq, dks[0], dk2, dvs[0], dv2, weights
    )
    out_ga, out_gb, fc1_ga, fc2_gb, fc1_gb, fc2_ga = owned(early, (wm,) * 4 + (U,) * 2, (3, 3, 4, 5, 4, 5))
    terms = joined([by_tensor(grads1[0, j]) for j in range(3)] + [by_head(grads1[1, j]) for j in range(3)])
    frames_grad, late = from_clip(pl_, dframes, terms)
    frames_grad = frames_grad.astype(F32)
    late = owned(late, (wm,) * 6, (0, 1, 2, 0, 1, 2))
    flip = lambda a: jnp.swapaxes(a, -1, -2)
    return (
        layer_output,
        frames_grad,
        flip(jnp.stack(late[:3])),
        jnp.stack(late[3:]),
        flip(out_ga),
        out_gb,
        flip(fc1_ga),
        fc1_gb,
        flip(fc2_ga),
        fc2_gb,
    )


def solution(mesh):
    placed = (
        P("dp", "tensor", None),
        P("dp", "tensor", None),
        P("dp"),
        P("dp", None),
        P(),
        P(),
        P(None, "dp", "tensor"),
        P("tensor", "dp"),
        P("dp", "tensor"),
        P("tensor", "dp"),
        P(),
        P(None, None, None, "tensor"),
        P(None, "tensor", None),
        P(),
        P(),
        P(None, None, "tensor"),
        P(None, "tensor", None),
        P(),
    )
    return jax.shard_map(
        body,
        mesh=mesh,
        in_specs=placed,
        out_specs=(
            P("dp", "tensor", None),
            P("dp", "tensor", None),
            P(None, None, "tensor", "dp"),
            P(None, None, "dp", "tensor"),
            P(None, "tensor", "dp"),
            P(None, "dp", "tensor"),
            P(None, "tensor", "dp"),
            P(None, "dp", "tensor"),
            P(None, "tensor", "dp"),
            P(None, "dp", "tensor"),
        ),
        check_vma=False,
    )
```

```python
import functools

import jax
import jax.numpy as jnp
from jax import lax
from jax.experimental import pallas as pl
from jax.experimental.pallas import tpu as pltpu
from jax.sharding import PartitionSpec as P

HEAD = 80
BF = jnp.bfloat16
F32 = jnp.float32


def mm(a, b):
    return jnp.dot(a, b, preferred_element_type=F32)


def mm_nt(a, b):
    return lax.dot_general(a, b, (((1,), (1,)), ((), ())), preferred_element_type=F32)


def mm_tn(a, b):
    return lax.dot_general(a, b, (((0,), (0,)), ((), ())), preferred_element_type=F32)


def norm_parts(values):
    center = values - jnp.mean(values, axis=-1, keepdims=True)
    rate = lax.rsqrt(jnp.mean(center * center, axis=-1, keepdims=True) + 1e-5)
    return center * rate, rate


def norm_back(z, rate, grad):
    return rate * (
        grad
        - jnp.mean(grad, axis=-1, keepdims=True)
        - z * jnp.mean(grad * z, axis=-1, keepdims=True)
    )


class Place:
    def __init__(self, clips, local_frames):
        self.D, self.T = lax.axis_size("dp"), lax.axis_size("tensor")
        self.d, self.t = lax.axis_index("dp"), lax.axis_index("tensor")
        self.core = self.d % 2
        self.C, self.LF = clips, local_frames
        self.Q = self.T // (2 * clips)
        self.S = local_frames // (2 * self.Q)
        self.rows = self.T * self.S
        self.swap = [(i, i ^ 1) for i in range(self.D)]

    def swap_core(self, x):
        return lax.ppermute(x, "dp", self.swap)

    def positions(self, core, q):
        source = jnp.arange(self.T, dtype=jnp.int32)[:, None] * self.LF
        inner = (q * 2 + core) * self.S + jnp.arange(self.S, dtype=jnp.int32)[None, :]
        return (source + inner).reshape(self.rows)


def by_chip(pl_, x):
    C, LF, W = x.shape
    parts = x.reshape(C, pl_.Q, 2, pl_.S, W)
    even, odd = parts[:, :, 0], parts[:, :, 1]
    first = pl_.core == 0
    mine, theirs = jnp.where(first, even, odd), jnp.where(first, odd, even)
    got = pl_.swap_core(theirs)
    both = jnp.stack([jnp.where(first, mine, got), jnp.where(first, got, mine)])
    return both.reshape(pl_.T, pl_.S, W)


def to_clip(pl_, both):
    return lax.all_to_all(both, "tensor", 0, 0).reshape(pl_.rows, both.shape[2])


def from_clip(pl_, y, terms):
    W = y.shape[-1]
    T = pl_.T
    sent = jnp.concatenate([y.reshape(T, pl_.S, W), terms.astype(BF).reshape(T, -1, W)], axis=1)
    return lax.all_to_all(sent, "tensor", 0, 0)


def from_sources(pl_, got, R):
    T, _, W = got.shape
    both = got[:, : pl_.S].reshape(2, pl_.C, pl_.Q, pl_.S, W)
    first = pl_.core == 0
    mine, theirs = jnp.where(first, both[0], both[1]), jnp.where(first, both[1], both[0])
    other = pl_.swap_core(theirs)
    even, odd = jnp.where(first, mine, other), jnp.where(first, other, mine)
    rows = jnp.stack([even, odd], axis=2).reshape(pl_.C, pl_.LF, W)
    return rows, got[:, pl_.S :].reshape(T, R, -1)


def to_owners(pl_, terms):
    T, R, w = terms.shape
    D = pl_.D
    parts = terms.reshape(T, D, R // D, w).swapaxes(0, 1)
    out = []
    for step in range(D):
        part = lax.dynamic_index_in_dim(parts, pl_.d ^ step, 0, False)
        out.append(lax.ppermute(part, "dp", [(i, i ^ step) for i in range(D)]) if step else part)
    return jnp.stack(out)


def ring(x, axis, stride, size):
    perm = [(i, (i + stride) % size) for i in range(size)]
    out = [x]
    for _ in range(size // stride - 1):
        out.append(lax.ppermute(out[-1], axis, perm))
    return jnp.stack(out)


class Gather:
    def __init__(self, place, first, second):
        self.place = place
        self.parts = (first, second)

    def line(self, between):
        size = self.place.T
        perm = [(i, (i + 2) % size) for i in range(size)]
        lines = [[v] for v in self.parts]
        for step in range(size // 2 - 1):
            for line in lines:
                line.append(lax.ppermute(line[-1], "tensor", perm))
            if step == 0:
                lines, between = lax.optimization_barrier((lines, between))
        self.parts = [jnp.stack(line) for line in lines]
        return between

    def pair(self, v):
        perm = [(i, i ^ 1) for i in range(self.place.T)]
        return jnp.stack([v, lax.ppermute(v, "tensor", perm)])

    def plane(self, v):
        return ring(v, "dp", 2, self.place.D)

    def middle(self):
        self.parts = [self.pair(self.parts[0]), self.plane(self.parts[1])]

    def last(self):
        self.parts = [self.plane(self.parts[0]), self.pair(self.parts[1])]

    def core(self):
        self.parts = [*self.parts, *[self.place.swap_core(v) for v in self.parts]]


def tie(gathers, *values):
    moved = [g.parts for g in gathers]
    moved, values = lax.optimization_barrier((moved, values))
    for g, parts in zip(gathers, moved):
        g.parts = list(parts)
    return values


def places(pl_, pair_first):
    T, D = pl_.T, pl_.D
    tt, dd = jnp.meshgrid(jnp.arange(T), jnp.arange(D), indexing="ij")
    fx = (pl_.t ^ tt) & 1
    s = ((pl_.t ^ fx) - tt) // 2 % (T // 2)
    fc = (pl_.d ^ dd) & 1
    u = ((pl_.d ^ fc) - dd) // 2 % (D // 2)
    if pair_first:
        index = ((fc * (D // 2) + u) * 2 + fx) * (T // 2) + s
    else:
        index = ((fc * 2 + fx) * (D // 2) + u) * (T // 2) + s
    return index.reshape(-1)


def plane_places(pl_):
    dd = jnp.arange(pl_.D)
    fc = (pl_.d ^ dd) & 1
    return fc * (pl_.D // 2) + ((pl_.d ^ fc) - dd) // 2 % (pl_.D // 2)


def group_values(pl_, x):
    out = [x, pl_.swap_core(x)]
    for step in range(1, pl_.Q):
        perm = [
            (i, i - i % pl_.Q + (i + step) % pl_.Q) for i in range(pl_.T)
        ]
        out.append(lax.ppermute(out[0], "tensor", perm))
        out.append(lax.ppermute(out[1], "tensor", perm))
    return out


def group_places(pl_):
    q = pl_.t % pl_.Q
    out = []
    for step in range(pl_.Q):
        sender = (q - step) % pl_.Q
        out.append((pl_.core, sender))
        out.append((1 - pl_.core, sender))
    return out


def group_received(pl_, blocks):
    total = pl_.swap_core(blocks[1])
    for step in range(1, pl_.Q):
        perm = [(i - i % pl_.Q + (i + step) % pl_.Q, i) for i in range(pl_.T)]
        own = lax.ppermute(blocks[2 * step], "tensor", perm)
        other = lax.ppermute(pl_.swap_core(blocks[2 * step + 1]), "tensor", perm)
        total = (total.astype(F32) + own.astype(F32) + other.astype(F32)).astype(BF)
    return total


RATE = HEAD**-0.5
TO_LOG2 = RATE * 1.4426950408889634
EXTRA = 16


def attend_kernel(q_ref, k_refs, v_refs, bias_ref, out_ref, expo_ref, inverse_ref):
    rows = q_ref.shape[1]
    keys = bias_ref.shape[1]
    k = jnp.concatenate(
        [jnp.concatenate([r[...] for r in k_refs], axis=1), bias_ref[...].astype(BF), jnp.zeros((EXTRA - 1, keys), BF)]
    ).T
    v = jnp.concatenate(
        [jnp.concatenate([r[...] for r in v_refs], axis=1), jnp.ones((EXTRA, keys), BF)]
    )
    q = jnp.concatenate([q_ref[...], jnp.ones((EXTRA, rows), BF)])
    scores = mm(k, q)
    top = jnp.max(scores, axis=0, keepdims=True)
    expo = jnp.exp2((scores - top) * TO_LOG2).astype(BF)
    expo_ref[0] = expo
    both = mm(v, expo)
    total = both[HEAD : HEAD + 1]
    out_ref[...] = (both[:HEAD] / total).astype(BF)
    inverse_ref[0] = 1.0 / total


def attend(q, ks, vs, bias):
    width, rows = q.shape
    heads, n = width // HEAD, len(ks)
    head = pl.BlockSpec((HEAD, rows), lambda h: (h, 0))

    def kernel(*refs):
        attend_kernel(refs[0], refs[1 : 1 + n], refs[1 + n : 1 + 2 * n], *refs[1 + 2 * n :])

    return pl.pallas_call(
        kernel,
        grid=(heads,),
        in_specs=[head] * (1 + 2 * n) + [pl.BlockSpec(bias.shape, lambda h: (0, 0))],
        out_specs=[
            head,
            pl.BlockSpec((1, bias.shape[1], rows), lambda h: (h, 0, 0)),
            pl.BlockSpec((1, 1, rows), lambda h: (h, 0, 0)),
        ],
        out_shape=[
            jax.ShapeDtypeStruct((width, rows), BF),
            jax.ShapeDtypeStruct((heads, bias.shape[1], rows), BF),
            jax.ShapeDtypeStruct((heads, 1, rows), F32),
        ],
        compiler_params=pltpu.CompilerParams(vmem_limit_bytes=56 * 2**20),
        cost_estimate=pl.CostEstimate(
            flops=4 * heads * rows * bias.shape[1] * 256, bytes_accessed=6 * width * rows, transcendentals=0
        ),
        name="attend_forward",
    )(q, *ks, *vs, bias)


def attend_back_kernel(
    q_ref, k_refs, v_refs, expo_ref, inverse_ref, mixed_ref, dmixed_ref, dq_ref, dk_refs, dv_refs, *, span
):
    rows = q_ref.shape[1]
    keys = expo_ref.shape[1]
    k = jnp.concatenate([r[...] for r in k_refs], axis=1)
    v = jnp.concatenate(
        [jnp.concatenate([r[...] for r in v_refs], axis=1), jnp.ones((EXTRA, keys), BF)]
    ).T
    inverse = inverse_ref[0]
    dmixed = dmixed_ref[...].astype(F32)
    delta = -jnp.sum(dmixed * mixed_ref[...].astype(F32), axis=0, keepdims=True) * inverse
    d0 = delta.astype(BF)
    d1 = (delta - d0.astype(F32)).astype(BF)
    dmixed = (dmixed * inverse).astype(BF)
    dmixed_more = jnp.concatenate([dmixed, d0, d1, jnp.zeros((EXTRA - 2, rows), BF)])
    q = q_ref[...]
    dk = jnp.zeros((HEAD, keys), F32)
    dv = jnp.zeros((HEAD, keys), F32)
    for start in range(0, rows, span):
        part = slice(start, start + span)
        expo = expo_ref[0, :, part]
        dscores = (expo.astype(F32) * mm(v, dmixed_more[:, part])).astype(BF)
        dq_ref[:, part] = (mm(k, dscores) * RATE).astype(BF)
        dk = dk + mm_nt(q[:, part], dscores)
        dv = dv + mm_nt(dmixed[:, part], expo)
    for i, (dk_ref, dv_ref) in enumerate(zip(dk_refs, dv_refs)):
        part = slice(i * rows, (i + 1) * rows)
        dk_ref[...] = (dk[:, part] * RATE).astype(BF)
        dv_ref[...] = dv[:, part].astype(BF)


def attend_back(q, ks, vs, expo, inverse, mixed, dmixed):
    width, rows = q.shape
    keys = expo.shape[1]
    heads, n = width // HEAD, len(ks)
    span = rows
    head = pl.BlockSpec((HEAD, rows), lambda h: (h, 0))

    def kernel(*refs):
        ins, outs = refs[: 5 + 2 * n], refs[5 + 2 * n :]
        attend_back_kernel(
            ins[0], ins[1 : 1 + n], ins[1 + n : 1 + 2 * n], *ins[1 + 2 * n :], outs[0], outs[1 : 1 + n], outs[1 + n :], span=span
        )

    return pl.pallas_call(
        kernel,
        grid=(heads,),
        in_specs=[head] * (1 + 2 * n)
        + [
            pl.BlockSpec((1, keys, rows), lambda h: (h, 0, 0)),
            pl.BlockSpec((1, 1, rows), lambda h: (h, 0, 0)),
            head,
            head,
        ],
        out_specs=[head] * (1 + 2 * n),
        out_shape=[jax.ShapeDtypeStruct((width, rows), BF)] * (1 + 2 * n),
        compiler_params=pltpu.CompilerParams(vmem_limit_bytes=56 * 2**20),
        cost_estimate=pl.CostEstimate(
            flops=8 * heads * rows * keys * 256, bytes_accessed=12 * width * rows, transcendentals=0
        ),
        name="attend_backward",
    )(q, *ks, *vs, expo, inverse, mixed, dmixed)


def heads_weights(pl_, parts):
    first, second, first_other, second_other = parts
    planes, pairs, lines, half, width = first.shape
    D, T = pl_.D, pl_.T
    if D == 4 and half == HEAD:
        index = plane_places(pl_)
        order = jnp.stack([index // 2, index % 2], axis=1).reshape(-1).astype(jnp.int32)
        flat = lambda v: v.reshape(*v.shape[:2], lines * half, width)
        return (flat(first), flat(second), flat(first_other), flat(second_other), order), True
    gathered = [
        jnp.stack([first, first_other]).reshape(D, T, half, width),
        jnp.stack([second, second_other]).transpose(0, 2, 1, 3, 4, 5).reshape(D, T, half, width),
    ]
    index = plane_places(pl_)
    gathered = [[lax.dynamic_index_in_dim(v, index[i], 0, False) for v in gathered] for i in range(D)]
    gathered = jnp.stack([jnp.concatenate(v, axis=1) for v in gathered])
    gathered = gathered.reshape(4, D // 4, T, 2 * half, width).transpose(0, 2, 1, 3, 4)
    gathered = gathered.reshape(4, 1, -1, width)
    middle = gathered.shape[2] // 2
    first, second = gathered[:, :, :middle], gathered[:, :, middle:].transpose(1, 0, 2, 3)
    order = jnp.stack([jnp.zeros(4, jnp.int32), jnp.arange(4, dtype=jnp.int32)], axis=1).reshape(-1)
    return (first, second, first, second, order), False


def weight_copies(refs, buf, sems, plane, other):
    first, second = refs[2 * other], refs[2 * other + 1]
    pairs, size = first.shape[1], first.shape[2]
    copies = [
        pltpu.make_async_copy(first.at[plane, x], buf.at[pl.ds(x * size, size)], sems.at[x])
        for x in range(pairs)
    ]
    pairs, at, size = second.shape[0], pairs * size, second.shape[2]
    return copies + [
        pltpu.make_async_copy(second.at[x, plane], buf.at[pl.ds(at + x * size, size)], sems.at[2 + x])
        for x in range(pairs)
    ]


def load_weight(refs, order_ref, number, buf, sems):
    for other in range(2):

        @pl.when(order_ref[2 * number] == other)
        def _():
            for copy in weight_copies(refs, buf, sems, order_ref[2 * number + 1], other):
                copy.start()


def weight_wait(refs, buf, sems):
    for copy in weight_copies(refs, buf, sems, 0, 0):
        copy.wait()


def weight_specs():
    return [pl.BlockSpec(memory_space=pl.ANY)] * 4 + [pl.BlockSpec(memory_space=pltpu.SMEM)]


def whole(shape, dims=0):
    return pl.BlockSpec(shape, lambda *_: (0,) * len(shape))


def block_of(rows):
    return 256 if rows % 256 == 0 else 128


def by_rows(size, width):
    return pl.BlockSpec((size, width), lambda i: (i, 0))


def by_columns(height, size):
    return pl.BlockSpec((height, size), lambda i: (0, i))


def project_kernel(x_ref, gain_ref, a_ref, mark_ref, sel_ref, *refs):
    *w_refs, order_ref, q_ref, k_ref, v_ref, low_ref, bufs, sems = refs
    i = pl.program_id(0)

    @pl.when(i == 0)
    def _():
        for j in range(3):
            load_weight(w_refs, order_ref, j, bufs.at[j], sems.at[j])

    z, _ = norm_parts(x_ref[...].astype(F32))
    n1 = (z * gain_ref[...]).astype(BF)
    for j, out_ref in enumerate((q_ref, k_ref, v_ref)):
        low = (mm(n1, a_ref[j]) * mark_ref[j]).astype(BF)
        low_ref[j] = mm_nt(sel_ref[j], low).astype(BF)

        @pl.when(i == 0)
        def _():
            weight_wait(w_refs, bufs.at[j], sems.at[j])

        out_ref[...] = mm_nt(bufs[j], jnp.concatenate([n1, low], axis=1)).astype(BF)


def project(x, gain, a, marks, sels, w):
    rows, width = x.shape
    AR, R = a.shape[2], sels.shape[1]
    size = rows
    return pl.pallas_call(
        project_kernel,
        grid=(rows // size,),
        in_specs=[
            by_rows(size, width),
            whole((1, width)),
            whole((3, width, AR)),
            whole((3, 1, AR)),
            whole((3, R, AR)),
            *weight_specs(),
        ],
        out_specs=[by_columns(width, size)] * 3 + [pl.BlockSpec((3, R, size), lambda i: (0, 0, i))],
        out_shape=[jax.ShapeDtypeStruct((width, rows), BF)] * 3 + [jax.ShapeDtypeStruct((3, R, rows), BF)],
        scratch_shapes=[
            pltpu.VMEM((3, width, width + AR), BF),
            pltpu.SemaphoreType.DMA((3, 4)),
        ],
        compiler_params=pltpu.CompilerParams(vmem_limit_bytes=56 * 2**20),
        cost_estimate=pl.CostEstimate(
            flops=6 * rows * width * width, bytes_accessed=6 * width * width, transcendentals=0
        ),
        name="project",
    )(x, gain, a, marks, sels, *w)


def leave_kernel(mixed_ref, x_ref, bo_ref, a1_ref, gain_ref, mark_ref, sel_ref, *refs):
    *w_refs, order_ref, hidden_ref, n2_ref, low_ref, buf, sems = refs
    i = pl.program_id(0)
    width = x_ref.shape[1]

    @pl.when(i == 0)
    def _():
        load_weight(w_refs, order_ref, 3, buf, sems)

    mixed = mixed_ref[...].T

    @pl.when(i == 0)
    def _():
        weight_wait(w_refs, buf, sems)

    both = mm(mixed, buf[...])
    low = (both[:, width:] * mark_ref[3]).astype(BF)
    low_ref[0] = mm_nt(sel_ref[3], low).astype(BF)
    hidden = x_ref[...].astype(F32) + both[:, :width] + mm(low, bo_ref[...])
    hidden_ref[...] = hidden
    z, _ = norm_parts(hidden)
    n2 = (z * gain_ref[...]).astype(BF)
    n2_ref[:, :width] = n2
    low = (mm(n2, a1_ref[...]) * mark_ref[4]).astype(BF)
    n2_ref[:, width:] = low
    low_ref[1] = mm_nt(sel_ref[4], low).astype(BF)


def leave(mixed, x, bo, a1, gain, marks, sels, w):
    rows, width = x.shape
    AR, R = a1.shape[1], sels.shape[1]
    size = block_of(rows)
    return pl.pallas_call(
        leave_kernel,
        grid=(rows // size,),
        in_specs=[
            by_columns(width, size),
            by_rows(size, width),
            whole((AR, width)),
            whole((width, AR)),
            whole((1, width)),
            whole((6, 1, AR)),
            whole((6, R, AR)),
            *weight_specs(),
        ],
        out_specs=[
            by_rows(size, width),
            by_rows(size, width + AR),
            pl.BlockSpec((2, R, size), lambda i: (0, 0, i)),
        ],
        out_shape=[
            jax.ShapeDtypeStruct((rows, width), F32),
            jax.ShapeDtypeStruct((rows, width + AR), BF),
            jax.ShapeDtypeStruct((2, R, rows), BF),
        ],
        scratch_shapes=[pltpu.VMEM((width, width + AR), BF), pltpu.SemaphoreType.DMA((4,))],
        compiler_params=pltpu.CompilerParams(vmem_limit_bytes=56 * 2**20),
        cost_estimate=pl.CostEstimate(
            flops=4 * rows * width * width, bytes_accessed=2 * width * width, transcendentals=0
        ),
        name="leave_attention",
    )(mixed, x, bo, a1, gain, marks, sels, *w)


def feed_kernel(
    x_ref, up_ref, live_ref, b2_ref, mark_ref, sel_ref, low_ref, w_ref, l_ref, acc1_ref, acc2_ref, ga_ref, gb_ref, s_ref, ld_ref
):
    width = up_ref.shape[1]

    @pl.when(pl.program_id(0) == 0)
    def _():
        acc1_ref[...] = jnp.zeros_like(acc1_ref)
        acc2_ref[...] = jnp.zeros_like(acc2_ref)
        seed = (up_ref[...].astype(F32) * live_ref[...]).astype(BF)
        s_ref[:, :width] = seed
        low = (mm_nt(seed, b2_ref[...]) * mark_ref[5]).astype(BF)
        s_ref[:, width:] = low
        ld_ref[...] = mm_nt(sel_ref[5], low).astype(BF)

    wide = w_ref.shape[3]
    first = w_ref[:, 0].reshape(-1, wide)
    second = w_ref[:, 1].reshape(-1, wide)
    upper = mm_nt(x_ref[:, :width], first) + mm(x_ref[:, width:], l_ref[0])
    cdf = 0.5 * (1.0 + lax.erf(upper * (0.5**0.5)))
    active = (upper * cdf).astype(BF)
    dactive = mm_nt(s_ref[:, :width], second) + mm(s_ref[:, width:], l_ref[1])
    slope = cdf + upper * jnp.exp(-0.5 * upper * upper) * (1.0 / (2.0 * jnp.pi) ** 0.5)
    dupper = (dactive * slope).astype(BF)
    acc1_ref[:, :width] += mm(active, second)
    acc1_ref[:, width:] += mm_nt(active, l_ref[1])
    acc2_ref[:, :width] += mm(dupper, first)
    acc2_ref[:, width:] += mm_nt(dupper, l_ref[0])
    ga_ref[...] = mm(ld_ref[...], active)
    gb_ref[...] = mm(low_ref[1], dupper)


def feed(x, upstream, live, b2, marks, sels, low, w, inner):
    rows, width = upstream.shape
    blocks, _, h, _ = w.shape
    wide = x.shape[1]
    AR, R = wide - width, low.shape[1]
    step = blocks
    while step * h > 1280:
        step //= 2
    part = pl.BlockSpec((R, step * h), lambda i: (0, i))
    return pl.pallas_call(
        feed_kernel,
        grid=(blocks // step,),
        in_specs=[
            whole((rows, wide)),
            whole((rows, width)),
            whole((rows, 1)),
            whole((AR, width)),
            whole((6, 1, AR)),
            whole((6, R, AR)),
            whole((2, R, rows)),
            pl.BlockSpec((step, 2, h, width), lambda i: (i, 0, 0, 0)),
            pl.BlockSpec((2, AR, step * h), lambda i: (0, 0, i)),
        ],
        out_specs=[whole((rows, wide)), whole((rows, wide)), part, part],
        out_shape=[jax.ShapeDtypeStruct((rows, wide), F32)] * 2
        + [jax.ShapeDtypeStruct((R, blocks * h), F32)] * 2,
        scratch_shapes=[pltpu.VMEM((rows, wide), BF), pltpu.VMEM((R, rows), BF)],
        compiler_params=pltpu.CompilerParams(vmem_limit_bytes=60 * 2**20),
        cost_estimate=pl.CostEstimate(
            flops=8 * rows * wide * blocks * h, bytes_accessed=4 * blocks * h * wide, transcendentals=0
        ),
        name="feed_forward",
    )(x, upstream, live, b2, marks, sels, low, w, inner)


def turn_kernel(
    acc1_ref, acc2_ref, hidden_ref, n2_ref, up_ref, live_ref, mixed_ref, bo_ref, a1_ref, b2_ref, gain_ref,
    mark_ref, sel_ref, low_ref, *refs
):
    *w_refs, order_ref, layer_ref, dhidden_ref, dmixed_ref, grad_ref, buf, sems = refs
    i = pl.program_id(0)
    width = hidden_ref.shape[1]

    @pl.when(i == 0)
    def _():
        load_weight(w_refs, order_ref, 3, buf, sems)
        grad_ref[...] = jnp.zeros_like(grad_ref)

    hidden = hidden_ref[...]
    seed = (up_ref[...].astype(F32) * live_ref[...]).astype(BF)
    low = (acc1_ref[:, width:] * mark_ref[5]).astype(BF)
    branch = acc1_ref[:, :width] + mm(low, b2_ref[...])
    layer_ref[...] = jnp.where(live_ref[...] > 0, hidden + branch, 0.0).astype(BF)
    grad_ref[3] += mm(mm_nt(sel_ref[5], low).astype(BF), seed)
    low = (acc2_ref[:, width:] * mark_ref[4]).astype(BF)
    grad_ref[2] += mm(mm_nt(sel_ref[4], low).astype(BF), n2_ref[:, :width])
    dn2 = acc2_ref[:, :width] + mm_nt(low, a1_ref[...])
    z, rate = norm_parts(hidden)
    dhidden = seed.astype(F32) + norm_back(z, rate, dn2 * gain_ref[...])
    dhidden_ref[...] = dhidden
    dattn = dhidden.astype(BF)
    grad_ref[1] += mm(low_ref[0], dattn)
    low = (mm_nt(dattn, bo_ref[...]) * mark_ref[3]).astype(BF)
    grad_ref[0] += mm_nt(mm_nt(sel_ref[3], low).astype(BF), mixed_ref[...])

    @pl.when(i == 0)
    def _():
        weight_wait(w_refs, buf, sems)

    dmixed_ref[...] = mm_nt(buf[...], jnp.concatenate([dattn, low], axis=1)).astype(BF)


def turn(acc1, acc2, hidden, n2, upstream, live, mixed, bo, a1, b2, gain, marks, sels, low, w):
    rows, width = hidden.shape
    AR, R = a1.shape[1], sels.shape[1]
    size = block_of(rows)
    return pl.pallas_call(
        turn_kernel,
        grid=(rows // size,),
        in_specs=[
            by_rows(size, width + AR),
            by_rows(size, width + AR),
            by_rows(size, width),
            by_rows(size, width + AR),
            by_rows(size, width),
            by_rows(size, 1),
            by_columns(width, size),
            whole((AR, width)),
            whole((width, AR)),
            whole((AR, width)),
            whole((1, width)),
            whole((6, 1, AR)),
            whole((6, R, AR)),
            pl.BlockSpec((2, R, size), lambda i: (0, 0, i)),
            *weight_specs(),
        ],
        out_specs=[by_rows(size, width), by_rows(size, width), by_columns(width, size), whole((4, R, width))],
        out_shape=[
            jax.ShapeDtypeStruct((rows, width), BF),
            jax.ShapeDtypeStruct((rows, width), F32),
            jax.ShapeDtypeStruct((width, rows), BF),
            jax.ShapeDtypeStruct((4, R, width), F32),
        ],
        scratch_shapes=[pltpu.VMEM((width, width + AR), BF), pltpu.SemaphoreType.DMA((4,))],
        compiler_params=pltpu.CompilerParams(vmem_limit_bytes=56 * 2**20),
        cost_estimate=pl.CostEstimate(
            flops=4 * rows * width * width, bytes_accessed=16 * rows * width, transcendentals=0
        ),
        name="turn",
    )(acc1, acc2, hidden, n2, upstream, live, mixed, bo, a1, b2, gain, marks, sels, low, *w)


def finish_kernel(
    x_ref, dhidden_ref, gain_ref, a_ref, mark_ref, sel_ref, low_ref, dq_ref, dk_ref, dk2_ref, dv_ref, dv2_ref, *refs
):
    *w_refs, order_ref, out_ref, grad_ref, bufs, sems = refs
    i = pl.program_id(0)
    width = x_ref.shape[1]

    @pl.when(i == 0)
    def _():
        for j in range(3):
            load_weight(w_refs, order_ref, j, bufs.at[j], sems.at[j])
        grad_ref[...] = jnp.zeros_like(grad_ref)

    z, rate = norm_parts(x_ref[...].astype(F32))
    n1 = (z * gain_ref[...]).astype(BF)
    dn1 = jnp.zeros(x_ref.shape, F32)
    lows, picked = [], []
    for j, own in enumerate((dq_ref, dk_ref, dv_ref)):
        dy = own[...]
        if j:
            dy = (dy.astype(F32) + (dk2_ref, dv2_ref)[j - 1][...].astype(F32)).astype(BF)

        @pl.when(i == 0)
        def _():
            weight_wait(w_refs, bufs.at[j], sems.at[j])

        both = mm(dy.T, bufs[j])
        low = (both[:, width:] * mark_ref[j]).astype(BF)
        lows.append(low)
        picked.append(mm_nt(sel_ref[j], low).astype(BF))
        grad_ref[1, j] += mm_nt(low_ref[j], dy)
        dn1 = dn1 + both[:, :width]
    dn1 = dn1 + mm_nt(jnp.concatenate(lows, axis=1), jnp.concatenate([a_ref[j] for j in range(3)], axis=1))
    grads = mm(jnp.concatenate(picked), n1)
    R = sel_ref.shape[1]
    for j in range(3):
        grad_ref[0, j] += grads[j * R : (j + 1) * R]
    out_ref[...] = (dhidden_ref[...] + norm_back(z, rate, dn1 * gain_ref[...])).astype(BF)


def finish(x, dhidden, gain, a, marks, sels, low, dq, dk, dk2, dv, dv2, w):
    rows, width = x.shape
    AR, R = a.shape[2], sels.shape[1]
    size = block_of(rows)
    return pl.pallas_call(
        finish_kernel,
        grid=(rows // size,),
        in_specs=[
            by_rows(size, width),
            by_rows(size, width),
            whole((1, width)),
            whole((3, width, AR)),
            whole((3, 1, AR)),
            whole((3, R, AR)),
            pl.BlockSpec((3, R, size), lambda i: (0, 0, i)),
        ]
        + [by_columns(width, size)] * 5
        + weight_specs(),
        out_specs=[by_rows(size, width), whole((2, 3, R, width))],
        out_shape=[
            jax.ShapeDtypeStruct((rows, width), BF),
            jax.ShapeDtypeStruct((2, 3, R, width), F32),
        ],
        scratch_shapes=[
            pltpu.VMEM((3, width, width + AR), BF),
            pltpu.SemaphoreType.DMA((3, 4)),
        ],
        compiler_params=pltpu.CompilerParams(vmem_limit_bytes=58 * 2**20),
        cost_estimate=pl.CostEstimate(
            flops=6 * rows * width * width, bytes_accessed=6 * width * width, transcendentals=0
        ),
        name="finish",
    )(x, dhidden, gain, a, marks, sels, low, dq, dk, dk2, dv, dv2, *w)


def body(
    frames,
    upstream,
    clip_frame_length,
    clip_adapter_index,
    gain1,
    gain2,
    w_qkv,
    w_out,
    w_up,
    w_down,
    qkv_a,
    qkv_b,
    out_a,
    out_b,
    fc1_a,
    fc1_b,
    fc2_a,
    fc2_b,
):
    C, LF, W = frames.shape
    pl_ = Place(C, LF)
    D, T, d, t = pl_.D, pl_.T, pl_.d, pl_.t
    Hc = w_qkv.shape[2]
    U = w_up.shape[1]
    A, R = fc1_a.shape[0], fc1_a.shape[2]
    AR = A * R
    rows = pl_.rows
    heads = W // HEAD

    meta = jnp.concatenate([clip_frame_length[:, None], clip_adapter_index], axis=1)
    metas = lax.all_gather(meta, "dp")
    qkvo = jnp.concatenate([w_qkv.transpose(0, 2, 1), w_out[None]]).reshape(4 * Hc, W // D)
    qkvo = lax.all_to_all(qkvo, "dp", 0, 1, tiled=True)
    qkvo_low = jnp.concatenate(
        [qkv_b.transpose(0, 3, 1, 2).reshape(3, Hc, AR), out_a.transpose(1, 0, 2).reshape(1, Hc, AR)]
    ).reshape(D, 4 * Hc // D, AR)
    qkvo = jnp.concatenate([qkvo, lax.dynamic_index_in_dim(qkvo_low, d, 0, False)], axis=1)
    ffn = jnp.stack([w_up.T, w_down])
    ffn = lax.all_to_all(ffn, "dp", 1, 2, tiled=True)
    count = qkvo.shape[0]
    half = count // 2
    heads_part = Gather(pl_, qkvo[:half], qkvo[half:])
    frames_by, upstream_by = by_chip(pl_, frames), by_chip(pl_, upstream)
    ffn = heads_part.line(ffn)
    frames_by, metas = tie([heads_part], frames_by, metas)
    all_ffn = lax.all_gather(ffn, ("tensor", "dp"))
    frames_in = to_clip(pl_, frames_by)
    heads_part.middle()
    heads_part.last()
    of_plane = jnp.repeat(lax.dynamic_slice_in_dim(metas, d - pl_.core, 2).reshape(2 * C, 7), pl_.Q, axis=0)
    hot_up, hot_down = [(of_plane[:, j, None] == jnp.arange(A)).astype(BF) for j in (5, 6)]
    inner_by = jnp.stack(
        [
            jnp.einsum("ta,aru->tru", hot_up, fc1_b, preferred_element_type=F32).astype(BF),
            jnp.einsum("ta,aru->tru", hot_down, fc2_a.swapaxes(1, 2), preferred_element_type=F32).astype(BF),
        ],
        axis=1,
    ).reshape(T, -1, W)
    upstream_by = jnp.concatenate([upstream_by, inner_by], axis=1)
    frames_in, upstream_by = tie([heads_part], frames_in, upstream_by)
    upstream_in = lax.all_to_all(upstream_by, "tensor", 0, 0)
    heads_part.core()
    weights, line = heads_weights(pl_, heads_part.parts)

    g = t // pl_.Q
    here = metas[d - pl_.core + g // C, g % C]
    length, picks = here[0], here[1:]
    marks = (jnp.arange(AR)[None, :] // R == picks[:, None]).astype(F32)

    flat_a = lambda a: a.swapaxes(-3, -2).reshape(*a.shape[:-3], W, AR)
    flat_b = lambda b: b.reshape(AR, W)
    marks = marks[:, None, :]
    sels = (jnp.arange(AR)[None, None, :] == (picks * R)[:, None, None] + jnp.arange(R)[None, :, None]).astype(BF)
    live = (pl_.positions(pl_.core, t % pl_.Q) < length).astype(F32)[:, None]
    keys_live = jnp.concatenate([pl_.positions(c, s) for c, s in group_places(pl_)]) < length
    bias = jnp.where(keys_live, 0.0, -1e30).astype(F32)[None]
    gain1, gain2 = gain1[None], gain2[None]
    a_all = flat_a(qkv_a)

    q, k, v, low1 = project(frames_in, gain1, a_all, marks[:3], sels[:3], weights)
    ks, vs = group_values(pl_, k), group_values(pl_, v)
    mixed, expo, inverse = attend(q, ks, vs, bias)
    bo, a1, b2 = flat_b(out_b), flat_a(fc1_a), flat_b(fc2_b)
    hidden, n2, low2 = leave(mixed, frames_in, bo, a1, gain2, marks, sels, weights)
    hidden, n2, low2, upstream_in = tie([], hidden, n2, low2, upstream_in)
    inner_in = upstream_in[:, pl_.S :].reshape(T, 2, R, U).transpose(1, 2, 0, 3).reshape(2, 1, R, T * U)
    upstream_in = upstream_in[:, : pl_.S].reshape(pl_.rows, W)
    inner_in = inner_in * marks[4:].astype(BF).reshape(2, A, R, 1)
    inner_in = inner_in.reshape(2, AR, T * U)
    acc1, acc2, unit_a, unit_b = feed(n2, upstream_in, live, b2, marks, sels, low2, all_ffn, inner_in)
    layer_rows, dhidden, dmixed, grads2 = turn(
        acc1, acc2, hidden, n2, upstream_in, live, mixed, bo, a1, b2, gain2, marks, sels, low2, weights
    )
    head_order = places(pl_, True).reshape(T, D)[:, d] % T
    clips = metas.reshape(D // 2, 2 * C, 7)[:, :, 1:]
    clips = jnp.repeat(clips, pl_.Q, axis=1)[:, None]
    clips = jnp.broadcast_to(clips, (D // 2, 2, T, 6)).reshape(D, T, 6)
    clips = jnp.take(clips, d ^ jnp.arange(D), axis=0).reshape(D * T, 6)
    hot = (clips[:, :, None] == jnp.arange(A)).astype(BF)
    by_tensor = lambda v: v.reshape(R, T, -1)

    def by_head(v):
        if line:
            v = v.reshape(R, 2, T, -1).swapaxes(1, 2)
        return jnp.take(by_tensor(v), head_order, axis=1)

    def joined(terms):
        return jnp.concatenate([v.astype(BF) for v in terms], axis=2).swapaxes(0, 1)

    def owned(got, sizes, picks_of):
        got = to_owners(pl_, got)
        got = got.reshape(D * T, R // D, -1)
        out, at = [], 0
        for size, j in zip(sizes, picks_of):
            out.append(
                jnp.einsum("sa,srw->arw", hot[:, j], got[:, :, at : at + size], preferred_element_type=F32)
            )
            at += size
        return out

    wm = W // T
    terms = joined([by_head(grads2[0]), *map(by_tensor, (grads2[1], grads2[2], grads2[3], unit_b, unit_a))])
    layer_got = from_clip(pl_, layer_rows, terms)
    dq, *dkv = attend_back(q, ks, vs, expo, inverse, mixed, dmixed)
    dks, dvs = dkv[: len(dkv) // 2], dkv[len(dkv) // 2 :]
    dk2, dv2 = group_received(pl_, dks), group_received(pl_, dvs)
    dq, layer_got = tie([], dq, layer_got)
    dframes, grads1 = finish(
        frames_in, dhidden, gain1, a_all, marks[:3], sels[:3], low1, dq, dks[0], dk2, dvs[0], dv2, weights
    )
    dframes, layer_got = tie([], dframes, layer_got)
    layer_output, early = from_sources(pl_, layer_got, R)
    out_ga, out_gb, fc1_ga, fc2_gb, fc1_gb, fc2_ga = owned(early, (wm,) * 4 + (U,) * 2, (3, 3, 4, 5, 4, 5))
    terms = joined([by_tensor(grads1[0, j]) for j in range(3)] + [by_head(grads1[1, j]) for j in range(3)])
    frames_grad, late = from_sources(pl_, from_clip(pl_, dframes, terms), R)
    frames_grad = frames_grad.astype(F32)
    late = owned(late, (wm,) * 6, (0, 1, 2, 0, 1, 2))
    flip = lambda a: jnp.swapaxes(a, -1, -2)
    return (
        layer_output,
        frames_grad,
        flip(jnp.stack(late[:3])),
        jnp.stack(late[3:]),
        flip(out_ga),
        out_gb,
        flip(fc1_ga),
        fc1_gb,
        flip(fc2_ga),
        fc2_gb,
    )


def solution(mesh):
    placed = (
        P("dp", "tensor", None),
        P("dp", "tensor", None),
        P("dp"),
        P("dp", None),
        P(),
        P(),
        P(None, "dp", "tensor"),
        P("tensor", "dp"),
        P("dp", "tensor"),
        P("tensor", "dp"),
        P(),
        P(None, None, None, "tensor"),
        P(None, "tensor", None),
        P(),
        P(),
        P(None, None, "tensor"),
        P(None, "tensor", None),
        P(),
    )
    return jax.shard_map(
        body,
        mesh=mesh,
        in_specs=placed,
        out_specs=(
            P("dp", "tensor", None),
            P("dp", "tensor", None),
            P(None, None, "tensor", "dp"),
            P(None, None, "dp", "tensor"),
            P(None, "tensor", "dp"),
            P(None, "dp", "tensor"),
            P(None, "tensor", "dp"),
            P(None, "dp", "tensor"),
            P(None, "tensor", "dp"),
            P(None, "dp", "tensor"),
        ),
        check_vma=False,
    )
```

```python
import functools

import jax
import jax.numpy as jnp
from jax import lax
from jax.experimental import pallas as pl
from jax.experimental.pallas import tpu as pltpu
from jax.sharding import PartitionSpec as P

HEAD = 80
BF = jnp.bfloat16
F32 = jnp.float32


def mm(a, b):
    return jnp.dot(a, b, preferred_element_type=F32)


def mm_nt(a, b):
    return lax.dot_general(a, b, (((1,), (1,)), ((), ())), preferred_element_type=F32)


def mm_tn(a, b):
    return lax.dot_general(a, b, (((0,), (0,)), ((), ())), preferred_element_type=F32)


def norm_parts(values):
    center = values - jnp.mean(values, axis=-1, keepdims=True)
    rate = lax.rsqrt(jnp.mean(center * center, axis=-1, keepdims=True) + 1e-5)
    return center * rate, rate


def norm_back(z, rate, grad):
    return rate * (
        grad
        - jnp.mean(grad, axis=-1, keepdims=True)
        - z * jnp.mean(grad * z, axis=-1, keepdims=True)
    )


class Place:
    def __init__(self, clips, local_frames):
        self.D, self.T = lax.axis_size("dp"), lax.axis_size("tensor")
        self.d, self.t = lax.axis_index("dp"), lax.axis_index("tensor")
        self.core = self.d % 2
        self.C, self.LF = clips, local_frames
        self.Q = self.T // (2 * clips)
        self.S = local_frames // (2 * self.Q)
        self.rows = self.T * self.S
        self.swap = [(i, i ^ 1) for i in range(self.D)]

    def swap_core(self, x):
        return lax.ppermute(x, "dp", self.swap)

    def positions(self, core, q):
        source = jnp.arange(self.T, dtype=jnp.int32)[:, None] * self.LF
        inner = (q * 2 + core) * self.S + jnp.arange(self.S, dtype=jnp.int32)[None, :]
        return (source + inner).reshape(self.rows)


def by_chip(pl_, x):
    C, LF, W = x.shape
    parts = x.reshape(C, pl_.Q, 2, pl_.S, W)
    even, odd = parts[:, :, 0], parts[:, :, 1]
    first = pl_.core == 0
    mine, theirs = jnp.where(first, even, odd), jnp.where(first, odd, even)
    got = pl_.swap_core(theirs)
    both = jnp.stack([jnp.where(first, mine, got), jnp.where(first, got, mine)])
    return both.reshape(pl_.T, pl_.S, W)


def to_clip(pl_, both):
    return lax.all_to_all(both, "tensor", 0, 0).reshape(pl_.rows, both.shape[2])


def from_clip(pl_, y, terms):
    W = y.shape[-1]
    T = pl_.T
    sent = jnp.concatenate([y.reshape(T, pl_.S, W), terms.astype(BF).reshape(T, -1, W)], axis=1)
    return lax.all_to_all(sent, "tensor", 0, 0)


def from_sources(pl_, got, R):
    T, _, W = got.shape
    both = got[:, : pl_.S].reshape(2, pl_.C, pl_.Q, pl_.S, W)
    first = pl_.core == 0
    mine, theirs = jnp.where(first, both[0], both[1]), jnp.where(first, both[1], both[0])
    other = pl_.swap_core(theirs)
    even, odd = jnp.where(first, mine, other), jnp.where(first, other, mine)
    rows = jnp.stack([even, odd], axis=2).reshape(pl_.C, pl_.LF, W)
    return rows, got[:, pl_.S :].reshape(T, R, -1)


def to_owners(pl_, terms):
    T, R, w = terms.shape
    D = pl_.D
    parts = terms.reshape(T, D, R // D, w).swapaxes(0, 1)
    out = []
    for step in range(D):
        part = lax.dynamic_index_in_dim(parts, pl_.d ^ step, 0, False)
        out.append(lax.ppermute(part, "dp", [(i, i ^ step) for i in range(D)]) if step else part)
    return jnp.stack(out)


def ring(x, axis, stride, size):
    perm = [(i, (i + stride) % size) for i in range(size)]
    out = [x]
    for _ in range(size // stride - 1):
        out.append(lax.ppermute(out[-1], axis, perm))
    return jnp.stack(out)


class Gather:
    def __init__(self, place, first, second):
        self.place = place
        self.parts = (first, second)

    def line(self, between):
        size = self.place.T
        perm = [(i, (i + 2) % size) for i in range(size)]
        lines = [[v] for v in self.parts]
        for step in range(size // 2 - 1):
            for line in lines:
                line.append(lax.ppermute(line[-1], "tensor", perm))
            if step == min(1, size // 2 - 2):
                lines, between = lax.optimization_barrier((lines, between))
        self.parts = [jnp.stack(line) for line in lines]
        return between

    def pair(self, v):
        perm = [(i, i ^ 1) for i in range(self.place.T)]
        return jnp.stack([v, lax.ppermute(v, "tensor", perm)])

    def plane(self, v):
        return ring(v, "dp", 2, self.place.D)

    def middle(self):
        self.parts = [self.pair(self.parts[0]), self.plane(self.parts[1])]

    def last(self):
        self.parts = [self.plane(self.parts[0]), self.pair(self.parts[1])]

    def core(self):
        self.parts = [*self.parts, *[self.place.swap_core(v) for v in self.parts]]


def tie(gathers, *values):
    moved = [g.parts for g in gathers]
    moved, values = lax.optimization_barrier((moved, values))
    for g, parts in zip(gathers, moved):
        g.parts = list(parts)
    return values


def places(pl_, pair_first):
    T, D = pl_.T, pl_.D
    tt, dd = jnp.meshgrid(jnp.arange(T), jnp.arange(D), indexing="ij")
    fx = (pl_.t ^ tt) & 1
    s = ((pl_.t ^ fx) - tt) // 2 % (T // 2)
    fc = (pl_.d ^ dd) & 1
    u = ((pl_.d ^ fc) - dd) // 2 % (D // 2)
    if pair_first:
        index = ((fc * (D // 2) + u) * 2 + fx) * (T // 2) + s
    else:
        index = ((fc * 2 + fx) * (D // 2) + u) * (T // 2) + s
    return index.reshape(-1)


def plane_places(pl_):
    dd = jnp.arange(pl_.D)
    fc = (pl_.d ^ dd) & 1
    return fc * (pl_.D // 2) + ((pl_.d ^ fc) - dd) // 2 % (pl_.D // 2)


def group_values(pl_, x):
    out = [x, pl_.swap_core(x)]
    for step in range(1, pl_.Q):
        perm = [
            (i, i - i % pl_.Q + (i + step) % pl_.Q) for i in range(pl_.T)
        ]
        out.append(lax.ppermute(out[0], "tensor", perm))
        out.append(lax.ppermute(out[1], "tensor", perm))
    return out


def group_places(pl_):
    q = pl_.t % pl_.Q
    out = []
    for step in range(pl_.Q):
        sender = (q - step) % pl_.Q
        out.append((pl_.core, sender))
        out.append((1 - pl_.core, sender))
    return out


def group_received(pl_, blocks):
    total = pl_.swap_core(blocks[1])
    for step in range(1, pl_.Q):
        perm = [(i - i % pl_.Q + (i + step) % pl_.Q, i) for i in range(pl_.T)]
        own = lax.ppermute(blocks[2 * step], "tensor", perm)
        other = lax.ppermute(pl_.swap_core(blocks[2 * step + 1]), "tensor", perm)
        total = (total.astype(F32) + own.astype(F32) + other.astype(F32)).astype(BF)
    return total


RATE = HEAD**-0.5
TO_LOG2 = RATE * 1.4426950408889634
EXTRA = 16


def attend_kernel(q_ref, k_refs, v_refs, bias_ref, out_ref, expo_ref, inverse_ref):
    rows = q_ref.shape[1]
    keys = bias_ref.shape[1]
    k = jnp.concatenate(
        [jnp.concatenate([r[...] for r in k_refs], axis=1), bias_ref[...].astype(BF), jnp.zeros((EXTRA - 1, keys), BF)]
    ).T
    v = jnp.concatenate(
        [jnp.concatenate([r[...] for r in v_refs], axis=1), jnp.ones((EXTRA, keys), BF)]
    )
    q = jnp.concatenate([q_ref[...], jnp.ones((EXTRA, rows), BF)])
    scores = mm(k, q)
    top = jnp.max(scores, axis=0, keepdims=True)
    expo = jnp.exp2((scores - top) * TO_LOG2).astype(BF)
    expo_ref[0] = expo
    both = mm(v, expo)
    total = both[HEAD : HEAD + 1]
    out_ref[...] = (both[:HEAD] / total).astype(BF)
    inverse_ref[0] = 1.0 / total


def attend(q, ks, vs, bias):
    width, rows = q.shape
    heads, n = width // HEAD, len(ks)
    head = pl.BlockSpec((HEAD, rows), lambda h: (h, 0))

    def kernel(*refs):
        attend_kernel(refs[0], refs[1 : 1 + n], refs[1 + n : 1 + 2 * n], *refs[1 + 2 * n :])

    return pl.pallas_call(
        kernel,
        grid=(heads,),
        in_specs=[head] * (1 + 2 * n) + [pl.BlockSpec(bias.shape, lambda h: (0, 0))],
        out_specs=[
            head,
            pl.BlockSpec((1, bias.shape[1], rows), lambda h: (h, 0, 0)),
            pl.BlockSpec((1, 1, rows), lambda h: (h, 0, 0)),
        ],
        out_shape=[
            jax.ShapeDtypeStruct((width, rows), BF),
            jax.ShapeDtypeStruct((heads, bias.shape[1], rows), BF),
            jax.ShapeDtypeStruct((heads, 1, rows), F32),
        ],
        compiler_params=pltpu.CompilerParams(vmem_limit_bytes=56 * 2**20),
        cost_estimate=pl.CostEstimate(
            flops=4 * heads * rows * bias.shape[1] * 256, bytes_accessed=6 * width * rows, transcendentals=0
        ),
        name="attend_forward",
    )(q, *ks, *vs, bias)


def attend_back_kernel(
    q_ref, k_refs, v_refs, expo_ref, inverse_ref, mixed_ref, dmixed_ref, dq_ref, dk_refs, dv_refs, *, span
):
    rows = q_ref.shape[1]
    keys = expo_ref.shape[1]
    k = jnp.concatenate([r[...] for r in k_refs], axis=1)
    v = jnp.concatenate(
        [jnp.concatenate([r[...] for r in v_refs], axis=1), jnp.ones((EXTRA, keys), BF)]
    ).T
    inverse = inverse_ref[0]
    dmixed = dmixed_ref[...].astype(F32)
    delta = -jnp.sum(dmixed * mixed_ref[...].astype(F32), axis=0, keepdims=True) * inverse
    d0 = delta.astype(BF)
    d1 = (delta - d0.astype(F32)).astype(BF)
    dmixed = (dmixed * inverse).astype(BF)
    dmixed_more = jnp.concatenate([dmixed, d0, d1, jnp.zeros((EXTRA - 2, rows), BF)])
    q = q_ref[...]
    dk = jnp.zeros((HEAD, keys), F32)
    dv = jnp.zeros((HEAD, keys), F32)
    for start in range(0, rows, span):
        part = slice(start, start + span)
        expo = expo_ref[0, :, part]
        dscores = (expo.astype(F32) * mm(v, dmixed_more[:, part])).astype(BF)
        dq_ref[:, part] = (mm(k, dscores) * RATE).astype(BF)
        dk = dk + mm_nt(q[:, part], dscores)
        dv = dv + mm_nt(dmixed[:, part], expo)
    for i, (dk_ref, dv_ref) in enumerate(zip(dk_refs, dv_refs)):
        part = slice(i * rows, (i + 1) * rows)
        dk_ref[...] = (dk[:, part] * RATE).astype(BF)
        dv_ref[...] = dv[:, part].astype(BF)


def attend_back(q, ks, vs, expo, inverse, mixed, dmixed):
    width, rows = q.shape
    keys = expo.shape[1]
    heads, n = width // HEAD, len(ks)
    span = rows
    head = pl.BlockSpec((HEAD, rows), lambda h: (h, 0))

    def kernel(*refs):
        ins, outs = refs[: 5 + 2 * n], refs[5 + 2 * n :]
        attend_back_kernel(
            ins[0], ins[1 : 1 + n], ins[1 + n : 1 + 2 * n], *ins[1 + 2 * n :], outs[0], outs[1 : 1 + n], outs[1 + n :], span=span
        )

    return pl.pallas_call(
        kernel,
        grid=(heads,),
        in_specs=[head] * (1 + 2 * n)
        + [
            pl.BlockSpec((1, keys, rows), lambda h: (h, 0, 0)),
            pl.BlockSpec((1, 1, rows), lambda h: (h, 0, 0)),
            head,
            head,
        ],
        out_specs=[head] * (1 + 2 * n),
        out_shape=[jax.ShapeDtypeStruct((width, rows), BF)] * (1 + 2 * n),
        compiler_params=pltpu.CompilerParams(vmem_limit_bytes=56 * 2**20),
        cost_estimate=pl.CostEstimate(
            flops=8 * heads * rows * keys * 256, bytes_accessed=12 * width * rows, transcendentals=0
        ),
        name="attend_backward",
    )(q, *ks, *vs, expo, inverse, mixed, dmixed)


def heads_weights(pl_, parts):
    first, second, first_other, second_other = parts
    planes, pairs, lines, half, width = first.shape
    D, T = pl_.D, pl_.T
    if D == 4 and half == HEAD:
        index = plane_places(pl_)
        order = jnp.stack([index // 2, index % 2], axis=1).reshape(-1).astype(jnp.int32)
        flat = lambda v: v.reshape(*v.shape[:2], lines * half, width)
        return (flat(first), flat(second), flat(first_other), flat(second_other), order), True
    gathered = [
        jnp.stack([first, first_other]).reshape(D, T, half, width),
        jnp.stack([second, second_other]).transpose(0, 2, 1, 3, 4, 5).reshape(D, T, half, width),
    ]
    index = plane_places(pl_)
    gathered = [[lax.dynamic_index_in_dim(v, index[i], 0, False) for v in gathered] for i in range(D)]
    gathered = jnp.stack([jnp.concatenate(v, axis=1) for v in gathered])
    gathered = gathered.reshape(4, D // 4, T, 2 * half, width).transpose(0, 2, 1, 3, 4)
    gathered = gathered.reshape(4, 1, -1, width)
    middle = gathered.shape[2] // 2
    first, second = gathered[:, :, :middle], gathered[:, :, middle:].transpose(1, 0, 2, 3)
    order = jnp.stack([jnp.zeros(4, jnp.int32), jnp.arange(4, dtype=jnp.int32)], axis=1).reshape(-1)
    return (first, second, first, second, order), False


def weight_copies(refs, buf, sems, plane, other):
    first, second = refs[2 * other], refs[2 * other + 1]
    pairs, size = first.shape[1], first.shape[2]
    copies = [
        pltpu.make_async_copy(first.at[plane, x], buf.at[pl.ds(x * size, size)], sems.at[x])
        for x in range(pairs)
    ]
    pairs, at, size = second.shape[0], pairs * size, second.shape[2]
    return copies + [
        pltpu.make_async_copy(second.at[x, plane], buf.at[pl.ds(at + x * size, size)], sems.at[2 + x])
        for x in range(pairs)
    ]


def load_weight(refs, order_ref, number, buf, sems):
    for other in range(2):

        @pl.when(order_ref[2 * number] == other)
        def _():
            for copy in weight_copies(refs, buf, sems, order_ref[2 * number + 1], other):
                copy.start()


def weight_wait(refs, buf, sems):
    for copy in weight_copies(refs, buf, sems, 0, 0):
        copy.wait()


def weight_specs():
    return [pl.BlockSpec(memory_space=pl.ANY)] * 4 + [pl.BlockSpec(memory_space=pltpu.SMEM)]


def whole(shape, dims=0):
    return pl.BlockSpec(shape, lambda *_: (0,) * len(shape))


def block_of(rows):
    return 256 if rows % 256 == 0 else 128


def by_rows(size, width):
    return pl.BlockSpec((size, width), lambda i: (i, 0))


def by_columns(height, size):
    return pl.BlockSpec((height, size), lambda i: (0, i))


def project_kernel(x_ref, gain_ref, a_ref, mark_ref, sel_ref, *refs):
    *w_refs, order_ref, q_ref, k_ref, v_ref, low_ref, bufs, sems = refs
    i = pl.program_id(0)

    @pl.when(i == 0)
    def _():
        for j in range(3):
            load_weight(w_refs, order_ref, j, bufs.at[j], sems.at[j])

    z, _ = norm_parts(x_ref[...].astype(F32))
    n1 = (z * gain_ref[...]).astype(BF)
    for j, out_ref in enumerate((q_ref, k_ref, v_ref)):
        low = (mm(n1, a_ref[j]) * mark_ref[j]).astype(BF)
        low_ref[j] = mm_nt(sel_ref[j], low).astype(BF)

        @pl.when(i == 0)
        def _():
            weight_wait(w_refs, bufs.at[j], sems.at[j])

        out_ref[...] = mm_nt(bufs[j], jnp.concatenate([n1, low], axis=1)).astype(BF)


def project(x, gain, a, marks, sels, w):
    rows, width = x.shape
    AR, R = a.shape[2], sels.shape[1]
    size = rows
    return pl.pallas_call(
        project_kernel,
        grid=(rows // size,),
        in_specs=[
            by_rows(size, width),
            whole((1, width)),
            whole((3, width, AR)),
            whole((3, 1, AR)),
            whole((3, R, AR)),
            *weight_specs(),
        ],
        out_specs=[by_columns(width, size)] * 3 + [pl.BlockSpec((3, R, size), lambda i: (0, 0, i))],
        out_shape=[jax.ShapeDtypeStruct((width, rows), BF)] * 3 + [jax.ShapeDtypeStruct((3, R, rows), BF)],
        scratch_shapes=[
            pltpu.VMEM((3, width, width + AR), BF),
            pltpu.SemaphoreType.DMA((3, 4)),
        ],
        compiler_params=pltpu.CompilerParams(vmem_limit_bytes=56 * 2**20),
        cost_estimate=pl.CostEstimate(
            flops=6 * rows * width * width, bytes_accessed=6 * width * width, transcendentals=0
        ),
        name="project",
    )(x, gain, a, marks, sels, *w)


def leave_kernel(mixed_ref, x_ref, bo_ref, a1_ref, gain_ref, mark_ref, sel_ref, *refs):
    *w_refs, order_ref, hidden_ref, n2_ref, low_ref, buf, sems = refs
    i = pl.program_id(0)
    width = x_ref.shape[1]

    @pl.when(i == 0)
    def _():
        load_weight(w_refs, order_ref, 3, buf, sems)

    mixed = mixed_ref[...].T

    @pl.when(i == 0)
    def _():
        weight_wait(w_refs, buf, sems)

    both = mm(mixed, buf[...])
    low = (both[:, width:] * mark_ref[3]).astype(BF)
    low_ref[0] = mm_nt(sel_ref[3], low).astype(BF)
    hidden = x_ref[...].astype(F32) + both[:, :width] + mm(low, bo_ref[...])
    hidden_ref[...] = hidden
    z, _ = norm_parts(hidden)
    n2 = (z * gain_ref[...]).astype(BF)
    n2_ref[:, :width] = n2
    low = (mm(n2, a1_ref[...]) * mark_ref[4]).astype(BF)
    n2_ref[:, width:] = low
    low_ref[1] = mm_nt(sel_ref[4], low).astype(BF)


def leave(mixed, x, bo, a1, gain, marks, sels, w):
    rows, width = x.shape
    AR, R = a1.shape[1], sels.shape[1]
    size = block_of(rows)
    return pl.pallas_call(
        leave_kernel,
        grid=(rows // size,),
        in_specs=[
            by_columns(width, size),
            by_rows(size, width),
            whole((AR, width)),
            whole((width, AR)),
            whole((1, width)),
            whole((6, 1, AR)),
            whole((6, R, AR)),
            *weight_specs(),
        ],
        out_specs=[
            by_rows(size, width),
            by_rows(size, width + AR),
            pl.BlockSpec((2, R, size), lambda i: (0, 0, i)),
        ],
        out_shape=[
            jax.ShapeDtypeStruct((rows, width), F32),
            jax.ShapeDtypeStruct((rows, width + AR), BF),
            jax.ShapeDtypeStruct((2, R, rows), BF),
        ],
        scratch_shapes=[pltpu.VMEM((width, width + AR), BF), pltpu.SemaphoreType.DMA((4,))],
        compiler_params=pltpu.CompilerParams(vmem_limit_bytes=56 * 2**20),
        cost_estimate=pl.CostEstimate(
            flops=4 * rows * width * width, bytes_accessed=2 * width * width, transcendentals=0
        ),
        name="leave_attention",
    )(mixed, x, bo, a1, gain, marks, sels, *w)


def feed_kernel(
    x_ref, up_ref, live_ref, b2_ref, mark_ref, sel_ref, low_ref, w_ref, l_ref, acc1_ref, acc2_ref, ga_ref, gb_ref, s_ref, ld_ref
):
    width = up_ref.shape[1]

    @pl.when(pl.program_id(0) == 0)
    def _():
        acc1_ref[...] = jnp.zeros_like(acc1_ref)
        acc2_ref[...] = jnp.zeros_like(acc2_ref)
        seed = (up_ref[...].astype(F32) * live_ref[...]).astype(BF)
        s_ref[:, :width] = seed
        low = (mm_nt(seed, b2_ref[...]) * mark_ref[5]).astype(BF)
        s_ref[:, width:] = low
        ld_ref[...] = mm_nt(sel_ref[5], low).astype(BF)

    wide = w_ref.shape[3]
    first = w_ref[:, 0].reshape(-1, wide)
    second = w_ref[:, 1].reshape(-1, wide)
    upper = mm_nt(x_ref[:, :width], first) + mm(x_ref[:, width:], l_ref[0])
    cdf = 0.5 * (1.0 + lax.erf(upper * (0.5**0.5)))
    active = (upper * cdf).astype(BF)
    dactive = mm_nt(s_ref[:, :width], second) + mm(s_ref[:, width:], l_ref[1])
    slope = cdf + upper * jnp.exp(-0.5 * upper * upper) * (1.0 / (2.0 * jnp.pi) ** 0.5)
    dupper = (dactive * slope).astype(BF)
    acc1_ref[:, :width] += mm(active, second)
    acc1_ref[:, width:] += mm_nt(active, l_ref[1])
    acc2_ref[:, :width] += mm(dupper, first)
    acc2_ref[:, width:] += mm_nt(dupper, l_ref[0])
    ga_ref[...] = mm(ld_ref[...], active).astype(BF)
    gb_ref[...] = mm(low_ref[1], dupper).astype(BF)


def feed(x, upstream, live, b2, marks, sels, low, w, inner):
    rows, width = upstream.shape
    blocks, _, h, _ = w.shape
    wide = x.shape[1]
    AR, R = wide - width, low.shape[1]
    step = blocks
    while step * h > 1280:
        step //= 2
    part = pl.BlockSpec((R, step * h), lambda i: (0, i))
    return pl.pallas_call(
        feed_kernel,
        grid=(blocks // step,),
        in_specs=[
            whole((rows, wide)),
            whole((rows, width)),
            whole((rows, 1)),
            whole((AR, width)),
            whole((6, 1, AR)),
            whole((6, R, AR)),
            whole((2, R, rows)),
            pl.BlockSpec((step, 2, h, width), lambda i: (i, 0, 0, 0)),
            pl.BlockSpec((2, AR, step * h), lambda i: (0, 0, i)),
        ],
        out_specs=[whole((rows, wide)), whole((rows, wide)), part, part],
        out_shape=[jax.ShapeDtypeStruct((rows, wide), F32)] * 2
        + [jax.ShapeDtypeStruct((R, blocks * h), BF)] * 2,
        scratch_shapes=[pltpu.VMEM((rows, wide), BF), pltpu.VMEM((R, rows), BF)],
        compiler_params=pltpu.CompilerParams(vmem_limit_bytes=60 * 2**20),
        cost_estimate=pl.CostEstimate(
            flops=8 * rows * wide * blocks * h, bytes_accessed=4 * blocks * h * wide, transcendentals=0
        ),
        name="feed_forward",
    )(x, upstream, live, b2, marks, sels, low, w, inner)


def turn_kernel(
    acc1_ref, acc2_ref, hidden_ref, n2_ref, up_ref, live_ref, mixed_ref, bo_ref, a1_ref, b2_ref, gain_ref,
    mark_ref, sel_ref, low_ref, *refs
):
    *w_refs, order_ref, layer_ref, dhidden_ref, dmixed_ref, sums_ref, buf, sems, grad_ref = refs
    i = pl.program_id(0)
    width = hidden_ref.shape[1]

    @pl.when(i == 0)
    def _():
        load_weight(w_refs, order_ref, 3, buf, sems)
        grad_ref[...] = jnp.zeros_like(grad_ref)

    hidden = hidden_ref[...]
    seed = (up_ref[...].astype(F32) * live_ref[...]).astype(BF)
    low = (acc1_ref[:, width:] * mark_ref[5]).astype(BF)
    branch = acc1_ref[:, :width] + mm(low, b2_ref[...])
    layer_ref[...] = jnp.where(live_ref[...] > 0, hidden + branch, 0.0).astype(BF)
    grad_ref[3] += mm(mm_nt(sel_ref[5], low).astype(BF), seed)
    low = (acc2_ref[:, width:] * mark_ref[4]).astype(BF)
    grad_ref[2] += mm(mm_nt(sel_ref[4], low).astype(BF), n2_ref[:, :width])
    dn2 = acc2_ref[:, :width] + mm_nt(low, a1_ref[...])
    z, rate = norm_parts(hidden)
    dhidden = seed.astype(F32) + norm_back(z, rate, dn2 * gain_ref[...])
    dhidden_ref[...] = dhidden
    dattn = dhidden.astype(BF)
    grad_ref[1] += mm(low_ref[0], dattn)
    low = (mm_nt(dattn, bo_ref[...]) * mark_ref[3]).astype(BF)
    grad_ref[0] += mm_nt(mm_nt(sel_ref[3], low).astype(BF), mixed_ref[...])

    @pl.when(i == 0)
    def _():
        weight_wait(w_refs, buf, sems)

    dmixed_ref[...] = mm_nt(buf[...], jnp.concatenate([dattn, low], axis=1)).astype(BF)

    @pl.when(i == pl.num_programs(0) - 1)
    def _():
        sums_ref[...] = grad_ref[...].astype(BF)


def turn(acc1, acc2, hidden, n2, upstream, live, mixed, bo, a1, b2, gain, marks, sels, low, w):
    rows, width = hidden.shape
    AR, R = a1.shape[1], sels.shape[1]
    size = block_of(rows)
    return pl.pallas_call(
        turn_kernel,
        grid=(rows // size,),
        in_specs=[
            by_rows(size, width + AR),
            by_rows(size, width + AR),
            by_rows(size, width),
            by_rows(size, width + AR),
            by_rows(size, width),
            by_rows(size, 1),
            by_columns(width, size),
            whole((AR, width)),
            whole((width, AR)),
            whole((AR, width)),
            whole((1, width)),
            whole((6, 1, AR)),
            whole((6, R, AR)),
            pl.BlockSpec((2, R, size), lambda i: (0, 0, i)),
            *weight_specs(),
        ],
        out_specs=[by_rows(size, width), by_rows(size, width), by_columns(width, size), whole((4, R, width))],
        out_shape=[
            jax.ShapeDtypeStruct((rows, width), BF),
            jax.ShapeDtypeStruct((rows, width), F32),
            jax.ShapeDtypeStruct((width, rows), BF),
            jax.ShapeDtypeStruct((4, R, width), BF),
        ],
        scratch_shapes=[
            pltpu.VMEM((width, width + AR), BF),
            pltpu.SemaphoreType.DMA((4,)),
            pltpu.VMEM((4, R, width), F32),
        ],
        compiler_params=pltpu.CompilerParams(vmem_limit_bytes=56 * 2**20),
        cost_estimate=pl.CostEstimate(
            flops=4 * rows * width * width, bytes_accessed=16 * rows * width, transcendentals=0
        ),
        name="turn",
    )(acc1, acc2, hidden, n2, upstream, live, mixed, bo, a1, b2, gain, marks, sels, low, *w)


def finish_kernel(
    x_ref, dhidden_ref, gain_ref, a_ref, mark_ref, sel_ref, low_ref, dq_ref, dk_ref, dk2_ref, dv_ref, dv2_ref, *refs
):
    *w_refs, order_ref, out_ref, sums_ref, bufs, sems, grad_ref = refs
    i = pl.program_id(0)
    width = x_ref.shape[1]

    @pl.when(i == 0)
    def _():
        for j in range(3):
            load_weight(w_refs, order_ref, j, bufs.at[j], sems.at[j])
        grad_ref[...] = jnp.zeros_like(grad_ref)

    z, rate = norm_parts(x_ref[...].astype(F32))
    n1 = (z * gain_ref[...]).astype(BF)
    dn1 = jnp.zeros(x_ref.shape, F32)
    lows, picked = [], []
    for j, own in enumerate((dq_ref, dk_ref, dv_ref)):
        dy = own[...]
        if j:
            dy = (dy.astype(F32) + (dk2_ref, dv2_ref)[j - 1][...].astype(F32)).astype(BF)

        @pl.when(i == 0)
        def _():
            weight_wait(w_refs, bufs.at[j], sems.at[j])

        both = mm(dy.T, bufs[j])
        low = (both[:, width:] * mark_ref[j]).astype(BF)
        lows.append(low)
        picked.append(mm_nt(sel_ref[j], low).astype(BF))
        grad_ref[1, j] += mm_nt(low_ref[j], dy)
        dn1 = dn1 + both[:, :width]
    dn1 = dn1 + mm_nt(jnp.concatenate(lows, axis=1), jnp.concatenate([a_ref[j] for j in range(3)], axis=1))
    grads = mm(jnp.concatenate(picked), n1)
    R = sel_ref.shape[1]
    for j in range(3):
        grad_ref[0, j] += grads[j * R : (j + 1) * R]
    out_ref[...] = (dhidden_ref[...] + norm_back(z, rate, dn1 * gain_ref[...])).astype(BF)

    @pl.when(i == pl.num_programs(0) - 1)
    def _():
        sums_ref[...] = grad_ref[...].astype(BF)


def finish(x, dhidden, gain, a, marks, sels, low, dq, dk, dk2, dv, dv2, w):
    rows, width = x.shape
    AR, R = a.shape[2], sels.shape[1]
    size = block_of(rows)
    return pl.pallas_call(
        finish_kernel,
        grid=(rows // size,),
        in_specs=[
            by_rows(size, width),
            by_rows(size, width),
            whole((1, width)),
            whole((3, width, AR)),
            whole((3, 1, AR)),
            whole((3, R, AR)),
            pl.BlockSpec((3, R, size), lambda i: (0, 0, i)),
        ]
        + [by_columns(width, size)] * 5
        + weight_specs(),
        out_specs=[by_rows(size, width), whole((2, 3, R, width))],
        out_shape=[
            jax.ShapeDtypeStruct((rows, width), BF),
            jax.ShapeDtypeStruct((2, 3, R, width), BF),
        ],
        scratch_shapes=[
            pltpu.VMEM((3, width, width + AR), BF),
            pltpu.SemaphoreType.DMA((3, 4)),
            pltpu.VMEM((2, 3, R, width), F32),
        ],
        compiler_params=pltpu.CompilerParams(vmem_limit_bytes=58 * 2**20),
        cost_estimate=pl.CostEstimate(
            flops=6 * rows * width * width, bytes_accessed=6 * width * width, transcendentals=0
        ),
        name="finish",
    )(x, dhidden, gain, a, marks, sels, low, dq, dk, dk2, dv, dv2, *w)


def body(
    frames,
    upstream,
    clip_frame_length,
    clip_adapter_index,
    gain1,
    gain2,
    w_qkv,
    w_out,
    w_up,
    w_down,
    qkv_a,
    qkv_b,
    out_a,
    out_b,
    fc1_a,
    fc1_b,
    fc2_a,
    fc2_b,
):
    C, LF, W = frames.shape
    pl_ = Place(C, LF)
    D, T, d, t = pl_.D, pl_.T, pl_.d, pl_.t
    Hc = w_qkv.shape[2]
    U = w_up.shape[1]
    A, R = fc1_a.shape[0], fc1_a.shape[2]
    AR = A * R
    rows = pl_.rows
    heads = W // HEAD

    meta = jnp.concatenate([clip_frame_length[:, None], clip_adapter_index], axis=1)
    metas = lax.all_gather(meta, "dp")
    qkvo = jnp.concatenate([w_qkv.transpose(0, 2, 1), w_out[None]]).reshape(4 * Hc, W // D)
    qkvo = lax.all_to_all(qkvo, "dp", 0, 1, tiled=True)
    qkvo_low = jnp.concatenate(
        [qkv_b.transpose(0, 3, 1, 2).reshape(3, Hc, AR), out_a.transpose(1, 0, 2).reshape(1, Hc, AR)]
    ).reshape(D, 4 * Hc // D, AR)
    qkvo = jnp.concatenate([qkvo, lax.dynamic_index_in_dim(qkvo_low, d, 0, False)], axis=1)
    ffn = jnp.stack([w_up.T, w_down])
    ffn = lax.all_to_all(ffn, "dp", 1, 2, tiled=True)
    count = qkvo.shape[0]
    half = count // 2
    heads_part = Gather(pl_, qkvo[:half], qkvo[half:])
    frames_by, upstream_by = by_chip(pl_, frames), by_chip(pl_, upstream)
    ffn, metas = heads_part.line((ffn, metas))
    of_plane = jnp.repeat(lax.dynamic_slice_in_dim(metas, d - pl_.core, 2).reshape(2 * C, 7), pl_.Q, axis=0)
    hot_up, hot_down = [(of_plane[:, j, None] == jnp.arange(A)).astype(BF) for j in (5, 6)]
    inner_by = jnp.stack(
        [
            jnp.einsum("ta,aru->tru", hot_up, fc1_b, preferred_element_type=F32).astype(BF),
            jnp.einsum("ta,aru->tru", hot_down, fc2_a.swapaxes(1, 2), preferred_element_type=F32).astype(BF),
        ],
        axis=1,
    ).reshape(T, -1, W)
    frames_by = jnp.concatenate([frames_by, inner_by], axis=1)
    (frames_by,) = tie([heads_part], frames_by)
    all_ffn = lax.all_gather(ffn, ("tensor", "dp"))
    frames_in = lax.all_to_all(frames_by, "tensor", 0, 0)
    heads_part.middle()
    heads_part.last()
    frames_in, upstream_by = tie([heads_part], frames_in, upstream_by)
    inner_in = frames_in[:, pl_.S :].reshape(T, 2, R, U).transpose(1, 2, 0, 3).reshape(2, 1, R, T * U)
    frames_in = frames_in[:, : pl_.S].reshape(pl_.rows, W)
    upstream_in = to_clip(pl_, upstream_by)
    heads_part.core()
    weights, line = heads_weights(pl_, heads_part.parts)

    g = t // pl_.Q
    here = metas[d - pl_.core + g // C, g % C]
    length, picks = here[0], here[1:]
    marks = (jnp.arange(AR)[None, :] // R == picks[:, None]).astype(F32)

    flat_a = lambda a: a.swapaxes(-3, -2).reshape(*a.shape[:-3], W, AR)
    flat_b = lambda b: b.reshape(AR, W)
    marks = marks[:, None, :]
    sels = (jnp.arange(AR)[None, None, :] == (picks * R)[:, None, None] + jnp.arange(R)[None, :, None]).astype(BF)
    live = (pl_.positions(pl_.core, t % pl_.Q) < length).astype(F32)[:, None]
    keys_live = jnp.concatenate([pl_.positions(c, s) for c, s in group_places(pl_)]) < length
    bias = jnp.where(keys_live, 0.0, -1e30).astype(F32)[None]
    gain1, gain2 = gain1[None], gain2[None]
    a_all = flat_a(qkv_a)

    q, k, v, low1 = project(frames_in, gain1, a_all, marks[:3], sels[:3], weights)
    ks, vs = group_values(pl_, k), group_values(pl_, v)
    mixed, expo, inverse = attend(q, ks, vs, bias)
    bo, a1, b2 = flat_b(out_b), flat_a(fc1_a), flat_b(fc2_b)
    hidden, n2, low2 = leave(mixed, frames_in, bo, a1, gain2, marks, sels, weights)
    hidden, n2, low2, upstream_in = tie([], hidden, n2, low2, upstream_in)
    inner_in = inner_in * marks[4:].astype(BF).reshape(2, A, R, 1)
    inner_in = inner_in.reshape(2, AR, T * U)
    acc1, acc2, unit_a, unit_b = feed(n2, upstream_in, live, b2, marks, sels, low2, all_ffn, inner_in)
    layer_rows, dhidden, dmixed, grads2 = turn(
        acc1, acc2, hidden, n2, upstream_in, live, mixed, bo, a1, b2, gain2, marks, sels, low2, weights
    )
    head_order = places(pl_, True).reshape(T, D)[:, d] % T
    clips = metas.reshape(D // 2, 2 * C, 7)[:, :, 1:]
    clips = jnp.repeat(clips, pl_.Q, axis=1)[:, None]
    clips = jnp.broadcast_to(clips, (D // 2, 2, T, 6)).reshape(D, T, 6)
    clips = jnp.take(clips, d ^ jnp.arange(D), axis=0).reshape(D * T, 6)
    hot = (clips[:, :, None] == jnp.arange(A)).astype(BF)
    by_tensor = lambda v: v.reshape(R, T, -1)

    def by_head(v):
        if line:
            v = v.reshape(R, 2, T, -1).swapaxes(1, 2)
        return jnp.take(by_tensor(v), head_order, axis=1)

    def joined(terms):
        return jnp.concatenate([v.astype(BF) for v in terms], axis=2).swapaxes(0, 1)

    def owned(got, sizes, picks_of):
        got = to_owners(pl_, got)
        got = got.reshape(D * T, R // D, -1)
        out, at = [], 0
        for size, j in zip(sizes, picks_of):
            out.append(
                jnp.einsum("sa,srw->arw", hot[:, j], got[:, :, at : at + size], preferred_element_type=F32)
            )
            at += size
        return out

    wm = W // T
    terms = joined([by_head(grads2[0]), *map(by_tensor, (grads2[1], grads2[2], grads2[3], unit_b, unit_a))])
    layer_got = from_clip(pl_, layer_rows, terms)
    dq, *dkv = attend_back(q, ks, vs, expo, inverse, mixed, dmixed)
    dks, dvs = dkv[: len(dkv) // 2], dkv[len(dkv) // 2 :]
    dk2, dv2 = group_received(pl_, dks), group_received(pl_, dvs)
    dq, layer_got = tie([], dq, layer_got)
    dframes, grads1 = finish(
        frames_in, dhidden, gain1, a_all, marks[:3], sels[:3], low1, dq, dks[0], dk2, dvs[0], dv2, weights
    )
    dframes, layer_got = tie([], dframes, layer_got)
    layer_output, early = from_sources(pl_, layer_got, R)
    out_ga, out_gb, fc1_ga, fc2_gb, fc1_gb, fc2_ga = owned(early, (wm,) * 4 + (U,) * 2, (3, 3, 4, 5, 4, 5))
    terms = joined([by_tensor(grads1[0, j]) for j in range(3)] + [by_head(grads1[1, j]) for j in range(3)])
    frames_grad, late = from_sources(pl_, from_clip(pl_, dframes, terms), R)
    frames_grad = frames_grad.astype(F32)
    late = owned(late, (wm,) * 6, (0, 1, 2, 0, 1, 2))
    flip = lambda a: jnp.swapaxes(a, -1, -2)
    return (
        layer_output,
        frames_grad,
        flip(jnp.stack(late[:3])),
        jnp.stack(late[3:]),
        flip(out_ga),
        out_gb,
        flip(fc1_ga),
        fc1_gb,
        flip(fc2_ga),
        fc2_gb,
    )


def solution(mesh):
    placed = (
        P("dp", "tensor", None),
        P("dp", "tensor", None),
        P("dp"),
        P("dp", None),
        P(),
        P(),
        P(None, "dp", "tensor"),
        P("tensor", "dp"),
        P("dp", "tensor"),
        P("tensor", "dp"),
        P(),
        P(None, None, None, "tensor"),
        P(None, "tensor", None),
        P(),
        P(),
        P(None, None, "tensor"),
        P(None, "tensor", None),
        P(),
    )
    return jax.shard_map(
        body,
        mesh=mesh,
        in_specs=placed,
        out_specs=(
            P("dp", "tensor", None),
            P("dp", "tensor", None),
            P(None, None, "tensor", "dp"),
            P(None, None, "dp", "tensor"),
            P(None, "tensor", "dp"),
            P(None, "dp", "tensor"),
            P(None, "tensor", "dp"),
            P(None, "dp", "tensor"),
            P(None, "tensor", "dp"),
            P(None, "dp", "tensor"),
        ),
        check_vma=False,
    )
```

```python
import functools

import jax
import jax.numpy as jnp
from jax import lax
from jax.experimental import pallas as pl
from jax.experimental.pallas import tpu as pltpu
from jax.sharding import PartitionSpec as P

HEAD = 80
BF = jnp.bfloat16
F32 = jnp.float32


def mm(a, b):
    return jnp.dot(a, b, preferred_element_type=F32)


def mm_nt(a, b):
    return lax.dot_general(a, b, (((1,), (1,)), ((), ())), preferred_element_type=F32)


def mm_tn(a, b):
    return lax.dot_general(a, b, (((0,), (0,)), ((), ())), preferred_element_type=F32)


def norm_parts(values):
    center = values - jnp.mean(values, axis=-1, keepdims=True)
    rate = lax.rsqrt(jnp.mean(center * center, axis=-1, keepdims=True) + 1e-5)
    return center * rate, rate


def norm_back(z, rate, grad):
    return rate * (
        grad
        - jnp.mean(grad, axis=-1, keepdims=True)
        - z * jnp.mean(grad * z, axis=-1, keepdims=True)
    )


class Place:
    def __init__(self, clips, local_frames):
        self.D, self.T = lax.axis_size("dp"), lax.axis_size("tensor")
        self.d, self.t = lax.axis_index("dp"), lax.axis_index("tensor")
        self.core = self.d % 2
        self.C, self.LF = clips, local_frames
        self.Q = self.T // (2 * clips)
        self.S = local_frames // (2 * self.Q)
        self.rows = self.T * self.S
        self.swap = [(i, i ^ 1) for i in range(self.D)]

    def swap_core(self, x):
        return lax.ppermute(x, "dp", self.swap)

    def positions(self, core, q):
        source = jnp.arange(self.T, dtype=jnp.int32)[:, None] * self.LF
        inner = (q * 2 + core) * self.S + jnp.arange(self.S, dtype=jnp.int32)[None, :]
        return (source + inner).reshape(self.rows)


def by_chip(pl_, x):
    C, LF, W = x.shape
    parts = x.reshape(C, pl_.Q, 2, pl_.S, W)
    even, odd = parts[:, :, 0], parts[:, :, 1]
    first = pl_.core == 0
    mine, theirs = jnp.where(first, even, odd), jnp.where(first, odd, even)
    got = pl_.swap_core(theirs)
    both = jnp.stack([jnp.where(first, mine, got), jnp.where(first, got, mine)])
    return both.reshape(pl_.T, pl_.S, W)


def to_clip(pl_, both):
    return lax.all_to_all(both, "tensor", 0, 0).reshape(pl_.rows, both.shape[2])


def from_clip(pl_, y, terms):
    W = y.shape[-1]
    T = pl_.T
    sent = jnp.concatenate([y.reshape(T, pl_.S, W), terms.astype(BF).reshape(T, -1, W)], axis=1)
    return lax.all_to_all(sent, "tensor", 0, 0)


def from_sources(pl_, got, R):
    T, _, W = got.shape
    both = got[:, : pl_.S].reshape(2, pl_.C, pl_.Q, pl_.S, W)
    first = pl_.core == 0
    mine, theirs = jnp.where(first, both[0], both[1]), jnp.where(first, both[1], both[0])
    other = pl_.swap_core(theirs)
    even, odd = jnp.where(first, mine, other), jnp.where(first, other, mine)
    rows = jnp.stack([even, odd], axis=2).reshape(pl_.C, pl_.LF, W)
    return rows, got[:, pl_.S :].reshape(T, R, -1)


def to_owners(pl_, terms):
    T, R, w = terms.shape
    D = pl_.D
    parts = terms.reshape(T, D, R // D, w).swapaxes(0, 1)
    out = []
    for step in range(D):
        part = lax.dynamic_index_in_dim(parts, pl_.d ^ step, 0, False)
        out.append(lax.ppermute(part, "dp", [(i, i ^ step) for i in range(D)]) if step else part)
    return jnp.stack(out)


def ring(x, axis, stride, size):
    perm = [(i, (i + stride) % size) for i in range(size)]
    out = [x]
    for _ in range(size // stride - 1):
        out.append(lax.ppermute(out[-1], axis, perm))
    return jnp.stack(out)


class Gather:
    def __init__(self, place, first, second):
        self.place = place
        self.parts = (first, second)

    def line(self, between):
        size = self.place.T
        perm = [(i, (i + 2) % size) for i in range(size)]
        lines = [[v] for v in self.parts]
        for step in range(size // 2 - 1):
            for line in lines:
                line.append(lax.ppermute(line[-1], "tensor", perm))
            if step == min(1, size // 2 - 2):
                lines, between = lax.optimization_barrier((lines, between))
        self.parts = [jnp.stack(line) for line in lines]
        return between

    def pair(self, v):
        perm = [(i, i ^ 1) for i in range(self.place.T)]
        return jnp.stack([v, lax.ppermute(v, "tensor", perm)])

    def plane(self, v):
        return ring(v, "dp", 2, self.place.D)

    def middle(self):
        self.parts = [self.pair(self.parts[0]), self.plane(self.parts[1])]

    def last(self):
        self.parts = [self.plane(self.parts[0]), self.pair(self.parts[1])]

    def core(self):
        self.parts = [*self.parts, *[self.place.swap_core(v) for v in self.parts]]


def tie(gathers, *values):
    moved = [g.parts for g in gathers]
    moved, values = lax.optimization_barrier((moved, values))
    for g, parts in zip(gathers, moved):
        g.parts = list(parts)
    return values


def places(pl_, pair_first):
    T, D = pl_.T, pl_.D
    tt, dd = jnp.meshgrid(jnp.arange(T), jnp.arange(D), indexing="ij")
    fx = (pl_.t ^ tt) & 1
    s = ((pl_.t ^ fx) - tt) // 2 % (T // 2)
    fc = (pl_.d ^ dd) & 1
    u = ((pl_.d ^ fc) - dd) // 2 % (D // 2)
    if pair_first:
        index = ((fc * (D // 2) + u) * 2 + fx) * (T // 2) + s
    else:
        index = ((fc * 2 + fx) * (D // 2) + u) * (T // 2) + s
    return index.reshape(-1)


def plane_places(pl_):
    dd = jnp.arange(pl_.D)
    fc = (pl_.d ^ dd) & 1
    return fc * (pl_.D // 2) + ((pl_.d ^ fc) - dd) // 2 % (pl_.D // 2)


def group_values(pl_, x):
    out = [x, pl_.swap_core(x)]
    for step in range(1, pl_.Q):
        perm = [
            (i, i - i % pl_.Q + (i + step) % pl_.Q) for i in range(pl_.T)
        ]
        out.append(lax.ppermute(out[0], "tensor", perm))
        out.append(lax.ppermute(out[1], "tensor", perm))
    return out


def group_places(pl_):
    q = pl_.t % pl_.Q
    out = []
    for step in range(pl_.Q):
        sender = (q - step) % pl_.Q
        out.append((pl_.core, sender))
        out.append((1 - pl_.core, sender))
    return out


def group_received(pl_, blocks):
    total = pl_.swap_core(blocks[1])
    for step in range(1, pl_.Q):
        perm = [(i - i % pl_.Q + (i + step) % pl_.Q, i) for i in range(pl_.T)]
        own = lax.ppermute(blocks[2 * step], "tensor", perm)
        other = lax.ppermute(pl_.swap_core(blocks[2 * step + 1]), "tensor", perm)
        total = (total.astype(F32) + own.astype(F32) + other.astype(F32)).astype(BF)
    return total


RATE = HEAD**-0.5
TO_LOG2 = RATE * 1.4426950408889634
EXTRA = 16


def attend_kernel(q_ref, k_refs, v_refs, bias_ref, out_ref, expo_ref, inverse_ref):
    rows = q_ref.shape[1]
    keys = bias_ref.shape[1]
    k = jnp.concatenate(
        [jnp.concatenate([r[...] for r in k_refs], axis=1), bias_ref[...].astype(BF), jnp.zeros((EXTRA - 1, keys), BF)]
    ).T
    v = jnp.concatenate(
        [jnp.concatenate([r[...] for r in v_refs], axis=1), jnp.ones((EXTRA, keys), BF)]
    )
    q = jnp.concatenate([q_ref[...], jnp.ones((EXTRA, rows), BF)])
    scores = mm(k, q)
    top = jnp.max(scores, axis=0, keepdims=True)
    expo = jnp.exp2((scores - top) * TO_LOG2).astype(BF)
    expo_ref[0] = expo
    both = mm(v, expo)
    total = both[HEAD : HEAD + 1]
    out_ref[...] = (both[:HEAD] / total).astype(BF)
    inverse_ref[0] = 1.0 / total


def attend(q, ks, vs, bias):
    width, rows = q.shape
    heads, n = width // HEAD, len(ks)
    head = pl.BlockSpec((HEAD, rows), lambda h: (h, 0))

    def kernel(*refs):
        attend_kernel(refs[0], refs[1 : 1 + n], refs[1 + n : 1 + 2 * n], *refs[1 + 2 * n :])

    return pl.pallas_call(
        kernel,
        grid=(heads,),
        in_specs=[head] * (1 + 2 * n) + [pl.BlockSpec(bias.shape, lambda h: (0, 0))],
        out_specs=[
            head,
            pl.BlockSpec((1, bias.shape[1], rows), lambda h: (h, 0, 0)),
            pl.BlockSpec((1, 1, rows), lambda h: (h, 0, 0)),
        ],
        out_shape=[
            jax.ShapeDtypeStruct((width, rows), BF),
            jax.ShapeDtypeStruct((heads, bias.shape[1], rows), BF),
            jax.ShapeDtypeStruct((heads, 1, rows), F32),
        ],
        compiler_params=pltpu.CompilerParams(vmem_limit_bytes=56 * 2**20),
        cost_estimate=pl.CostEstimate(
            flops=4 * heads * rows * bias.shape[1] * 256, bytes_accessed=6 * width * rows, transcendentals=0
        ),
        name="attend_forward",
    )(q, *ks, *vs, bias)


def attend_back_kernel(
    q_ref, k_refs, v_refs, expo_ref, inverse_ref, mixed_ref, dmixed_ref, dq_ref, dk_refs, dv_refs, *, span
):
    rows = q_ref.shape[1]
    keys = expo_ref.shape[1]
    k = jnp.concatenate([r[...] for r in k_refs], axis=1)
    v = jnp.concatenate(
        [jnp.concatenate([r[...] for r in v_refs], axis=1), jnp.ones((EXTRA, keys), BF)]
    ).T
    inverse = inverse_ref[0]
    dmixed = dmixed_ref[...].astype(F32)
    delta = -jnp.sum(dmixed * mixed_ref[...].astype(F32), axis=0, keepdims=True) * inverse
    d0 = delta.astype(BF)
    d1 = (delta - d0.astype(F32)).astype(BF)
    dmixed = (dmixed * inverse).astype(BF)
    dmixed_more = jnp.concatenate([dmixed, d0, d1, jnp.zeros((EXTRA - 2, rows), BF)])
    q = q_ref[...]
    dk = jnp.zeros((HEAD, keys), F32)
    dv = jnp.zeros((HEAD, keys), F32)
    for start in range(0, rows, span):
        part = slice(start, start + span)
        expo = expo_ref[0, :, part]
        dscores = (expo.astype(F32) * mm(v, dmixed_more[:, part])).astype(BF)
        dq_ref[:, part] = (mm(k, dscores) * RATE).astype(BF)
        dk = dk + mm_nt(q[:, part], dscores)
        dv = dv + mm_nt(dmixed[:, part], expo)
    for i, (dk_ref, dv_ref) in enumerate(zip(dk_refs, dv_refs)):
        part = slice(i * rows, (i + 1) * rows)
        dk_ref[...] = (dk[:, part] * RATE).astype(BF)
        dv_ref[...] = dv[:, part].astype(BF)


def attend_back(q, ks, vs, expo, inverse, mixed, dmixed):
    width, rows = q.shape
    keys = expo.shape[1]
    heads, n = width // HEAD, len(ks)
    span = rows
    head = pl.BlockSpec((HEAD, rows), lambda h: (h, 0))

    def kernel(*refs):
        ins, outs = refs[: 5 + 2 * n], refs[5 + 2 * n :]
        attend_back_kernel(
            ins[0], ins[1 : 1 + n], ins[1 + n : 1 + 2 * n], *ins[1 + 2 * n :], outs[0], outs[1 : 1 + n], outs[1 + n :], span=span
        )

    return pl.pallas_call(
        kernel,
        grid=(heads,),
        in_specs=[head] * (1 + 2 * n)
        + [
            pl.BlockSpec((1, keys, rows), lambda h: (h, 0, 0)),
            pl.BlockSpec((1, 1, rows), lambda h: (h, 0, 0)),
            head,
            head,
        ],
        out_specs=[head] * (1 + 2 * n),
        out_shape=[jax.ShapeDtypeStruct((width, rows), BF)] * (1 + 2 * n),
        compiler_params=pltpu.CompilerParams(vmem_limit_bytes=56 * 2**20),
        cost_estimate=pl.CostEstimate(
            flops=8 * heads * rows * keys * 256, bytes_accessed=12 * width * rows, transcendentals=0
        ),
        name="attend_backward",
    )(q, *ks, *vs, expo, inverse, mixed, dmixed)


def heads_weights(pl_, parts):
    first, second, first_other, second_other = parts
    planes, pairs, lines, half, width = first.shape
    D, T = pl_.D, pl_.T
    if D == 4 and half == HEAD:
        index = plane_places(pl_)
        order = jnp.stack([index // 2, index % 2], axis=1).reshape(-1).astype(jnp.int32)
        flat = lambda v: v.reshape(*v.shape[:2], lines * half, width)
        return (flat(first), flat(second), flat(first_other), flat(second_other), order), True
    gathered = [
        jnp.stack([first, first_other]).reshape(D, T, half, width),
        jnp.stack([second, second_other]).transpose(0, 2, 1, 3, 4, 5).reshape(D, T, half, width),
    ]
    index = plane_places(pl_)
    gathered = [[lax.dynamic_index_in_dim(v, index[i], 0, False) for v in gathered] for i in range(D)]
    gathered = jnp.stack([jnp.concatenate(v, axis=1) for v in gathered])
    gathered = gathered.reshape(4, D // 4, T, 2 * half, width).transpose(0, 2, 1, 3, 4)
    gathered = gathered.reshape(4, 1, -1, width)
    middle = gathered.shape[2] // 2
    first, second = gathered[:, :, :middle], gathered[:, :, middle:].transpose(1, 0, 2, 3)
    order = jnp.stack([jnp.zeros(4, jnp.int32), jnp.arange(4, dtype=jnp.int32)], axis=1).reshape(-1)
    return (first, second, first, second, order), False


def weight_copies(refs, buf, sems, plane, other):
    first, second = refs[2 * other], refs[2 * other + 1]
    pairs, size = first.shape[1], first.shape[2]
    copies = [
        pltpu.make_async_copy(first.at[plane, x], buf.at[pl.ds(x * size, size)], sems.at[x])
        for x in range(pairs)
    ]
    pairs, at, size = second.shape[0], pairs * size, second.shape[2]
    return copies + [
        pltpu.make_async_copy(second.at[x, plane], buf.at[pl.ds(at + x * size, size)], sems.at[2 + x])
        for x in range(pairs)
    ]


def load_weight(refs, order_ref, number, buf, sems):
    for other in range(2):

        @pl.when(order_ref[2 * number] == other)
        def _():
            for copy in weight_copies(refs, buf, sems, order_ref[2 * number + 1], other):
                copy.start()


def weight_wait(refs, buf, sems):
    for copy in weight_copies(refs, buf, sems, 0, 0):
        copy.wait()


def weight_specs():
    return [pl.BlockSpec(memory_space=pl.ANY)] * 4 + [pl.BlockSpec(memory_space=pltpu.SMEM)]


def whole(shape, dims=0):
    return pl.BlockSpec(shape, lambda *_: (0,) * len(shape))


def block_of(rows):
    return 256 if rows % 256 == 0 else 128


def by_rows(size, width):
    return pl.BlockSpec((size, width), lambda i: (i, 0))


def by_columns(height, size):
    return pl.BlockSpec((height, size), lambda i: (0, i))


def project_kernel(x_ref, gain_ref, a_ref, mark_ref, sel_ref, *refs):
    *w_refs, order_ref, q_ref, k_ref, v_ref, low_ref, bufs, sems = refs
    i = pl.program_id(0)

    @pl.when(i == 0)
    def _():
        for j in range(3):
            load_weight(w_refs, order_ref, j, bufs.at[j], sems.at[j])

    z, _ = norm_parts(x_ref[...].astype(F32))
    n1 = (z * gain_ref[...]).astype(BF)
    lows = mm(n1, jnp.concatenate([a_ref[j] for j in range(3)], axis=1))
    for j, out_ref in enumerate((q_ref, k_ref, v_ref)):
        AR = a_ref.shape[2]
        low = (lows[:, j * AR : (j + 1) * AR] * mark_ref[j]).astype(BF)
        low_ref[j] = mm_nt(sel_ref[j], low).astype(BF)

        @pl.when(i == 0)
        def _():
            weight_wait(w_refs, bufs.at[j], sems.at[j])

        out_ref[...] = mm_nt(bufs[j], jnp.concatenate([n1, low], axis=1)).astype(BF)


def project(x, gain, a, marks, sels, w):
    rows, width = x.shape
    AR, R = a.shape[2], sels.shape[1]
    size = rows
    return pl.pallas_call(
        project_kernel,
        grid=(rows // size,),
        in_specs=[
            by_rows(size, width),
            whole((1, width)),
            whole((3, width, AR)),
            whole((3, 1, AR)),
            whole((3, R, AR)),
            *weight_specs(),
        ],
        out_specs=[by_columns(width, size)] * 3 + [pl.BlockSpec((3, R, size), lambda i: (0, 0, i))],
        out_shape=[jax.ShapeDtypeStruct((width, rows), BF)] * 3 + [jax.ShapeDtypeStruct((3, R, rows), BF)],
        scratch_shapes=[
            pltpu.VMEM((3, width, width + AR), BF),
            pltpu.SemaphoreType.DMA((3, 4)),
        ],
        compiler_params=pltpu.CompilerParams(vmem_limit_bytes=56 * 2**20),
        cost_estimate=pl.CostEstimate(
            flops=6 * rows * width * width, bytes_accessed=6 * width * width, transcendentals=0
        ),
        name="project",
    )(x, gain, a, marks, sels, *w)


def leave_kernel(mixed_ref, x_ref, bo_ref, a1_ref, gain_ref, mark_ref, sel_ref, *refs):
    *w_refs, order_ref, hidden_ref, n2_ref, low_ref, buf, sems = refs
    i = pl.program_id(0)
    width = x_ref.shape[1]

    @pl.when(i == 0)
    def _():
        load_weight(w_refs, order_ref, 3, buf, sems)

    mixed = mixed_ref[...].T

    @pl.when(i == 0)
    def _():
        weight_wait(w_refs, buf, sems)

    both = mm(mixed, buf[...])
    low = (both[:, width:] * mark_ref[3]).astype(BF)
    low_ref[0] = mm_nt(sel_ref[3], low).astype(BF)
    hidden = x_ref[...].astype(F32) + both[:, :width] + mm(low, bo_ref[...])
    hidden_ref[...] = hidden
    z, _ = norm_parts(hidden)
    n2 = (z * gain_ref[...]).astype(BF)
    n2_ref[:, :width] = n2
    low = (mm(n2, a1_ref[...]) * mark_ref[4]).astype(BF)
    n2_ref[:, width:] = low
    low_ref[1] = mm_nt(sel_ref[4], low).astype(BF)


def leave(mixed, x, bo, a1, gain, marks, sels, w):
    rows, width = x.shape
    AR, R = a1.shape[1], sels.shape[1]
    size = rows
    return pl.pallas_call(
        leave_kernel,
        grid=(rows // size,),
        in_specs=[
            by_columns(width, size),
            by_rows(size, width),
            whole((AR, width)),
            whole((width, AR)),
            whole((1, width)),
            whole((6, 1, AR)),
            whole((6, R, AR)),
            *weight_specs(),
        ],
        out_specs=[
            by_rows(size, width),
            by_rows(size, width + AR),
            pl.BlockSpec((2, R, size), lambda i: (0, 0, i)),
        ],
        out_shape=[
            jax.ShapeDtypeStruct((rows, width), F32),
            jax.ShapeDtypeStruct((rows, width + AR), BF),
            jax.ShapeDtypeStruct((2, R, rows), BF),
        ],
        scratch_shapes=[pltpu.VMEM((width, width + AR), BF), pltpu.SemaphoreType.DMA((4,))],
        compiler_params=pltpu.CompilerParams(vmem_limit_bytes=56 * 2**20),
        cost_estimate=pl.CostEstimate(
            flops=4 * rows * width * width, bytes_accessed=2 * width * width, transcendentals=0
        ),
        name="leave_attention",
    )(mixed, x, bo, a1, gain, marks, sels, *w)


def feed_kernel(
    x_ref, up_ref, live_ref, b2_ref, mark_ref, sel_ref, low_ref, w_ref, l_ref, acc1_ref, acc2_ref, ga_ref, gb_ref, s_ref, ld_ref
):
    width = up_ref.shape[1]

    @pl.when(pl.program_id(0) == 0)
    def _():
        acc1_ref[...] = jnp.zeros_like(acc1_ref)
        acc2_ref[...] = jnp.zeros_like(acc2_ref)
        seed = (up_ref[...].astype(F32) * live_ref[...]).astype(BF)
        s_ref[:, :width] = seed
        low = (mm_nt(seed, b2_ref[...]) * mark_ref[5]).astype(BF)
        s_ref[:, width:] = low
        ld_ref[...] = mm_nt(sel_ref[5], low).astype(BF)

    wide = w_ref.shape[3]
    first = w_ref[:, 0].reshape(-1, wide)
    second = w_ref[:, 1].reshape(-1, wide)
    upper = mm_nt(x_ref[:, :width], first) + mm(x_ref[:, width:], l_ref[0])
    cdf = 0.5 * (1.0 + lax.erf(upper * (0.5**0.5)))
    active = (upper * cdf).astype(BF)
    dactive = mm_nt(s_ref[:, :width], second) + mm(s_ref[:, width:], l_ref[1])
    slope = cdf + upper * jnp.exp(-0.5 * upper * upper) * (1.0 / (2.0 * jnp.pi) ** 0.5)
    dupper = (dactive * slope).astype(BF)
    acc1_ref[:, :width] += mm(active, second)
    acc1_ref[:, width:] += mm_nt(active, l_ref[1])
    acc2_ref[:, :width] += mm(dupper, first)
    acc2_ref[:, width:] += mm_nt(dupper, l_ref[0])
    ga_ref[...] = mm(ld_ref[...], active).astype(BF)
    gb_ref[...] = mm(low_ref[1], dupper).astype(BF)


def feed(x, upstream, live, b2, marks, sels, low, w, inner):
    rows, width = upstream.shape
    blocks, _, h, _ = w.shape
    wide = x.shape[1]
    AR, R = wide - width, low.shape[1]
    step = blocks
    while step * h > 1280:
        step //= 2
    part = pl.BlockSpec((R, step * h), lambda i: (0, i))
    return pl.pallas_call(
        feed_kernel,
        grid=(blocks // step,),
        in_specs=[
            whole((rows, wide)),
            whole((rows, width)),
            whole((rows, 1)),
            whole((AR, width)),
            whole((6, 1, AR)),
            whole((6, R, AR)),
            whole((2, R, rows)),
            pl.BlockSpec((step, 2, h, width), lambda i: (i, 0, 0, 0)),
            pl.BlockSpec((2, AR, step * h), lambda i: (0, 0, i)),
        ],
        out_specs=[whole((rows, wide)), whole((rows, wide)), part, part],
        out_shape=[jax.ShapeDtypeStruct((rows, wide), F32)] * 2
        + [jax.ShapeDtypeStruct((R, blocks * h), BF)] * 2,
        scratch_shapes=[pltpu.VMEM((rows, wide), BF), pltpu.VMEM((R, rows), BF)],
        compiler_params=pltpu.CompilerParams(vmem_limit_bytes=60 * 2**20),
        cost_estimate=pl.CostEstimate(
            flops=8 * rows * wide * blocks * h, bytes_accessed=4 * blocks * h * wide, transcendentals=0
        ),
        name="feed_forward",
    )(x, upstream, live, b2, marks, sels, low, w, inner)


def turn_kernel(
    acc1_ref, acc2_ref, hidden_ref, n2_ref, up_ref, live_ref, mixed_ref, bo_ref, a1_ref, b2_ref, gain_ref,
    mark_ref, sel_ref, low_ref, *refs
):
    *w_refs, order_ref, layer_ref, dhidden_ref, dmixed_ref, sums_ref, buf, sems, grad_ref = refs
    i = pl.program_id(0)
    width = hidden_ref.shape[1]

    @pl.when(i == 0)
    def _():
        load_weight(w_refs, order_ref, 3, buf, sems)
        grad_ref[...] = jnp.zeros_like(grad_ref)

    hidden = hidden_ref[...]
    seed = (up_ref[...].astype(F32) * live_ref[...]).astype(BF)
    low = (acc1_ref[:, width:] * mark_ref[5]).astype(BF)
    branch = acc1_ref[:, :width] + mm(low, b2_ref[...])
    layer_ref[...] = jnp.where(live_ref[...] > 0, hidden + branch, 0.0).astype(BF)
    grad_ref[3] += mm(mm_nt(sel_ref[5], low).astype(BF), seed)
    low = (acc2_ref[:, width:] * mark_ref[4]).astype(BF)
    grad_ref[2] += mm(mm_nt(sel_ref[4], low).astype(BF), n2_ref[:, :width])
    dn2 = acc2_ref[:, :width] + mm_nt(low, a1_ref[...])
    z, rate = norm_parts(hidden)
    dhidden = seed.astype(F32) + norm_back(z, rate, dn2 * gain_ref[...])
    dhidden_ref[...] = dhidden
    dattn = dhidden.astype(BF)
    grad_ref[1] += mm(low_ref[0], dattn)
    low = (mm_nt(dattn, bo_ref[...]) * mark_ref[3]).astype(BF)
    grad_ref[0] += mm_nt(mm_nt(sel_ref[3], low).astype(BF), mixed_ref[...])

    @pl.when(i == 0)
    def _():
        weight_wait(w_refs, buf, sems)

    dmixed_ref[...] = mm_nt(buf[...], jnp.concatenate([dattn, low], axis=1)).astype(BF)

    @pl.when(i == pl.num_programs(0) - 1)
    def _():
        sums_ref[...] = grad_ref[...].astype(BF)


def turn(acc1, acc2, hidden, n2, upstream, live, mixed, bo, a1, b2, gain, marks, sels, low, w):
    rows, width = hidden.shape
    AR, R = a1.shape[1], sels.shape[1]
    size = block_of(rows)
    return pl.pallas_call(
        turn_kernel,
        grid=(rows // size,),
        in_specs=[
            by_rows(size, width + AR),
            by_rows(size, width + AR),
            by_rows(size, width),
            by_rows(size, width + AR),
            by_rows(size, width),
            by_rows(size, 1),
            by_columns(width, size),
            whole((AR, width)),
            whole((width, AR)),
            whole((AR, width)),
            whole((1, width)),
            whole((6, 1, AR)),
            whole((6, R, AR)),
            pl.BlockSpec((2, R, size), lambda i: (0, 0, i)),
            *weight_specs(),
        ],
        out_specs=[by_rows(size, width), by_rows(size, width), by_columns(width, size), whole((4, R, width))],
        out_shape=[
            jax.ShapeDtypeStruct((rows, width), BF),
            jax.ShapeDtypeStruct((rows, width), F32),
            jax.ShapeDtypeStruct((width, rows), BF),
            jax.ShapeDtypeStruct((4, R, width), BF),
        ],
        scratch_shapes=[
            pltpu.VMEM((width, width + AR), BF),
            pltpu.SemaphoreType.DMA((4,)),
            pltpu.VMEM((4, R, width), F32),
        ],
        compiler_params=pltpu.CompilerParams(vmem_limit_bytes=56 * 2**20),
        cost_estimate=pl.CostEstimate(
            flops=4 * rows * width * width, bytes_accessed=16 * rows * width, transcendentals=0
        ),
        name="turn",
    )(acc1, acc2, hidden, n2, upstream, live, mixed, bo, a1, b2, gain, marks, sels, low, *w)


def finish_kernel(
    x_ref, dhidden_ref, gain_ref, a_ref, mark_ref, sel_ref, low_ref, dq_ref, dk_ref, dk2_ref, dv_ref, dv2_ref, *refs
):
    *w_refs, order_ref, out_ref, sums_ref, bufs, sems, grad_ref = refs
    i = pl.program_id(0)
    width = x_ref.shape[1]

    @pl.when(i == 0)
    def _():
        for j in range(3):
            load_weight(w_refs, order_ref, j, bufs.at[j], sems.at[j])
        grad_ref[...] = jnp.zeros_like(grad_ref)

    z, rate = norm_parts(x_ref[...].astype(F32))
    n1 = (z * gain_ref[...]).astype(BF)
    dn1 = jnp.zeros(x_ref.shape, F32)
    lows, picked = [], []
    for j, own in enumerate((dq_ref, dk_ref, dv_ref)):
        dy = own[...]
        if j:
            dy = (dy.astype(F32) + (dk2_ref, dv2_ref)[j - 1][...].astype(F32)).astype(BF)

        @pl.when(i == 0)
        def _():
            weight_wait(w_refs, bufs.at[j], sems.at[j])

        both = mm(dy.T, bufs[j])
        low = (both[:, width:] * mark_ref[j]).astype(BF)
        lows.append(low)
        picked.append(mm_nt(sel_ref[j], low).astype(BF))
        grad_ref[1, j] += mm_nt(low_ref[j], dy)
        dn1 = dn1 + both[:, :width]
    dn1 = dn1 + mm_nt(jnp.concatenate(lows, axis=1), jnp.concatenate([a_ref[j] for j in range(3)], axis=1))
    grads = mm(jnp.concatenate(picked), n1)
    R = sel_ref.shape[1]
    for j in range(3):
        grad_ref[0, j] += grads[j * R : (j + 1) * R]
    out_ref[...] = (dhidden_ref[...] + norm_back(z, rate, dn1 * gain_ref[...])).astype(BF)

    @pl.when(i == pl.num_programs(0) - 1)
    def _():
        sums_ref[...] = grad_ref[...].astype(BF)


def finish(x, dhidden, gain, a, marks, sels, low, dq, dk, dk2, dv, dv2, w):
    rows, width = x.shape
    AR, R = a.shape[2], sels.shape[1]
    size = block_of(rows)
    return pl.pallas_call(
        finish_kernel,
        grid=(rows // size,),
        in_specs=[
            by_rows(size, width),
            by_rows(size, width),
            whole((1, width)),
            whole((3, width, AR)),
            whole((3, 1, AR)),
            whole((3, R, AR)),
            pl.BlockSpec((3, R, size), lambda i: (0, 0, i)),
        ]
        + [by_columns(width, size)] * 5
        + weight_specs(),
        out_specs=[by_rows(size, width), whole((2, 3, R, width))],
        out_shape=[
            jax.ShapeDtypeStruct((rows, width), BF),
            jax.ShapeDtypeStruct((2, 3, R, width), BF),
        ],
        scratch_shapes=[
            pltpu.VMEM((3, width, width + AR), BF),
            pltpu.SemaphoreType.DMA((3, 4)),
            pltpu.VMEM((2, 3, R, width), F32),
        ],
        compiler_params=pltpu.CompilerParams(vmem_limit_bytes=58 * 2**20),
        cost_estimate=pl.CostEstimate(
            flops=6 * rows * width * width, bytes_accessed=6 * width * width, transcendentals=0
        ),
        name="finish",
    )(x, dhidden, gain, a, marks, sels, low, dq, dk, dk2, dv, dv2, *w)


def body(
    frames,
    upstream,
    clip_frame_length,
    clip_adapter_index,
    gain1,
    gain2,
    w_qkv,
    w_out,
    w_up,
    w_down,
    qkv_a,
    qkv_b,
    out_a,
    out_b,
    fc1_a,
    fc1_b,
    fc2_a,
    fc2_b,
):
    C, LF, W = frames.shape
    pl_ = Place(C, LF)
    D, T, d, t = pl_.D, pl_.T, pl_.d, pl_.t
    Hc = w_qkv.shape[2]
    U = w_up.shape[1]
    A, R = fc1_a.shape[0], fc1_a.shape[2]
    AR = A * R
    rows = pl_.rows
    heads = W // HEAD

    meta = jnp.concatenate([clip_frame_length[:, None], clip_adapter_index], axis=1)
    metas = lax.all_gather(meta, "dp")
    qkvo = jnp.concatenate([w_qkv.transpose(0, 2, 1), w_out[None]]).reshape(4 * Hc, W // D)
    qkvo = lax.all_to_all(qkvo, "dp", 0, 1, tiled=True)
    qkvo_low = jnp.concatenate(
        [qkv_b.transpose(0, 3, 1, 2).reshape(3, Hc, AR), out_a.transpose(1, 0, 2).reshape(1, Hc, AR)]
    ).reshape(D, 4 * Hc // D, AR)
    qkvo = jnp.concatenate([qkvo, lax.dynamic_index_in_dim(qkvo_low, d, 0, False)], axis=1)
    ffn = jnp.stack([w_up.T, w_down])
    ffn = lax.all_to_all(ffn, "dp", 1, 2, tiled=True)
    count = qkvo.shape[0]
    half = count // 2
    heads_part = Gather(pl_, qkvo[:half], qkvo[half:])
    frames_by, upstream_by = by_chip(pl_, frames), by_chip(pl_, upstream)
    ffn, metas = heads_part.line((ffn, metas))
    of_plane = jnp.repeat(lax.dynamic_slice_in_dim(metas, d - pl_.core, 2).reshape(2 * C, 7), pl_.Q, axis=0)
    hot_up, hot_down = [(of_plane[:, j, None] == jnp.arange(A)).astype(BF) for j in (5, 6)]
    inner_by = jnp.stack(
        [
            jnp.einsum("ta,aru->tru", hot_up, fc1_b, preferred_element_type=F32).astype(BF),
            jnp.einsum("ta,aru->tru", hot_down, fc2_a.swapaxes(1, 2), preferred_element_type=F32).astype(BF),
        ],
        axis=1,
    ).reshape(T, -1, W)
    frames_by = jnp.concatenate([frames_by, inner_by], axis=1)
    (frames_by,) = tie([heads_part], frames_by)
    all_ffn = lax.all_gather(ffn, ("tensor", "dp"))
    frames_in = lax.all_to_all(frames_by, "tensor", 0, 0)
    heads_part.middle()
    heads_part.last()
    frames_in, upstream_by = tie([heads_part], frames_in, upstream_by)
    inner_in = frames_in[:, pl_.S :].reshape(T, 2, R, U).transpose(1, 2, 0, 3).reshape(2, 1, R, T * U)
    frames_in = frames_in[:, : pl_.S].reshape(pl_.rows, W)
    upstream_in = to_clip(pl_, upstream_by)
    heads_part.core()
    weights, line = heads_weights(pl_, heads_part.parts)

    g = t // pl_.Q
    here = metas[d - pl_.core + g // C, g % C]
    length, picks = here[0], here[1:]
    marks = (jnp.arange(AR)[None, :] // R == picks[:, None]).astype(F32)

    flat_a = lambda a: a.swapaxes(-3, -2).reshape(*a.shape[:-3], W, AR)
    flat_b = lambda b: b.reshape(AR, W)
    marks = marks[:, None, :]
    sels = (jnp.arange(AR)[None, None, :] == (picks * R)[:, None, None] + jnp.arange(R)[None, :, None]).astype(BF)
    live = (pl_.positions(pl_.core, t % pl_.Q) < length).astype(F32)[:, None]
    keys_live = jnp.concatenate([pl_.positions(c, s) for c, s in group_places(pl_)]) < length
    bias = jnp.where(keys_live, 0.0, -1e30).astype(F32)[None]
    gain1, gain2 = gain1[None], gain2[None]
    a_all = flat_a(qkv_a)

    q, k, v, low1 = project(frames_in, gain1, a_all, marks[:3], sels[:3], weights)
    ks, vs = group_values(pl_, k), group_values(pl_, v)
    mixed, expo, inverse = attend(q, ks, vs, bias)
    bo, a1, b2 = flat_b(out_b), flat_a(fc1_a), flat_b(fc2_b)
    hidden, n2, low2 = leave(mixed, frames_in, bo, a1, gain2, marks, sels, weights)
    hidden, n2, low2, upstream_in = tie([], hidden, n2, low2, upstream_in)
    inner_in = inner_in * marks[4:].astype(BF).reshape(2, A, R, 1)
    inner_in = inner_in.reshape(2, AR, T * U)
    acc1, acc2, unit_a, unit_b = feed(n2, upstream_in, live, b2, marks, sels, low2, all_ffn, inner_in)
    layer_rows, dhidden, dmixed, grads2 = turn(
        acc1, acc2, hidden, n2, upstream_in, live, mixed, bo, a1, b2, gain2, marks, sels, low2, weights
    )
    head_order = places(pl_, True).reshape(T, D)[:, d] % T
    clips = metas.reshape(D // 2, 2 * C, 7)[:, :, 1:]
    clips = jnp.repeat(clips, pl_.Q, axis=1)[:, None]
    clips = jnp.broadcast_to(clips, (D // 2, 2, T, 6)).reshape(D, T, 6)
    clips = jnp.take(clips, d ^ jnp.arange(D), axis=0).reshape(D * T, 6)
    hot = (clips[:, :, None] == jnp.arange(A)).astype(BF)
    by_tensor = lambda v: v.reshape(R, T, -1)

    def by_head(v):
        if line:
            v = v.reshape(R, 2, T, -1).swapaxes(1, 2)
        return jnp.take(by_tensor(v), head_order, axis=1)

    def joined(terms):
        return jnp.concatenate([v.astype(BF) for v in terms], axis=2).swapaxes(0, 1)

    def owned(got, sizes, picks_of):
        got = to_owners(pl_, got)
        got = got.reshape(D * T, R // D, -1)
        out, at = [], 0
        for size, j in zip(sizes, picks_of):
            out.append(
                jnp.einsum("sa,srw->arw", hot[:, j], got[:, :, at : at + size], preferred_element_type=F32)
            )
            at += size
        return out

    wm = W // T
    terms = joined([by_head(grads2[0]), *map(by_tensor, (grads2[1], grads2[2], grads2[3], unit_b, unit_a))])
    layer_got = from_clip(pl_, layer_rows, terms)
    dq, *dkv = attend_back(q, ks, vs, expo, inverse, mixed, dmixed)
    dks, dvs = dkv[: len(dkv) // 2], dkv[len(dkv) // 2 :]
    dk2, dv2 = group_received(pl_, dks), group_received(pl_, dvs)
    dq, layer_got = tie([], dq, layer_got)
    dframes, grads1 = finish(
        frames_in, dhidden, gain1, a_all, marks[:3], sels[:3], low1, dq, dks[0], dk2, dvs[0], dv2, weights
    )
    dframes, layer_got = tie([], dframes, layer_got)
    layer_output, early = from_sources(pl_, layer_got, R)
    out_ga, out_gb, fc1_ga, fc2_gb, fc1_gb, fc2_ga = owned(early, (wm,) * 4 + (U,) * 2, (3, 3, 4, 5, 4, 5))
    terms = joined([by_tensor(grads1[0, j]) for j in range(3)] + [by_head(grads1[1, j]) for j in range(3)])
    frames_grad, late = from_sources(pl_, from_clip(pl_, dframes, terms), R)
    frames_grad = frames_grad.astype(F32)
    late = owned(late, (wm,) * 6, (0, 1, 2, 0, 1, 2))
    flip = lambda a: jnp.swapaxes(a, -1, -2)
    return (
        layer_output,
        frames_grad,
        flip(jnp.stack(late[:3])),
        jnp.stack(late[3:]),
        flip(out_ga),
        out_gb,
        flip(fc1_ga),
        fc1_gb,
        flip(fc2_ga),
        fc2_gb,
    )


def solution(mesh):
    placed = (
        P("dp", "tensor", None),
        P("dp", "tensor", None),
        P("dp"),
        P("dp", None),
        P(),
        P(),
        P(None, "dp", "tensor"),
        P("tensor", "dp"),
        P("dp", "tensor"),
        P("tensor", "dp"),
        P(),
        P(None, None, None, "tensor"),
        P(None, "tensor", None),
        P(),
        P(),
        P(None, None, "tensor"),
        P(None, "tensor", None),
        P(),
    )
    return jax.shard_map(
        body,
        mesh=mesh,
        in_specs=placed,
        out_specs=(
            P("dp", "tensor", None),
            P("dp", "tensor", None),
            P(None, None, "tensor", "dp"),
            P(None, None, "dp", "tensor"),
            P(None, "tensor", "dp"),
            P(None, "dp", "tensor"),
            P(None, "tensor", "dp"),
            P(None, "dp", "tensor"),
            P(None, "tensor", "dp"),
            P(None, "dp", "tensor"),
        ),
        check_vma=False,
    )
```
